32 devices in a mesh: ens: 2 (over y), mem: 4 (over x, core), lon: 4 (over z).
Axes of the slice: x: 2, y: 2, z: 4, core: 2. Of those that a mesh axis runs over, the one named last changes fastest.
Arguments:
- initial_state: float32 [8, 4, 4, 256, 128], P(('ens', 'mem'), None, None, 'lon'), parts along dimension 0, may hold values from -1.25 to 1.25
- ancestor: int32 [8], P(('ens', 'mem')), parts along dimension 0, may hold values from 0 to 3
- selector: int32 [8], P(('ens', 'mem')), parts along dimension 0, may hold values from 0 to 3
- perturbations: float32 [8, 4, 4, 256, 128], P('ens', None, None, 'lon'), parts along dimension 0, may hold values from -0.5 to 0.5
- diffusivity: float32 [4, 256, 128], P(None, 'lon'), may hold values from 0.05 to 0.3
- region_weight: float32 [256, 128], P('lon'), may hold values from 0.3 to 27, as said below
Outputs:
- final_state: float32 [8, 4, 4, 256, 128], P(('ens', 'mem'), None, None, 'lon'), parts along dimension 0
- actions: float32 [8, 2], P(('ens', 'mem')), parts along dimension 0
The draws below stay inside these ranges and needn't reach their ends.
There are 2 independent parts, one for each index of `ens`. The reference program is written for one: setup_inputs(seed, part) draws one part's arguments, and reference() takes and returns one part's arrays. A program takes and returns all parts, laid end to end along the dimension named above; an argument that names none is the same for every part. Nothing has to cross between parts.
Inputs may be any that keep to these rules, and one draw needn't show every extreme that they name: `region_weight`: Positive.
All inputs are finite; a program needn't handle non-finite values.
Results may differ from the reference program's by a relative error of at most 0.0001.
Values sent between devices are 32-bit elements; how exact they have to be, the bound alone decides.
No kernel may reach another device: no remote copies, remote signals or barrier semaphores. Data moves between devices by JAX's collectives and lax.ppermute only.
A program may use at most 64 MiB of HBM per device.

```python
import math
import jax
import jax.numpy as jnp
import numpy as np

FIELDS = 4
LAT = 128
LEV = 4
NPERT = 4
STEPS = 3
LON = 256
MEMBERS = 4


def draw_region_weight(key, part):
    base = jax.random.uniform(key, (LON, LAT), jnp.float32, jnp.log(0.3), jnp.log(3.0))
    ramp = jnp.log(3.0) * jnp.arange(LON, dtype=jnp.float32)[:, None] / LON
    return jnp.exp(base + ramp)


def with_ends(entries, own_key, low, top_value):
    longest = entries.shape.index(max(entries.shape))
    spots = []
    for shift in (0, 1):
        where = [jax.random.randint(jax.random.fold_in(own_key, axis), (), 0, length) for axis, length in enumerate(entries.shape)]
        where[longest] = (where[longest] + shift) % entries.shape[longest]
        spots.append(tuple(where))
    return entries.at[spots[0]].set(low).at[spots[1]].set(top_value)


def block_scale(key, dims, pieces, low, high):
    factor_of = 1.0
    for dim, blocks in pieces:
        steps = jax.random.uniform(jax.random.fold_in(jax.random.fold_in(key, 6), dim), (blocks,), jnp.float32, low / len(pieces), high / len(pieces))
        factor_of = factor_of * jnp.repeat(jnp.exp(steps), dims[dim] // blocks).reshape((-1,) + (1,) * (len(dims) - 1 - dim))
    return factor_of


def rank_table(count, slope):
    weights = [(1 << 20) // math.isqrt(standing ** slope) + 1 for standing in range(1, count + 1)]
    width = 1 + sum(weights) // (1 << 30)
    return np.cumsum(np.array([max(1, weight // width) for weight in weights]))


def skewed_ids(stream_key, extent, count, slope):
    table = rank_table(count, slope)
    ticket = jax.random.randint(jax.random.fold_in(stream_key, 1), extent, 0, int(table[count - 1]))
    rank = jnp.searchsorted(jnp.asarray(table, jnp.int32), ticket, side="right")
    return jax.random.permutation(jax.random.fold_in(stream_key, 2), count)[rank].astype(jnp.int32)


def normal_values(rng, shape, width, limit, shards=(), held_as=jnp.bfloat16):
    array = jax.random.normal(rng, shape, jnp.float32) * width
    if len(shards) > 0:
        array = block_scale(rng, shape, shards, -0.22, 0.18) * array
    return jnp.clip(array, min=-limit, max=limit).astype(held_as)


def setup_inputs(seed: int = 0, part: int = 0) -> dict:
    key_list = jax.random.split(jax.random.key(seed), 7)
    own_keys = jax.random.split(jax.random.fold_in(key_list[6], part), 7)
    return {
        "initial_state": normal_values(own_keys[0], (MEMBERS, FIELDS, LEV, LON, LAT), 0.5, 1.25, ((0, 4), (3, 4)), jnp.float32),
        "ancestor": with_ends(skewed_ids(own_keys[1], (MEMBERS,), MEMBERS, 2), jax.random.fold_in(own_keys[1], 3), 0, MEMBERS - 1).astype(jnp.int32),
        "selector": with_ends(jax.random.randint(own_keys[2], (MEMBERS,), 0, NPERT), jax.random.fold_in(own_keys[2], 1), 0, NPERT - 1).astype(jnp.int32),
        "perturbations": normal_values(own_keys[3], (NPERT, FIELDS, LEV, LON, LAT), 0.2, 0.5, ((3, 4),), jnp.float32),
        "diffusivity": jnp.clip(0.05 + 0.25 * jax.random.uniform(key_list[4], (LEV, LON, LAT), jnp.float32) ** block_scale(key_list[4], (LEV, LON, LAT), ((1, 4),), -0.2, 0.2), 0.05, 0.3),
        "region_weight": draw_region_weight(jax.random.fold_in(key_list[6], 71), part),
    }


TIME_STEP = 0.2


def shifted_lat(tracer_field, upward_flux):
    if upward_flux:
        return jnp.concatenate([tracer_field[..., 1:], tracer_field[..., -1:]], axis=-1)
    return jnp.concatenate([tracer_field[..., :1], tracer_field[..., :-1]], axis=-1)


def cycle_pad(tracer_field):
    return jnp.concatenate([tracer_field[..., -1:, :], tracer_field, tracer_field[..., :1, :]], axis=-2)


def advance(padded, kappa_pad):
    centre = padded[..., 1:-1, :]
    west_cell = padded[..., :-2, :]
    east_cell = padded[..., 2:, :]
    south_cell = shifted_lat(centre, False)
    north_cell = shifted_lat(centre, True)
    kappa_mid = kappa_pad[..., 1:-1, :]
    kappa_west = 0.5 * (kappa_mid + kappa_pad[..., :-2, :])
    kappa_east = 0.5 * (kappa_mid + kappa_pad[..., 2:, :])
    kappa_south = 0.5 * (kappa_mid + shifted_lat(kappa_mid, False))
    kappa_north = 0.5 * (kappa_mid + shifted_lat(kappa_mid, True))
    zonal_wind = centre[:, 0:1]
    merid_wind = centre[:, 1:2]
    transport = (jnp.maximum(zonal_wind, 0.0) * (centre - west_cell)
                 + jnp.minimum(zonal_wind, 0.0) * (east_cell - centre)
                 + jnp.maximum(merid_wind, 0.0) * (centre - south_cell)
                 + jnp.minimum(merid_wind, 0.0) * (north_cell - centre))
    mixing = (kappa_east * (east_cell - centre) - kappa_west * (centre - west_cell)
              + kappa_north * (north_cell - centre) - kappa_south * (centre - south_cell))
    return centre + TIME_STEP * (mixing - transport)


def measure(tracer_field, clone_weight):
    thermal_field = tracer_field[:, 2]
    return jnp.sum(clone_weight * thermal_field * thermal_field, axis=(1, 2, 3))


def reference(initial_state, ancestor, selector, perturbations, diffusivity, region_weight):
    kappa_pad = cycle_pad(diffusivity)
    cell_count = LEV * LON * LAT

    def integrate_block(present_state):
        running = jnp.zeros((present_state.shape[0],), jnp.float32)
        for section in range(STEPS):
            present_state = advance(cycle_pad(present_state), kappa_pad)
            running = running + measure(present_state, region_weight) / cell_count
        return present_state, running

    middle, first_action = integrate_block(initial_state)
    cloned = jnp.take(middle, ancestor, axis=0) + jnp.take(perturbations, selector, axis=0)
    final_state, second_action = integrate_block(cloned)
    return final_state, jnp.stack([first_action, second_action], axis=1)
```

```python
import functools
import jax
import jax.numpy as jnp
from jax import lax
from jax.experimental import pallas as pl
from jax.experimental.pallas import tpu as pltpu
from jax.sharding import PartitionSpec as P

STEPS = 3
TIME_STEP = 0.2
TILE = 8
TOP = 2 * TILE
VMEM_LIMIT = 48 * 1024 * 1024

ANY = pl.BlockSpec(memory_space=pl.ANY)
VMEM = pl.BlockSpec(memory_space=pltpu.VMEM)
SMEM = pl.BlockSpec(memory_space=pltpu.SMEM)


def call(kernel, out_shape, in_specs, out_specs, scratch_shapes, name, flops=0):
    return pl.pallas_call(
        kernel,
        out_shape=out_shape,
        in_specs=in_specs,
        out_specs=out_specs,
        scratch_shapes=scratch_shapes,
        name=name,
        compiler_params=pltpu.CompilerParams(vmem_limit_bytes=VMEM_LIMIT),
        cost_estimate=pl.CostEstimate(flops=flops, bytes_accessed=1 << 20, transcendentals=0),
    )


def f32(*shape):
    return jax.ShapeDtypeStruct(shape, jnp.float32)


def lane_steps(rows):
    lane = lax.broadcasted_iota(jnp.int32, (rows, 128), 1)
    north = jnp.where(lane == 127, 0.0, TIME_STEP).astype(jnp.float32)
    south = jnp.where(lane == 0, 0.0, TIME_STEP).astype(jnp.float32)
    return north, south


def advance(level, source, target, coef, fields, blocks):
    north_step, south_step = lane_steps(TILE)
    for block in blocks:
        row = TILE + TILE * block
        here = pl.ds(row, TILE)
        zonal = source[0, here, :]
        merid = source[1, here, :]
        spot = pl.ds(TILE * block, TILE)
        east = coef[level, 0, spot, :] - TIME_STEP * jnp.minimum(zonal, 0.0)
        west = coef[level, 1, spot, :] + TIME_STEP * jnp.maximum(zonal, 0.0)
        north = coef[level, 2, spot, :] - north_step * jnp.minimum(merid, 0.0)
        south = coef[level, 3, spot, :] + south_step * jnp.maximum(merid, 0.0)
        keep = 1.0 - ((east + west) + (north + south))
        for field in fields:
            centre = source[field, here, :]
            moved = (
                keep * centre
                + east * source[field, pl.ds(row + 1, TILE), :]
                + west * source[field, pl.ds(row - 1, TILE), :]
                + north * pltpu.roll(centre, 127, 1)
                + south * pltpu.roll(centre, 1, 1)
            )
            target[field, here, :] = moved


def observe(values, weight, rows):
    total = jnp.zeros((TILE, 128), jnp.float32)
    for block in range(rows // TILE):
        spot = values[2, pl.ds(TOP + TILE * block, TILE), :]
        total = total + weight[pl.ds(TILE * block, TILE), :] * spot * spot
    return total


def packed_rows(planes, own_planes, levels):
    chosen = 0
    own = chosen + 6 * planes
    added = own + 3 * own_planes
    kappa = added + 3 * planes
    total = kappa + 6 * levels
    return chosen, own, added, kappa, -(-total // TILE) * TILE


def relation(general, ancestor):
    if general:
        return 2
    return lax.axis_index("mem") ^ ancestor


def forward_kernel(asked, own, sister, edges, inner, sems):
    rows = own.shape[3]
    partner = lax.axis_index("mem") ^ 2
    odd = (asked[0] ^ partner) & 1

    def send(source):
        copies = [
            pltpu.make_async_copy(source.at[0, :, :, pl.ds(0, TILE), :], edges.at[:, :, pl.ds(0, TILE), :], sems.at[0]),
            pltpu.make_async_copy(
                source.at[0, :, :, pl.ds(rows - TILE, TILE), :], edges.at[:, :, pl.ds(TILE, TILE), :], sems.at[1]
            ),
            pltpu.make_async_copy(source.at[0, :, :, pl.ds(TILE, rows - 2 * TILE), :], inner, sems.at[2]),
        ]
        for copy in copies:
            copy.start()
        for copy in copies:
            copy.wait()

    @pl.when(odd == 0)
    def _():
        send(own)

    @pl.when(odd == 1)
    def _():
        send(sister)


def pack_kernel(general, ancestor, selector, own, sister, got_edges, perturbations, kappa, out_a, out_b,
                chosen, mine, added, sems):
    rows = own.shape[3]
    fields, levels = own.shape[1], own.shape[2]
    rel = relation(general, ancestor[0])
    low, high = pl.ds(0, TILE), pl.ds(rows - TILE, TILE)

    def edge_copies(source, target, first):
        return [
            pltpu.make_async_copy(source.at[:, :, low, :], target.at[:, :, pl.ds(0, TILE), :], sems.at[first]),
            pltpu.make_async_copy(source.at[:, :, high, :], target.at[:, :, pl.ds(TILE, TILE), :], sems.at[first + 1]),
        ]

    waits = edge_copies(own.at[0], mine, 0) + edge_copies(perturbations.at[selector[0]], added, 2)
    for copy in waits:
        copy.start()

    @pl.when(rel == 0)
    def _():
        for copy in edge_copies(own.at[0], chosen, 4):
            copy.start()
            copy.wait()

    @pl.when(rel == 1)
    def _():
        for copy in edge_copies(sister.at[0], chosen, 4):
            copy.start()
            copy.wait()

    @pl.when(rel > 1)
    def _():
        copy = pltpu.make_async_copy(got_edges, chosen, sems.at[4])
        copy.start()
        copy.wait()

    for copy in waits:
        copy.wait()
    even = lax.rem(lax.axis_index("lon"), 2) == 0

    def put(offset, low_rows, high_rows):
        count = low_rows.shape[0]
        out_a[pl.ds(offset, count), :] = jnp.where(even, high_rows, low_rows)
        out_b[pl.ds(offset, count), :] = jnp.where(even, low_rows, high_rows)

    at_chosen, at_own, at_added, at_kappa, _ = packed_rows(fields * levels, 3 * levels, levels)
    for field in range(fields):
        for level in range(levels):
            plane = field * levels + level
            put(at_chosen + 6 * plane, chosen[field, level, 0:6, :], chosen[field, level, 10:16, :])
            if field < 3:
                put(at_own + 3 * plane, mine[field, level, 0:3, :], mine[field, level, 13:16, :])
            put(at_added + 3 * plane, added[field, level, 0:3, :], added[field, level, 13:16, :])
    for level in range(levels):
        put(at_kappa + 6 * level, kappa[level, 0:6, :], kappa[level, rows - 6 : rows, :])


def first_kernel(own, kappa, weight, got_a, got_b, coef, action, halo, present, following, padded, sem):
    fields, levels, rows = own.shape[1], own.shape[2], own.shape[3]
    even = lax.rem(lax.axis_index("lon"), 2) == 0
    a, b = got_a[...], got_b[...]
    halo[0] = jnp.where(even, b, a)
    halo[1] = jnp.where(even, a, b)
    _, at_own, _, at_kappa, _ = packed_rows(fields * levels, 3 * levels, levels)
    blocks = rows // TILE + 2
    end = TOP + rows
    north_step, south_step = lane_steps(TILE)
    for level in range(levels):
        padded[level, pl.ds(TOP, rows), :] = kappa[level]
        padded[level, pl.ds(TOP - 6, 6), :] = halo[0, pl.ds(at_kappa + 6 * level, 6), :]
        padded[level, pl.ds(end, 6), :] = halo[1, pl.ds(at_kappa + 6 * level, 6), :]
        for field in range(3):
            plane = field * levels + level
            present[level, field, pl.ds(TOP, rows), :] = own[0, field, level]
            present[level, field, pl.ds(TOP - 3, 3), :] = halo[0, pl.ds(at_own + 3 * plane, 3), :]
            present[level, field, pl.ds(end, 3), :] = halo[1, pl.ds(at_own + 3 * plane, 3), :]

    def each(level, total):
        for block in range(blocks):
            row = TILE + TILE * block
            spot = pl.ds(TILE * block, TILE)
            centre = padded[level, pl.ds(row, TILE), :]
            half = 0.5 * TIME_STEP
            coef[level, 0, spot, :] = half * (centre + padded[level, pl.ds(row + 1, TILE), :])
            coef[level, 1, spot, :] = half * (centre + padded[level, pl.ds(row - 1, TILE), :])
            coef[level, 2, spot, :] = (0.5 * north_step) * (centre + pltpu.roll(centre, 127, 1))
            coef[level, 3, spot, :] = (0.5 * south_step) * (centre + pltpu.roll(centre, 1, 1))
        now, later = present.at[level], following
        for step in range(STEPS):
            last = step == STEPS - 1
            advance(level, now, later, coef, (2,) if last else (0, 1, 2), range(1, blocks - 1) if last else range(blocks))
            total = total + observe(later, weight, rows)
            now, later = later, now
        return total

    action[...] = lax.fori_loop(0, levels, each, jnp.zeros((TILE, 128), jnp.float32))


def second_kernel(general, scale, ancestor, selector, own, sister, got_edges, got_inner, perturbations, got_a, got_b,
                  coef, weight, action, final, sums, halo, present, following, added, sems):
    fields, levels, rows = own.shape[1], own.shape[2], own.shape[3]
    rel = relation(general, ancestor[0])
    bump = pltpu.make_async_copy(perturbations.at[selector[0]], added.at[:, :, pl.ds(TOP, rows), :], sems.at[0])
    bump.start()
    strip = pl.ds(TOP, rows)

    def whole(source):
        copy = pltpu.make_async_copy(source.at[0], present.at[:, :, strip, :], sems.at[1])
        copy.start()
        copy.wait()

    @pl.when(rel == 0)
    def _():
        whole(own)

    @pl.when(rel == 1)
    def _():
        whole(sister)

    @pl.when(rel > 1)
    def _():
        copies = [
            pltpu.make_async_copy(got_edges.at[:, :, pl.ds(0, TILE), :], present.at[:, :, pl.ds(TOP, TILE), :], sems.at[1]),
            pltpu.make_async_copy(
                got_edges.at[:, :, pl.ds(TILE, TILE), :], present.at[:, :, pl.ds(TOP + rows - TILE, TILE), :], sems.at[2]
            ),
            pltpu.make_async_copy(got_inner, present.at[:, :, pl.ds(TOP + TILE, rows - 2 * TILE), :], sems.at[3]),
        ]
        for copy in copies:
            copy.start()
        for copy in copies:
            copy.wait()

    even = lax.rem(lax.axis_index("lon"), 2) == 0
    a, b = got_a[...], got_b[...]
    halo[0] = jnp.where(even, b, a)
    halo[1] = jnp.where(even, a, b)
    at_chosen, _, at_added, _, _ = packed_rows(fields * levels, 3 * levels, levels)
    end = TOP + rows
    for field in range(fields):
        for level in range(levels):
            plane = field * levels + level
            present[field, level, pl.ds(TOP - 6, 6), :] = halo[0, pl.ds(at_chosen + 6 * plane, 6), :]
            present[field, level, pl.ds(end, 6), :] = halo[1, pl.ds(at_chosen + 6 * plane, 6), :]
            added[field, level, pl.ds(TOP - 3, 3), :] = halo[0, pl.ds(at_added + 3 * plane, 3), :]
            added[field, level, pl.ds(end, 3), :] = halo[1, pl.ds(at_added + 3 * plane, 3), :]
    bump.wait()
    blocks = rows // TILE + 2

    def each(level, total):
        now, later = present.at[:, level], following
        for step in range(2 * STEPS):
            last = step == 2 * STEPS - 1
            advance(level, now, later, coef, range(fields), range(1, blocks - 1) if last else range(blocks))
            if step == STEPS - 1:
                for field in range(fields):
                    for block in range(blocks):
                        spot = pl.ds(TILE + TILE * block, TILE)
                        later[field, spot, :] = later[field, spot, :] + added[field, level, spot, :]
            if step >= STEPS:
                total = total + observe(later, weight, rows)
            now, later = later, now
        for field in range(fields):
            final[0, field, level] = now[field, pl.ds(TOP, rows), :]
        return total

    total = lax.fori_loop(0, levels, each, jnp.zeros((TILE, 128), jnp.float32))
    first = jnp.sum(action[...]) * scale
    second = jnp.sum(total) * scale
    lane = lax.broadcasted_iota(jnp.int32, (1, 128), 1)
    sums[...] = jnp.where(lane == 0, first, jnp.where(lane == 1, second, 0.0))


def body(initial_state, ancestor, selector, perturbations, diffusivity, region_weight):
    _, fields, levels, rows, lat = initial_state.shape
    members, strips = lax.axis_size("mem"), lax.axis_size("lon")
    planes = fields * levels
    general = members != 4
    scale = 1.0 / (levels * lat * rows * strips)

    def across(value, axis, bit):
        return lax.ppermute(value, axis, [(i, i ^ bit) for i in range(lax.axis_size(axis))])

    ancestor = jnp.clip(ancestor, 0, members - 1)
    if general:
        gathered = lax.all_gather(initial_state, "mem", axis=0, tiled=True)
        picked = jnp.take(gathered, ancestor, axis=0)[0]
        sister = initial_state
        got_edges = jnp.concatenate([picked[:, :, :TILE], picked[:, :, rows - TILE :]], axis=2)
        got_inner = picked[:, :, TILE : rows - TILE]
    else:
        asked = across(ancestor, "mem", 2)
        sister = across(initial_state, "mem", 1)
        edges, inner = call(
            forward_kernel,
            (f32(fields, levels, 2 * TILE, lat), f32(fields, levels, rows - 2 * TILE, lat)),
            [SMEM, ANY, ANY],
            (ANY, ANY),
            [pltpu.SemaphoreType.DMA((3,))],
            "forward",
        )(asked, initial_state, sister)
        got_edges = across(edges, "mem", 2)
        got_inner = across(inner, "mem", 2)

    total_rows = packed_rows(planes, 3 * levels, levels)[-1]
    edge_scratch = pltpu.VMEM((fields, levels, 2 * TILE, lat), jnp.float32)
    to_a, to_b = call(
        functools.partial(pack_kernel, general),
        (f32(total_rows, lat), f32(total_rows, lat)),
        [SMEM, SMEM, ANY, ANY, ANY, ANY, VMEM],
        (VMEM, VMEM),
        [edge_scratch, edge_scratch, edge_scratch, pltpu.SemaphoreType.DMA((6,))],
        "pack",
    )(ancestor, selector, initial_state, sister, got_edges, perturbations, diffusivity)
    pairs_a = [(i, i ^ 1) for i in range(strips)]
    pairs_b = [(i, (i + 1 if i % 2 else i - 1) % strips) for i in range(strips)]
    got_a = lax.ppermute(to_a, "lon", pairs_a)
    got_b = lax.ppermute(to_b, "lon", pairs_b)

    padded = rows + 2 * TOP
    coef, action = call(
        first_kernel,
        (f32(levels, 4, rows + 2 * TILE, lat), f32(TILE, lat)),
        [VMEM] * 5,
        (VMEM, VMEM),
        [
            pltpu.VMEM((2, total_rows, lat), jnp.float32),
            pltpu.VMEM((levels, 3, padded, lat), jnp.float32),
            pltpu.VMEM((3, padded, lat), jnp.float32),
            pltpu.VMEM((levels, padded, lat), jnp.float32),
            pltpu.SemaphoreType.DMA,
        ],
        "first_window",
    )(initial_state, diffusivity, region_weight, got_a, got_b)
    final_state, sums = call(
        functools.partial(second_kernel, general, scale),
        (f32(1, fields, levels, rows, lat), f32(1, lat)),
        [SMEM, SMEM, ANY, ANY, ANY, ANY, ANY, VMEM, VMEM, VMEM, VMEM, VMEM],
        (VMEM, VMEM),
        [
            pltpu.VMEM((2, total_rows, lat), jnp.float32),
            pltpu.VMEM((fields, levels, padded, lat), jnp.float32),
            pltpu.VMEM((fields, padded, lat), jnp.float32),
            pltpu.VMEM((fields, levels, padded, lat), jnp.float32),
            pltpu.SemaphoreType.DMA((4,)),
        ],
        "clone_window",
    )(ancestor, selector, initial_state, sister, got_edges, got_inner, perturbations, got_a, got_b, coef, region_weight, action)
    bit = 1
    while bit < strips:
        sums = sums + across(sums, "lon", bit)
        bit *= 2
    return final_state, sums[:, :2]


def solution(mesh):
    in_specs = (
        P(("ens", "mem"), None, None, "lon", None),
        P(("ens", "mem")),
        P(("ens", "mem")),
        P("ens", None, None, "lon", None),
        P(None, "lon", None),
        P("lon", None),
    )
    out_specs = (P(("ens", "mem"), None, None, "lon", None), P(("ens", "mem"), None))
    return jax.shard_map(body, mesh=mesh, in_specs=in_specs, out_specs=out_specs, check_vma=False)
```

```python
import functools
import jax
import jax.numpy as jnp
from jax import lax
from jax.experimental import pallas as pl
from jax.experimental.pallas import tpu as pltpu
from jax.sharding import PartitionSpec as P

STEPS = 3
TIME_STEP = 0.2
TILE = 8
TOP = 2 * TILE
CUTS = (0, 2, 4)
VMEM_LIMIT = 48 * 1024 * 1024

ANY = pl.BlockSpec(memory_space=pl.ANY)
HBM = pl.BlockSpec(memory_space=pltpu.HBM)
VMEM = pl.BlockSpec(memory_space=pltpu.VMEM)
SMEM = pl.BlockSpec(memory_space=pltpu.SMEM)


def call(kernel, out_shape, in_specs, out_specs, scratch_shapes, name, flops=0):
    return pl.pallas_call(
        kernel,
        out_shape=out_shape,
        in_specs=in_specs,
        out_specs=out_specs,
        scratch_shapes=scratch_shapes,
        name=name,
        compiler_params=pltpu.CompilerParams(vmem_limit_bytes=VMEM_LIMIT),
        cost_estimate=pl.CostEstimate(flops=flops, bytes_accessed=1 << 20, transcendentals=0),
    )


def f32(*shape):
    return jax.ShapeDtypeStruct(shape, jnp.float32)


def lane_steps(rows):
    lane = lax.broadcasted_iota(jnp.int32, (rows, 128), 1)
    north = jnp.where(lane == 127, 0.0, TIME_STEP).astype(jnp.float32)
    south = jnp.where(lane == 0, 0.0, TIME_STEP).astype(jnp.float32)
    return north, south


def advance(level, source, target, coef, fields, blocks):
    north_step, south_step = lane_steps(TILE)
    for block in blocks:
        row = TILE + TILE * block
        here = pl.ds(row, TILE)
        zonal = source[0, here, :]
        merid = source[1, here, :]
        spot = pl.ds(TILE * block, TILE)
        east = coef[level, 0, spot, :] - TIME_STEP * jnp.minimum(zonal, 0.0)
        west = coef[level, 1, spot, :] + TIME_STEP * jnp.maximum(zonal, 0.0)
        north = coef[level, 2, spot, :] - north_step * jnp.minimum(merid, 0.0)
        south = coef[level, 3, spot, :] + south_step * jnp.maximum(merid, 0.0)
        keep = 1.0 - ((east + west) + (north + south))
        for field in fields:
            centre = source[field, here, :]
            moved = (
                keep * centre
                + east * source[field, pl.ds(row + 1, TILE), :]
                + west * source[field, pl.ds(row - 1, TILE), :]
                + north * pltpu.roll(centre, 127, 1)
                + south * pltpu.roll(centre, 1, 1)
            )
            target[field, here, :] = moved


def observe(values, weight, rows):
    total = jnp.zeros((TILE, 128), jnp.float32)
    for block in range(rows // TILE):
        spot = values[2, pl.ds(TOP + TILE * block, TILE), :]
        total = total + weight[pl.ds(TILE * block, TILE), :] * spot * spot
    return total


def early_rows(planes, own_planes, levels):
    own = 0
    added = own + 3 * own_planes
    kappa = added + 3 * planes
    total = kappa + 6 * levels
    return own, added, kappa, -(-total // TILE) * TILE


def relation(general, ancestor):
    if general:
        return 2
    return lax.axis_index("mem") ^ ancestor


def run(copies):
    for copy in copies:
        copy.start()
    for copy in copies:
        copy.wait()


def edge_copies(source, target, sems, first):
    rows = source.shape[2]
    return [
        pltpu.make_async_copy(source.at[:, :, pl.ds(0, TILE), :], target.at[:, :, pl.ds(0, TILE), :], sems.at[first]),
        pltpu.make_async_copy(
            source.at[:, :, pl.ds(rows - TILE, TILE), :], target.at[:, :, pl.ds(TILE, TILE), :], sems.at[first + 1]
        ),
    ]


def edge_kernel(own, edges, sems):
    run(edge_copies(own.at[0], edges, sems, 0))


def forward_kernel(asked, own, sister, edges, *refs):
    rows = own.shape[3]
    odd = (asked[0] ^ lax.axis_index("mem")) & 1
    middle = pl.ds(TILE, rows - 2 * TILE)
    *inner, sems = refs

    def send(source):
        run([
            pltpu.make_async_copy(source.at[0, pl.ds(low, high - low), :, middle, :], part, sems.at[i])
            for i, (low, high, part) in enumerate(zip(CUTS, CUTS[1:], inner))
        ])

    @pl.when(odd == 0)
    def _():
        send(own)

    @pl.when(odd == 1)
    def _():
        send(sister)


def pair_put(out_a, out_b, even, offset, low_rows, high_rows):
    spot = pl.ds(offset, low_rows.shape[0])
    out_a[spot, :] = jnp.where(even, high_rows, low_rows)
    out_b[spot, :] = jnp.where(even, low_rows, high_rows)


def pair_get(halo, got_a, got_b, even):
    a, b = got_a[...], got_b[...]
    halo[0] = jnp.where(even, b, a)
    halo[1] = jnp.where(even, a, b)


def even_strip():
    return lax.rem(lax.axis_index("lon"), 2) == 0


def early_kernel(selector, edges, perturbations, kappa, out_a, out_b, added, sems):
    fields, levels = edges.shape[:2]
    rows = kappa.shape[1]
    which = jnp.clip(selector[0], 0, perturbations.shape[0] - 1)
    run(edge_copies(perturbations.at[which], added, sems, 0))
    even = even_strip()
    put = functools.partial(pair_put, out_a, out_b, even)
    at_own, at_added, at_kappa, _ = early_rows(fields * levels, 3 * levels, levels)
    for field in range(fields):
        for level in range(levels):
            plane = field * levels + level
            if field < 3:
                put(at_own + 3 * plane, edges[field, level, 0:3, :], edges[field, level, 13:16, :])
            put(at_added + 3 * plane, added[field, level, 0:3, :], added[field, level, 13:16, :])
    for level in range(levels):
        put(at_kappa + 6 * level, kappa[level, 0:6, :], kappa[level, rows - 6 : rows, :])


def late_kernel(general, ancestor, edges, sister, got_edges, got_odd, out_a, out_b, chosen, sems):
    fields, levels = edges.shape[:2]
    rel = relation(general, ancestor[0])

    @pl.when(rel == 0)
    def _():
        run([pltpu.make_async_copy(edges, chosen, sems.at[0])])

    @pl.when(rel == 1)
    def _():
        run(edge_copies(sister.at[0], chosen, sems, 0))

    @pl.when(rel == 2)
    def _():
        run([pltpu.make_async_copy(got_edges, chosen, sems.at[0])])

    @pl.when(rel > 2)
    def _():
        run([pltpu.make_async_copy(got_odd, chosen, sems.at[0])])

    even = even_strip()
    for field in range(fields):
        for level in range(levels):
            at = 6 * (field * levels + level)
            pair_put(out_a, out_b, even, at, chosen[field, level, 0:6, :], chosen[field, level, 10:16, :])


def first_kernel(own, kappa, weight, got_a, got_b, coef, action, halo, present, following, padded):
    fields, levels, rows = own.shape[1], own.shape[2], own.shape[3]
    pair_get(halo, got_a, got_b, even_strip())
    at_own, _, at_kappa, _ = early_rows(fields * levels, 3 * levels, levels)
    blocks = rows // TILE + 2
    end = TOP + rows
    north_step, south_step = lane_steps(TILE)
    for level in range(levels):
        padded[level, pl.ds(TOP, rows), :] = kappa[level]
        padded[level, pl.ds(TOP - 6, 6), :] = halo[0, pl.ds(at_kappa + 6 * level, 6), :]
        padded[level, pl.ds(end, 6), :] = halo[1, pl.ds(at_kappa + 6 * level, 6), :]
        for field in range(3):
            plane = field * levels + level
            present[level, field, pl.ds(TOP, rows), :] = own[0, field, level]
            present[level, field, pl.ds(TOP - 3, 3), :] = halo[0, pl.ds(at_own + 3 * plane, 3), :]
            present[level, field, pl.ds(end, 3), :] = halo[1, pl.ds(at_own + 3 * plane, 3), :]

    def each(level, total):
        for block in range(blocks):
            row = TILE + TILE * block
            spot = pl.ds(TILE * block, TILE)
            centre = padded[level, pl.ds(row, TILE), :]
            half = 0.5 * TIME_STEP
            coef[level, 0, spot, :] = half * (centre + padded[level, pl.ds(row + 1, TILE), :])
            coef[level, 1, spot, :] = half * (centre + padded[level, pl.ds(row - 1, TILE), :])
            coef[level, 2, spot, :] = (0.5 * north_step) * (centre + pltpu.roll(centre, 127, 1))
            coef[level, 3, spot, :] = (0.5 * south_step) * (centre + pltpu.roll(centre, 1, 1))
        now, later = present.at[level], following
        for step in range(STEPS):
            last = step == STEPS - 1
            advance(level, now, later, coef, (2,) if last else (0, 1, 2), range(1, blocks - 1) if last else range(blocks))
            total = total + observe(later, weight, rows)
            now, later = later, now
        return total

    action[...] = lax.fori_loop(0, levels, each, jnp.zeros((TILE, 128), jnp.float32))


def clone_kernel(general, scale, ancestor, selector, own, sister, got_edges, got_odd, perturbations,
                 early_a, early_b, late_a, late_b, coef, weight, action, *refs):
    parts = len(CUTS) - 1
    got_inner, refs = refs[:parts], refs[parts:]
    final, sums, early, late, present, following, added, chosen_sems, bump_sem, out_sems = refs
    fields, levels, rows = own.shape[1], own.shape[2], own.shape[3]
    rel = relation(general, ancestor[0])
    which = jnp.clip(selector[0], 0, perturbations.shape[0] - 1)
    end = TOP + rows
    strip = pl.ds(TOP, rows)

    def whole(source):
        for level in range(levels):
            pltpu.make_async_copy(source.at[0, :, level], present.at[:, level, strip, :], chosen_sems.at[level]).start()

    def joined(edges):
        for level in range(levels):
            inner = [
                (part.at[:, level], present.at[pl.ds(low, high - low), level, pl.ds(TOP + TILE, rows - 2 * TILE), :])
                for low, high, part in zip(CUTS, CUTS[1:], got_inner)
            ]
            for source, target in [
                (edges.at[:, level, pl.ds(0, TILE), :], present.at[:, level, pl.ds(TOP, TILE), :]),
                (edges.at[:, level, pl.ds(TILE, TILE), :], present.at[:, level, pl.ds(end - TILE, TILE), :]),
                *inner,
            ]:
                pltpu.make_async_copy(source, target, chosen_sems.at[level]).start()

    @pl.when(rel == 0)
    def _():
        whole(own)

    @pl.when(rel == 1)
    def _():
        whole(sister)

    @pl.when(rel == 2)
    def _():
        joined(got_edges)

    @pl.when(rel > 2)
    def _():
        joined(got_odd)

    bump = pltpu.make_async_copy(perturbations.at[which], added.at[:, :, strip, :], bump_sem)
    bump.start()
    even = even_strip()
    pair_get(early, early_a, early_b, even)
    pair_get(late, late_a, late_b, even)
    _, at_added, _, _ = early_rows(fields * levels, 3 * levels, levels)
    for field in range(fields):
        for level in range(levels):
            plane = field * levels + level
            present[field, level, pl.ds(TOP - 6, 6), :] = late[0, pl.ds(6 * plane, 6), :]
            present[field, level, pl.ds(end, 6), :] = late[1, pl.ds(6 * plane, 6), :]
            added[field, level, pl.ds(TOP - 3, 3), :] = early[0, pl.ds(at_added + 3 * plane, 3), :]
            added[field, level, pl.ds(end, 3), :] = early[1, pl.ds(at_added + 3 * plane, 3), :]
    bump.wait()
    blocks = rows // TILE + 2

    def each(level, total):
        pltpu.make_async_copy(own.at[0, :, level], present.at[:, level, strip, :], chosen_sems.at[level]).wait()
        now, later = present.at[:, level], following
        for step in range(2 * STEPS):
            last = step == 2 * STEPS - 1
            advance(level, now, later, coef, range(fields), range(1, blocks - 1) if last else range(blocks))
            if step == STEPS - 1:
                for field in range(fields):
                    for block in range(blocks):
                        spot = pl.ds(TILE + TILE * block, TILE)
                        later[field, spot, :] = later[field, spot, :] + added[field, level, spot, :]
            if step >= STEPS:
                total = total + observe(later, weight, rows)
            now, later = later, now
        pltpu.make_async_copy(now.at[:, strip, :], final.at[0, :, level], out_sems.at[level]).start()
        return total

    total = lax.fori_loop(0, levels, each, jnp.zeros((TILE, 128), jnp.float32))
    first = jnp.sum(action[...]) * scale
    second = jnp.sum(total) * scale
    lane = lax.broadcasted_iota(jnp.int32, (1, 128), 1)
    sums[...] = jnp.where(lane == 0, first, jnp.where(lane == 1, second, 0.0))
    for level in range(levels):
        pltpu.make_async_copy(present.at[:, level, strip, :], final.at[0, :, level], out_sems.at[level]).wait()


def body(initial_state, ancestor, selector, perturbations, diffusivity, region_weight):
    _, fields, levels, rows, lat = initial_state.shape
    members, strips = lax.axis_size("mem"), lax.axis_size("lon")
    planes = fields * levels
    general = members != 4
    scale = 1.0 / (levels * lat * rows * strips)
    dma = pltpu.SemaphoreType.DMA
    edge_shape = f32(fields, levels, 2 * TILE, lat)

    def across(value, axis, bit):
        return lax.ppermute(value, axis, [(i, i ^ bit) for i in range(lax.axis_size(axis))])

    def round_strips(a, b):
        pairs_a = [(i, i ^ 1) for i in range(strips)]
        pairs_b = [(i, (i + 1 if i % 2 else i - 1) % strips) for i in range(strips)]
        return lax.ppermute(a, "lon", pairs_a), lax.ppermute(b, "lon", pairs_b)

    own = pltpu.with_memory_space_constraint(initial_state, pltpu.HBM)
    perturbations = pltpu.with_memory_space_constraint(perturbations, pltpu.HBM)
    if not general:
        asked = across(ancestor, "mem", 2)
        sister = across(initial_state, "mem", 1)
    edges = call(edge_kernel, edge_shape, [HBM], ANY, [dma((2,))], "edges")(own)
    if general:
        gathered = lax.all_gather(initial_state, "mem", axis=0, tiled=True)
        picked = jnp.take(gathered, ancestor, axis=0)[0]
        sister = initial_state
        got_edges = got_odd = jnp.concatenate([picked[:, :, :TILE], picked[:, :, rows - TILE :]], axis=2)
        got_inner = [picked[low:high, :, TILE : rows - TILE] for low, high in zip(CUTS, CUTS[1:])]
    else:
        got_edges = across(edges, "mem", 2)
        inner = call(
            forward_kernel,
            [f32(high - low, levels, rows - 2 * TILE, lat) for low, high in zip(CUTS, CUTS[1:])],
            [SMEM, HBM, ANY, ANY],
            [ANY] * (len(CUTS) - 1),
            [dma((len(CUTS) - 1,))],
            "forward",
        )(asked, own, sister, edges)
        got_inner = [across(part, "mem", 2) for part in inner]
        got_odd = across(got_edges, "mem", 1)

    early_total = early_rows(planes, 3 * levels, levels)[-1]
    early = call(
        early_kernel,
        (f32(early_total, lat), f32(early_total, lat)),
        [SMEM, VMEM, HBM, VMEM],
        (VMEM, VMEM),
        [pltpu.VMEM(edge_shape.shape, jnp.float32), dma((2,))],
        "early_halo",
    )(selector, edges, perturbations, diffusivity)
    early = round_strips(*early)
    late = call(
        functools.partial(late_kernel, general),
        (f32(6 * planes, lat), f32(6 * planes, lat)),
        [SMEM, ANY, ANY, ANY, ANY],
        (VMEM, VMEM),
        [pltpu.VMEM(edge_shape.shape, jnp.float32), dma((2,))],
        "late_halo",
    )(ancestor, edges, sister, got_edges, got_odd)
    late = round_strips(*late)

    padded = rows + 2 * TOP
    coef, action = call(
        first_kernel,
        (f32(levels, 4, rows + 2 * TILE, lat), f32(TILE, lat)),
        [VMEM] * 5,
        (VMEM, VMEM),
        [
            pltpu.VMEM((2, early_total, lat), jnp.float32),
            pltpu.VMEM((levels, 3, padded, lat), jnp.float32),
            pltpu.VMEM((3, padded, lat), jnp.float32),
            pltpu.VMEM((levels, padded, lat), jnp.float32),
        ],
        "first_window",
    )(own, diffusivity, region_weight, *early)
    final_state, sums = call(
        functools.partial(clone_kernel, general, scale),
        (f32(1, fields, levels, rows, lat), f32(1, lat)),
        [SMEM, SMEM, HBM, ANY, ANY, ANY, HBM] + [VMEM] * 7 + [ANY] * len(got_inner),
        (HBM, VMEM),
        [
            pltpu.VMEM((2, early_total, lat), jnp.float32),
            pltpu.VMEM((2, 6 * planes, lat), jnp.float32),
            pltpu.VMEM((fields, levels, padded, lat), jnp.float32),
            pltpu.VMEM((fields, padded, lat), jnp.float32),
            pltpu.VMEM((fields, levels, padded, lat), jnp.float32),
            dma((levels,)),
            dma,
            dma((levels,)),
        ],
        "clone_window",
    )(ancestor, selector, own, sister, got_edges, got_odd, perturbations, *early, *late,
      coef, region_weight, action, *got_inner)
    if strips == 4:
        one, two, three = [across(sums, "lon", bit) for bit in (1, 2, 3)]
        sums = (sums + one) + (two + three)
    else:
        bit = 1
        while bit < strips:
            sums = sums + across(sums, "lon", bit)
            bit *= 2
    return final_state, sums[:, :2]


def solution(mesh):
    in_specs = (
        P(("ens", "mem"), None, None, "lon", None),
        P(("ens", "mem")),
        P(("ens", "mem")),
        P("ens", None, None, "lon", None),
        P(None, "lon", None),
        P("lon", None),
    )
    out_specs = (P(("ens", "mem"), None, None, "lon", None), P(("ens", "mem"), None))
    return jax.shard_map(body, mesh=mesh, in_specs=in_specs, out_specs=out_specs, check_vma=False)
```

```python
import functools
import jax
import jax.numpy as jnp
from jax import lax
from jax.experimental import pallas as pl
from jax.experimental.pallas import tpu as pltpu
from jax.sharding import PartitionSpec as P

STEPS = 3
TIME_STEP = 0.2
TILE = 8
TOP = 2 * TILE
CUTS = (0, 2, 4)
VMEM_LIMIT = 48 * 1024 * 1024

ANY = pl.BlockSpec(memory_space=pl.ANY)
HBM = pl.BlockSpec(memory_space=pltpu.HBM)
VMEM = pl.BlockSpec(memory_space=pltpu.VMEM)
SMEM = pl.BlockSpec(memory_space=pltpu.SMEM)


def call(kernel, out_shape, in_specs, out_specs, scratch_shapes, name, flops=0):
    return pl.pallas_call(
        kernel,
        out_shape=out_shape,
        in_specs=in_specs,
        out_specs=out_specs,
        scratch_shapes=scratch_shapes,
        name=name,
        compiler_params=pltpu.CompilerParams(vmem_limit_bytes=VMEM_LIMIT),
        cost_estimate=pl.CostEstimate(flops=flops, bytes_accessed=1 << 20, transcendentals=0),
    )


def f32(*shape):
    return jax.ShapeDtypeStruct(shape, jnp.float32)


def lane_steps(rows):
    lane = lax.broadcasted_iota(jnp.int32, (rows, 128), 1)
    north = jnp.where(lane == 127, 0.0, TIME_STEP).astype(jnp.float32)
    south = jnp.where(lane == 0, 0.0, TIME_STEP).astype(jnp.float32)
    return north, south


def advance(level, source, target, coef, fields, blocks):
    north_step, south_step = lane_steps(TILE)
    for block in blocks:
        row = TILE + TILE * block
        here = pl.ds(row, TILE)
        zonal = source[0, here, :]
        merid = source[1, here, :]
        spot = pl.ds(TILE * block, TILE)
        east = coef[level, 0, spot, :] - TIME_STEP * jnp.minimum(zonal, 0.0)
        west = coef[level, 1, spot, :] + TIME_STEP * jnp.maximum(zonal, 0.0)
        north = coef[level, 2, spot, :] - north_step * jnp.minimum(merid, 0.0)
        south = coef[level, 3, spot, :] + south_step * jnp.maximum(merid, 0.0)
        keep = 1.0 - ((east + west) + (north + south))
        for field in fields:
            centre = source[field, here, :]
            moved = (
                keep * centre
                + east * source[field, pl.ds(row + 1, TILE), :]
                + west * source[field, pl.ds(row - 1, TILE), :]
                + north * pltpu.roll(centre, 127, 1)
                + south * pltpu.roll(centre, 1, 1)
            )
            target[field, here, :] = moved


def observe(values, weight, rows):
    total = jnp.zeros((TILE, 128), jnp.float32)
    for block in range(rows // TILE):
        spot = values[2, pl.ds(TOP + TILE * block, TILE), :]
        total = total + weight[pl.ds(TILE * block, TILE), :] * spot * spot
    return total


def early_rows(planes, own_planes, levels):
    own = 0
    added = own + 3 * own_planes
    kappa = added + 3 * planes
    total = kappa + 6 * levels
    return own, added, kappa, -(-total // TILE) * TILE


def relation(general, ancestor):
    if general:
        return 2
    return lax.axis_index("mem") ^ ancestor


def run(copies):
    for copy in copies:
        copy.start()
    for copy in copies:
        copy.wait()


def edge_copies(source, target, sems, first):
    rows = source.shape[2]
    return [
        pltpu.make_async_copy(source.at[:, :, pl.ds(0, TILE), :], target.at[:, :, pl.ds(0, TILE), :], sems.at[first]),
        pltpu.make_async_copy(
            source.at[:, :, pl.ds(rows - TILE, TILE), :], target.at[:, :, pl.ds(TILE, TILE), :], sems.at[first + 1]
        ),
    ]


def pair_put(out_a, out_b, even, offset, low_rows, high_rows):
    spot = pl.ds(offset, low_rows.shape[0])
    out_a[spot, :] = jnp.where(even, high_rows, low_rows)
    out_b[spot, :] = jnp.where(even, low_rows, high_rows)


def pair_get(halo, got_a, got_b, even):
    a, b = got_a[...], got_b[...]
    halo[0] = jnp.where(even, b, a)
    halo[1] = jnp.where(even, a, b)


def even_strip():
    return lax.rem(lax.axis_index("lon"), 2) == 0


def start_kernel(selector, own, perturbations, kappa, edges, out_a, out_b, added, ends, sems):
    fields, levels, rows = own.shape[1:4]
    which = jnp.clip(selector[0], 0, perturbations.shape[0] - 1)
    low, high = pl.ds(0, TILE), pl.ds(TILE, TILE)
    first = edge_copies(own.at[0], edges, sems, 0) + edge_copies(perturbations.at[which], added, sems, 2)
    first += [
        pltpu.make_async_copy(kappa.at[:, low, :], ends.at[:, low, :], sems.at[4]),
        pltpu.make_async_copy(kappa.at[:, pl.ds(rows - TILE, TILE), :], ends.at[:, high, :], sems.at[5]),
    ]
    for copy in first:
        copy.start()
    for copy in first:
        copy.wait()
    even = even_strip()
    put = functools.partial(pair_put, out_a, out_b, even)
    at_own, at_added, at_kappa, _ = early_rows(fields * levels, 3 * levels, levels)
    for field in range(fields):
        for level in range(levels):
            plane = field * levels + level
            if field < 3:
                put(at_own + 3 * plane, edges[field, level, 0:3, :], edges[field, level, 13:16, :])
            put(at_added + 3 * plane, added[field, level, 0:3, :], added[field, level, 13:16, :])
    for level in range(levels):
        put(at_kappa + 6 * level, ends[level, 0:6, :], ends[level, 10:16, :])


def inner_kernel(own, *refs):
    *inner, sems = refs
    rows = own.shape[3]
    run([
        pltpu.make_async_copy(
            own.at[0, pl.ds(start, stop - start), :, pl.ds(TILE, rows - 2 * TILE), :], part, sems.at[i]
        )
        for i, (start, stop, part) in enumerate(zip(CUTS, CUTS[1:], inner))
    ])


def late_kernel(general, ancestor, edges, sister, got_edges, got_odd, out_a, out_b, chosen, sems):
    fields, levels = edges.shape[:2]
    rel = relation(general, ancestor[0])

    @pl.when(rel == 0)
    def _():
        run([pltpu.make_async_copy(edges, chosen, sems.at[0])])

    @pl.when(rel == 1)
    def _():
        run(edge_copies(sister.at[0], chosen, sems, 0))

    @pl.when(rel == 2)
    def _():
        run([pltpu.make_async_copy(got_edges, chosen, sems.at[0])])

    @pl.when(rel > 2)
    def _():
        run([pltpu.make_async_copy(got_odd, chosen, sems.at[0])])

    even = even_strip()
    for field in range(fields):
        for level in range(levels):
            at = 6 * (field * levels + level)
            pair_put(out_a, out_b, even, at, chosen[field, level, 0:6, :], chosen[field, level, 10:16, :])


def prepare_kernel(selector, own, kappa, weight, perturbations, got_a, got_b, coef, action, added,
                   halo, present, following, padded, sems):
    fields, levels, rows = own.shape[1:4]
    which = jnp.clip(selector[0], 0, perturbations.shape[0] - 1)
    strip = pl.ds(TOP, rows)
    copies = [
        pltpu.make_async_copy(kappa, padded.at[:, strip, :], sems.at[0]),
        pltpu.make_async_copy(own.at[0, pl.ds(0, 3)], present.at[:, :, strip, :], sems.at[1]),
        pltpu.make_async_copy(perturbations.at[which], added.at[:, :, strip, :], sems.at[2]),
    ]
    for copy in copies:
        copy.start()
    pair_get(halo, got_a, got_b, even_strip())
    at_own, at_added, at_kappa, _ = early_rows(fields * levels, 3 * levels, levels)
    blocks = rows // TILE + 2
    end = TOP + rows
    north_step, south_step = lane_steps(TILE)
    for level in range(levels):
        padded[level, pl.ds(TOP - 6, 6), :] = halo[0, pl.ds(at_kappa + 6 * level, 6), :]
        padded[level, pl.ds(end, 6), :] = halo[1, pl.ds(at_kappa + 6 * level, 6), :]
        for field in range(fields):
            plane = field * levels + level
            if field < 3:
                present[field, level, pl.ds(TOP - 3, 3), :] = halo[0, pl.ds(at_own + 3 * plane, 3), :]
                present[field, level, pl.ds(end, 3), :] = halo[1, pl.ds(at_own + 3 * plane, 3), :]
            added[field, level, pl.ds(TOP - 3, 3), :] = halo[0, pl.ds(at_added + 3 * plane, 3), :]
            added[field, level, pl.ds(end, 3), :] = halo[1, pl.ds(at_added + 3 * plane, 3), :]
    for copy in copies[:2]:
        copy.wait()

    def each(level, total):
        for block in range(blocks):
            row = TILE + TILE * block
            spot = pl.ds(TILE * block, TILE)
            centre = padded[level, pl.ds(row, TILE), :]
            half = 0.5 * TIME_STEP
            coef[level, 0, spot, :] = half * (centre + padded[level, pl.ds(row + 1, TILE), :])
            coef[level, 1, spot, :] = half * (centre + padded[level, pl.ds(row - 1, TILE), :])
            coef[level, 2, spot, :] = (0.5 * north_step) * (centre + pltpu.roll(centre, 127, 1))
            coef[level, 3, spot, :] = (0.5 * south_step) * (centre + pltpu.roll(centre, 1, 1))
        now, later = present.at[:, level], following
        for step in range(STEPS):
            last = step == STEPS - 1
            advance(level, now, later, coef, (2,) if last else (0, 1, 2), range(1, blocks - 1) if last else range(blocks))
            total = total + observe(later, weight, rows)
            now, later = later, now
        return total

    action[...] = lax.fori_loop(0, levels, each, jnp.zeros((TILE, 128), jnp.float32))
    copies[2].wait()


def clone_kernel(general, scale, ancestor, own, sister, got_edges, got_odd, late_a, late_b, coef, weight, action, added,
                 *refs):
    parts = len(CUTS) - 1
    got_inner, odd_inner, refs = refs[:parts], refs[parts : 2 * parts], refs[2 * parts :]
    final, sums, late, present, following, chosen_sems, out_sems = refs
    fields, levels, rows = own.shape[1:4]
    rel = relation(general, ancestor[0])
    end = TOP + rows
    strip = pl.ds(TOP, rows)

    def whole(source):
        for level in range(levels):
            pltpu.make_async_copy(source.at[0, :, level], present.at[:, level, strip, :], chosen_sems.at[level]).start()

    def joined(edges, inner):
        for level in range(levels):
            pieces = [
                (part.at[:, level], present.at[pl.ds(start, stop - start), level, pl.ds(TOP + TILE, rows - 2 * TILE), :])
                for start, stop, part in zip(CUTS, CUTS[1:], inner)
            ]
            for source, target in [
                (edges.at[:, level, pl.ds(0, TILE), :], present.at[:, level, pl.ds(TOP, TILE), :]),
                (edges.at[:, level, pl.ds(TILE, TILE), :], present.at[:, level, pl.ds(end - TILE, TILE), :]),
                *pieces,
            ]:
                pltpu.make_async_copy(source, target, chosen_sems.at[level]).start()

    @pl.when(rel == 0)
    def _():
        whole(own)

    @pl.when(rel == 1)
    def _():
        whole(sister)

    @pl.when(rel == 2)
    def _():
        joined(got_edges, got_inner)

    @pl.when(rel > 2)
    def _():
        joined(got_odd, odd_inner)

    pair_get(late, late_a, late_b, even_strip())
    for field in range(fields):
        for level in range(levels):
            plane = field * levels + level
            present[field, level, pl.ds(TOP - 6, 6), :] = late[0, pl.ds(6 * plane, 6), :]
            present[field, level, pl.ds(end, 6), :] = late[1, pl.ds(6 * plane, 6), :]
    blocks = rows // TILE + 2

    def each(level, total):
        pltpu.make_async_copy(own.at[0, :, level], present.at[:, level, strip, :], chosen_sems.at[level]).wait()
        now, later = present.at[:, level], following
        for step in range(2 * STEPS):
            last = step == 2 * STEPS - 1
            advance(level, now, later, coef, range(fields), range(1, blocks - 1) if last else range(blocks))
            if step == STEPS - 1:
                for field in range(fields):
                    for block in range(blocks):
                        spot = pl.ds(TILE + TILE * block, TILE)
                        later[field, spot, :] = later[field, spot, :] + added[field, level, spot, :]
            if step >= STEPS:
                total = total + observe(later, weight, rows)
            now, later = later, now
        pltpu.make_async_copy(now.at[:, strip, :], final.at[0, :, level], out_sems.at[level]).start()
        return total

    total = lax.fori_loop(0, levels, each, jnp.zeros((TILE, 128), jnp.float32))
    first = jnp.sum(action[...]) * scale
    second = jnp.sum(total) * scale
    lane = lax.broadcasted_iota(jnp.int32, (1, 128), 1)
    sums[...] = jnp.where(lane == 0, first, jnp.where(lane == 1, second, 0.0))
    for level in range(levels):
        pltpu.make_async_copy(present.at[:, level, strip, :], final.at[0, :, level], out_sems.at[level]).wait()


def body(initial_state, ancestor, selector, perturbations, diffusivity, region_weight):
    _, fields, levels, rows, lat = initial_state.shape
    members, strips = lax.axis_size("mem"), lax.axis_size("lon")
    planes = fields * levels
    general = members != 4
    scale = 1.0 / (levels * lat * rows * strips)
    dma = pltpu.SemaphoreType.DMA
    edge_shape = f32(fields, levels, 2 * TILE, lat)

    def across(value, axis, bit):
        return lax.ppermute(value, axis, [(i, i ^ bit) for i in range(lax.axis_size(axis))])

    def after(values, others):
        return lax.optimization_barrier((values, others))[0]

    def round_strips(a, b):
        pairs_a = [(i, i ^ 1) for i in range(strips)]
        pairs_b = [(i, (i + 1 if i % 2 else i - 1) % strips) for i in range(strips)]
        return lax.ppermute(a, "lon", pairs_a), lax.ppermute(b, "lon", pairs_b)

    own = pltpu.with_memory_space_constraint(initial_state, pltpu.HBM)
    perturbations = pltpu.with_memory_space_constraint(perturbations, pltpu.HBM)
    kappa = pltpu.with_memory_space_constraint(diffusivity, pltpu.HBM)
    sister = initial_state if general else across(initial_state, "mem", 1)

    early_total = early_rows(planes, 3 * levels, levels)[-1]
    parts = [f32(stop - start, levels, rows - 2 * TILE, lat) for start, stop in zip(CUTS, CUTS[1:])]
    edges, early_a, early_b = call(
        start_kernel,
        [edge_shape, f32(early_total, lat), f32(early_total, lat)],
        [SMEM, HBM, HBM, HBM],
        [VMEM] * 3,
        [pltpu.VMEM(edge_shape.shape, jnp.float32), pltpu.VMEM((levels, 2 * TILE, lat), jnp.float32), dma((6,))],
        "start",
    )(selector, own, perturbations, kappa)
    if general:
        gathered = lax.all_gather(initial_state, "mem", axis=0, tiled=True)
        picked = jnp.take(gathered, ancestor, axis=0)[0]
        got_edges = got_odd = jnp.concatenate([picked[:, :, :TILE], picked[:, :, rows - TILE :]], axis=2)
        got_inner = odd_inner = [picked[low:high, :, TILE : rows - TILE] for low, high in zip(CUTS, CUTS[1:])]
    else:
        got_edges = across(edges, "mem", 2)
        got_odd = across(got_edges, "mem", 1)
        inner = call(
            inner_kernel, parts, [HBM], [ANY] * len(parts), [dma((len(parts),))], "inner"
        )(after(own, (sister, edges)))
        got_inner = [across(part, "mem", 2) for part in inner]

    early = round_strips(early_a, early_b)
    late = call(
        functools.partial(late_kernel, general),
        (f32(6 * planes, lat), f32(6 * planes, lat)),
        [SMEM, ANY, ANY, ANY, ANY],
        (VMEM, VMEM),
        [pltpu.VMEM(edge_shape.shape, jnp.float32), dma((2,))],
        "late_halo",
    )(ancestor, edges, sister, got_edges, got_odd)
    late = round_strips(*late)

    padded = rows + 2 * TOP
    coef, action, added = call(
        prepare_kernel,
        (f32(levels, 4, rows + 2 * TILE, lat), f32(TILE, lat), f32(fields, levels, padded, lat)),
        [SMEM, HBM, HBM, VMEM, HBM, VMEM, VMEM],
        (VMEM, VMEM, VMEM),
        [
            pltpu.VMEM((2, early_total, lat), jnp.float32),
            pltpu.VMEM((3, levels, padded, lat), jnp.float32),
            pltpu.VMEM((3, padded, lat), jnp.float32),
            pltpu.VMEM((levels, padded, lat), jnp.float32),
            dma((3,)),
        ],
        "prepare",
    )(selector, own, kappa, region_weight, perturbations, *early)
    if not general:
        ready = after(got_inner, (late, action))
        odd_inner = [across(part, "mem", 1) for part in ready]
    final_state, sums = call(
        functools.partial(clone_kernel, general, scale),
        (f32(1, fields, levels, rows, lat), f32(1, lat)),
        [SMEM, HBM, ANY, ANY, ANY] + [VMEM] * 6 + [ANY] * (2 * len(parts)),
        (HBM, VMEM),
        [
            pltpu.VMEM((2, 6 * planes, lat), jnp.float32),
            pltpu.VMEM((fields, levels, padded, lat), jnp.float32),
            pltpu.VMEM((fields, padded, lat), jnp.float32),
            dma((levels,)),
            dma((levels,)),
        ],
        "clone_window",
    )(ancestor, own, sister, got_edges, got_odd, *late, coef, region_weight, action, added, *got_inner, *odd_inner)
    everyone = jnp.broadcast_to(sums, (strips, lat))
    sums = jnp.sum(lax.all_to_all(everyone, "lon", 0, 0), axis=0, keepdims=True)
    return final_state, sums[:, :2]


def solution(mesh):
    in_specs = (
        P(("ens", "mem"), None, None, "lon", None),
        P(("ens", "mem")),
        P(("ens", "mem")),
        P("ens", None, None, "lon", None),
        P(None, "lon", None),
        P("lon", None),
    )
    out_specs = (P(("ens", "mem"), None, None, "lon", None), P(("ens", "mem"), None))
    return jax.shard_map(body, mesh=mesh, in_specs=in_specs, out_specs=out_specs, check_vma=False)
```

```python
import functools
import jax
import jax.numpy as jnp
from jax import lax
from jax.experimental import pallas as pl
from jax.experimental.pallas import tpu as pltpu
from jax.sharding import PartitionSpec as P

STEPS = 3
TIME_STEP = 0.2
TILE = 8
TOP = 2 * TILE
CUTS = (0, 2, 4)
VMEM_LIMIT = 48 * 1024 * 1024

ANY = pl.BlockSpec(memory_space=pl.ANY)
HBM = pl.BlockSpec(memory_space=pltpu.HBM)
VMEM = pl.BlockSpec(memory_space=pltpu.VMEM)
SMEM = pl.BlockSpec(memory_space=pltpu.SMEM)


def call(kernel, out_shape, in_specs, out_specs, scratch_shapes, name, flops=0):
    return pl.pallas_call(
        kernel,
        out_shape=out_shape,
        in_specs=in_specs,
        out_specs=out_specs,
        scratch_shapes=scratch_shapes,
        name=name,
        compiler_params=pltpu.CompilerParams(vmem_limit_bytes=VMEM_LIMIT),
        cost_estimate=pl.CostEstimate(flops=flops, bytes_accessed=1 << 20, transcendentals=0),
    )


def f32(*shape):
    return jax.ShapeDtypeStruct(shape, jnp.float32)


def lane_steps(rows):
    lane = lax.broadcasted_iota(jnp.int32, (rows, 128), 1)
    north = jnp.where(lane == 127, 0.0, TIME_STEP).astype(jnp.float32)
    south = jnp.where(lane == 0, 0.0, TIME_STEP).astype(jnp.float32)
    return north, south


def advance(source, target, coef, fields, blocks):
    north_step, south_step = lane_steps(TILE)
    for level in range(source.shape[1]):
        for block in blocks:
            row = TILE + TILE * block
            here = pl.ds(row, TILE)
            zonal = source[0, level, here, :]
            merid = source[1, level, here, :]
            spot = pl.ds(TILE * block, TILE)
            east = coef[level, 0, spot, :] - TIME_STEP * jnp.minimum(zonal, 0.0)
            west = coef[level, 1, spot, :] + TIME_STEP * jnp.maximum(zonal, 0.0)
            north = coef[level, 2, spot, :] - north_step * jnp.minimum(merid, 0.0)
            south = coef[level, 3, spot, :] + south_step * jnp.maximum(merid, 0.0)
            keep = 1.0 - ((east + west) + (north + south))
            for field in fields:
                centre = source[field, level, here, :]
                target[field, level, here, :] = (
                    keep * centre
                    + east * source[field, level, pl.ds(row + 1, TILE), :]
                    + west * source[field, level, pl.ds(row - 1, TILE), :]
                    + north * pltpu.roll(centre, 127, 1)
                    + south * pltpu.roll(centre, 1, 1)
                )


def observe(values, weight):
    total = jnp.zeros((TILE, 128), jnp.float32)
    for block in range(weight.shape[0] // TILE):
        square = jnp.zeros((TILE, 128), jnp.float32)
        for level in range(values.shape[1]):
            spot = values[2, level, pl.ds(TOP + TILE * block, TILE), :]
            square = square + spot * spot
        total = total + weight[pl.ds(TILE * block, TILE), :] * square
    return total


def early_rows(planes, own_planes, levels):
    own = 0
    added = own + 3 * own_planes
    kappa = added + 3 * planes
    total = kappa + 6 * levels
    return own, added, kappa, -(-total // TILE) * TILE


def field_parts():
    return [pl.ds(start, stop - start) for start, stop in zip(CUTS, CUTS[1:])]


def start_all(copies):
    for copy in copies:
        copy.start()
    return copies


def wait_all(copies):
    for copy in copies:
        copy.wait()


def edge_copies(source, target, sems, first):
    rows = source.shape[-2]
    lead = (slice(None),) * (len(source.shape) - 2)
    return [
        pltpu.make_async_copy(
            source.at[(*lead, pl.ds(0, TILE))], target.at[(*lead, pl.ds(0, TILE))], sems.at[first]
        ),
        pltpu.make_async_copy(
            source.at[(*lead, pl.ds(rows - TILE, TILE))], target.at[(*lead, pl.ds(TILE, TILE))], sems.at[first + 1]
        ),
    ]


def pair_put(out_a, out_b, even, offset, low_rows, high_rows):
    spot = pl.ds(offset, low_rows.shape[0])
    out_a[spot, :] = jnp.where(even, high_rows, low_rows)
    out_b[spot, :] = jnp.where(even, low_rows, high_rows)


def pair_get(halo, got_a, got_b, even):
    a, b = got_a[...], got_b[...]
    halo[0] = jnp.where(even, b, a)
    halo[1] = jnp.where(even, a, b)


def even_strip():
    return lax.rem(lax.axis_index("lon"), 2) == 0


def edge_kernel(own, edges, sems):
    wait_all(start_all(edge_copies(own.at[0], edges, sems, 0)))


def early_kernel(general, ancestor, selector, own, edges, perturbations, kappa, *refs):
    *inner, out_a, out_b, chosen, added, ends, sems = refs
    fields, levels, rows = own.shape[1:4]
    which = jnp.clip(selector[0], 0, perturbations.shape[0] - 1)
    chosen[0] = 2 if general else lax.axis_index("mem") ^ ancestor[0]
    chosen[1] = which
    first = start_all(
        edge_copies(perturbations.at[which], added, sems, 0) + edge_copies(kappa, ends, sems, 2)
    )
    later = start_all([
        pltpu.make_async_copy(own.at[0, part, :, pl.ds(TILE, rows - 2 * TILE), :], target, sems.at[4 + i])
        for i, (part, target) in enumerate(zip(field_parts(), inner))
    ])
    wait_all(first)
    even = even_strip()
    put = functools.partial(pair_put, out_a, out_b, even)
    at_own, at_added, at_kappa, _ = early_rows(fields * levels, 3 * levels, levels)
    for field in range(fields):
        for level in range(levels):
            plane = field * levels + level
            if field < 3:
                put(at_own + 3 * plane, edges[field, level, 0:3, :], edges[field, level, 13:16, :])
            put(at_added + 3 * plane, added[field, level, 0:3, :], added[field, level, 13:16, :])
    for level in range(levels):
        put(at_kappa + 6 * level, ends[level, 0:6, :], ends[level, 10:16, :])
    wait_all(later)


def pick(rel, choices):
    for number, choice in enumerate(choices):
        pl.when(rel == number if number < 3 else rel > 2)(choice)


def late_kernel(chosen, edges, sister, got_edges, got_odd, out_a, out_b, taken, sems):
    fields, levels = edges.shape[:2]

    def whole(source):
        return lambda: wait_all(start_all([pltpu.make_async_copy(source, taken, sems.at[0])]))

    pick(chosen[0], [
        whole(edges),
        lambda: wait_all(start_all(edge_copies(sister.at[0], taken, sems, 0))),
        whole(got_edges),
        whole(got_odd),
    ])
    even = even_strip()
    for field in range(fields):
        for level in range(levels):
            at = 6 * (field * levels + level)
            pair_put(out_a, out_b, even, at, taken[field, level, 0:6, :], taken[field, level, 10:16, :])


def prepare_kernel(chosen, own, kappa, weight, perturbations, got_a, got_b, coef, action, added,
                   halo, present, following, padded, sems):
    fields, levels, rows = own.shape[1:4]
    strip = pl.ds(TOP, rows)
    copies = start_all([
        pltpu.make_async_copy(kappa, padded.at[:, strip, :], sems.at[0]),
        pltpu.make_async_copy(own.at[0, pl.ds(0, 3)], present.at[:, :, strip, :], sems.at[1]),
        pltpu.make_async_copy(perturbations.at[chosen[1]], added.at[:, :, strip, :], sems.at[2]),
    ])
    pair_get(halo, got_a, got_b, even_strip())
    at_own, at_added, at_kappa, _ = early_rows(fields * levels, 3 * levels, levels)
    end = TOP + rows
    for level in range(levels):
        padded[level, pl.ds(TOP - 6, 6), :] = halo[0, pl.ds(at_kappa + 6 * level, 6), :]
        padded[level, pl.ds(end, 6), :] = halo[1, pl.ds(at_kappa + 6 * level, 6), :]
        for field in range(fields):
            plane = field * levels + level
            if field < 3:
                present[field, level, pl.ds(TOP - 3, 3), :] = halo[0, pl.ds(at_own + 3 * plane, 3), :]
                present[field, level, pl.ds(end, 3), :] = halo[1, pl.ds(at_own + 3 * plane, 3), :]
            added[field, level, pl.ds(TOP - 3, 3), :] = halo[0, pl.ds(at_added + 3 * plane, 3), :]
            added[field, level, pl.ds(end, 3), :] = halo[1, pl.ds(at_added + 3 * plane, 3), :]
    blocks = range(rows // TILE + 2)
    north_step, south_step = lane_steps(TILE)
    wait_all(copies[:1])
    for level in range(levels):
        for block in blocks:
            row = TILE + TILE * block
            spot = pl.ds(TILE * block, TILE)
            centre = padded[level, pl.ds(row, TILE), :]
            half = 0.5 * TIME_STEP
            coef[level, 0, spot, :] = half * (centre + padded[level, pl.ds(row + 1, TILE), :])
            coef[level, 1, spot, :] = half * (centre + padded[level, pl.ds(row - 1, TILE), :])
            coef[level, 2, spot, :] = (0.5 * north_step) * (centre + pltpu.roll(centre, 127, 1))
            coef[level, 3, spot, :] = (0.5 * south_step) * (centre + pltpu.roll(centre, 1, 1))
    wait_all(copies[1:2])
    advance(present, following, coef, (0, 1, 2), blocks)
    total = observe(following, weight)
    advance(following, present, coef, (0, 1, 2), blocks)
    total = total + observe(present, weight)
    advance(present, following, coef, (2,), blocks[1:-1])
    action[...] = total + observe(following, weight)
    wait_all(copies[2:])


def clone_kernel(scale, chosen, own, sister, got_edges, got_odd, got_a, got_b, coef, weight, action, added, *refs):
    parts = len(CUTS) - 1
    got_inner, odd_inner, refs = refs[:parts], refs[parts : 2 * parts], refs[2 * parts :]
    final, sums, halo, present, following, sems, out_sems = refs
    fields, levels, rows = own.shape[1:4]
    end = TOP + rows
    strip = pl.ds(TOP, rows)
    taken = present.at[:, :, strip, :]
    low, high = pl.ds(0, TILE), pl.ds(TILE, TILE)

    def whole(source):
        return lambda: wait_all(start_all([pltpu.make_async_copy(source.at[0], taken, sems.at[0])]))

    def joined(edges, inner):
        return lambda: wait_all(start_all([
            pltpu.make_async_copy(edges.at[:, :, low, :], taken.at[:, :, low, :], sems.at[0]),
            pltpu.make_async_copy(edges.at[:, :, high, :], taken.at[:, :, pl.ds(rows - TILE, TILE), :], sems.at[1]),
            *[
                pltpu.make_async_copy(source, taken.at[part, :, pl.ds(TILE, rows - 2 * TILE), :], sems.at[2 + i])
                for i, (part, source) in enumerate(zip(field_parts(), inner))
            ],
        ]))

    pick(chosen[0], [whole(own), whole(sister), joined(got_edges, got_inner), joined(got_odd, odd_inner)])
    pair_get(halo, got_a, got_b, even_strip())
    for field in range(fields):
        for level in range(levels):
            plane = field * levels + level
            present[field, level, pl.ds(TOP - 6, 6), :] = halo[0, pl.ds(6 * plane, 6), :]
            present[field, level, pl.ds(end, 6), :] = halo[1, pl.ds(6 * plane, 6), :]
    blocks = range(rows // TILE + 2)
    every = range(fields)

    def two_steps(pair, total):
        advance(present, following, coef, every, blocks)

        @pl.when(pair == 1)
        def _():
            for field in every:
                for level in range(levels):
                    for block in blocks:
                        spot = pl.ds(TILE + TILE * block, TILE)
                        following[field, level, spot, :] += added[field, level, spot, :]

        advance(following, present, coef, every, blocks)
        return total + jnp.where(pair == 1, 1.0, 0.0) * observe(present, weight)

    total = lax.fori_loop(0, 2, two_steps, jnp.zeros((TILE, 128), jnp.float32))
    advance(present, following, coef, every, blocks)
    total = total + observe(following, weight)
    half = levels // 2
    outs = []
    for low, high in ((0, half), (half, levels)):
        part = pl.ds(low, high - low)
        advance(following.at[:, part], present.at[:, part], coef.at[part], every, blocks[1:-1])
        outs += start_all([
            pltpu.make_async_copy(present.at[:, part, strip, :], final.at[0, :, part], out_sems.at[len(outs)])
        ])
    total = total + observe(present, weight)
    first = jnp.sum(action[...]) * scale
    second = jnp.sum(total) * scale
    lane = lax.broadcasted_iota(jnp.int32, (1, 128), 1)
    sums[...] = jnp.where(lane == 0, first, jnp.where(lane == 1, second, 0.0))
    wait_all(outs)


def body(initial_state, ancestor, selector, perturbations, diffusivity, region_weight):
    _, fields, levels, rows, lat = initial_state.shape
    members, strips = lax.axis_size("mem"), lax.axis_size("lon")
    planes = fields * levels
    general = members != 4
    scale = 1.0 / (levels * lat * rows * strips)
    dma = pltpu.SemaphoreType.DMA

    def scratch(*shape):
        return pltpu.VMEM(shape, jnp.float32)

    def across(value, axis, bit):
        return lax.ppermute(value, axis, [(i, i ^ bit) for i in range(lax.axis_size(axis))])

    def after(values, others):
        return lax.optimization_barrier((values, others))[0]

    def round_strips(a, b):
        pairs_a = [(i, i ^ 1) for i in range(strips)]
        pairs_b = [(i, (i + 1 if i % 2 else i - 1) % strips) for i in range(strips)]
        return lax.ppermute(a, "lon", pairs_a), lax.ppermute(b, "lon", pairs_b)

    own = pltpu.with_memory_space_constraint(initial_state, pltpu.HBM)
    perturbations = pltpu.with_memory_space_constraint(perturbations, pltpu.HBM)
    kappa = pltpu.with_memory_space_constraint(diffusivity, pltpu.HBM)
    sister = initial_state if general else across(initial_state, "mem", 1)

    early_total = early_rows(planes, 3 * levels, levels)[-1]
    edges = call(edge_kernel, f32(fields, levels, 2 * TILE, lat), [HBM], ANY, [dma((2,))], "edges")(own)
    parts = [f32(part.size, levels, rows - 2 * TILE, lat) for part in field_parts()]
    *inner, early_a, early_b, chosen = call(
        functools.partial(early_kernel, general),
        (
            *parts,
            f32(early_total, lat),
            f32(early_total, lat),
            jax.ShapeDtypeStruct((2,), jnp.int32),
        ),
        [SMEM, SMEM, HBM, VMEM, HBM, HBM],
        (*[ANY] * len(parts), VMEM, VMEM, SMEM),
        [
            scratch(fields, levels, 2 * TILE, lat),
            scratch(levels, 2 * TILE, lat),
            dma((4 + len(parts),)),
        ],
        "early_halo",
    )(ancestor, selector, own, after(edges, sister), perturbations, kappa)
    if general:
        picked = jnp.take(lax.all_gather(initial_state, "mem", axis=0, tiled=True), ancestor, axis=0)[0]
        got_edges = got_odd = jnp.concatenate([picked[:, :, :TILE], picked[:, :, rows - TILE :]], axis=2)
        got_inner = odd_inner = [picked[low:high, :, TILE : rows - TILE] for low, high in zip(CUTS, CUTS[1:])]
    else:
        got_edges = across(edges, "mem", 2)
        got_odd = across(got_edges, "mem", 1)
        got_inner = [across(part, "mem", 2) for part in inner]

    early = round_strips(early_a, early_b)
    late = call(
        late_kernel,
        (f32(6 * planes, lat), f32(6 * planes, lat)),
        [SMEM, ANY, ANY, ANY, ANY],
        (VMEM, VMEM),
        [scratch(fields, levels, 2 * TILE, lat), dma((2,))],
        "late_halo",
    )(chosen, edges, sister, got_edges, got_odd)
    packed = late
    late = round_strips(*late)

    padded = rows + 2 * TOP
    coef, action, added = call(
        prepare_kernel,
        (f32(levels, 4, rows + 2 * TILE, lat), f32(TILE, lat), f32(fields, levels, padded, lat)),
        [SMEM, HBM, HBM, VMEM, HBM, VMEM, VMEM],
        (VMEM, VMEM, VMEM),
        [
            scratch(2, early_total, lat),
            scratch(3, levels, padded, lat),
            scratch(3, levels, padded, lat),
            scratch(levels, padded, lat),
            dma((3,)),
        ],
        "prepare",
    )(chosen, own, kappa, region_weight, perturbations, *early)
    if not general:
        odd_inner = [across(part, "mem", 1) for part in after(got_inner, (late, action))]
    final_state, sums = call(
        functools.partial(clone_kernel, scale),
        (f32(1, fields, levels, rows, lat), f32(1, lat)),
        [SMEM, HBM, ANY, ANY, ANY] + [VMEM] * 6 + [ANY] * (2 * len(parts)),
        (HBM, VMEM),
        [
            scratch(2, 6 * planes, lat),
            scratch(fields, levels, padded, lat),
            scratch(fields, levels, padded, lat),
            dma((2 + len(parts),)),
            dma((2,)),
        ],
        "clone_window",
    )(chosen, own, sister, got_edges, got_odd, *late, coef, region_weight, action, added, *got_inner, *odd_inner)
    if strips == 4:
        one, two, three = [across(sums, "lon", bit) for bit in (1, 2, 3)]
        sums = (sums + one) + (two + three)
    else:
        bit = 1
        while bit < strips:
            sums = sums + across(sums, "lon", bit)
            bit *= 2
    return final_state, sums[:, :2]


def solution(mesh):
    in_specs = (
        P(("ens", "mem"), None, None, "lon", None),
        P(("ens", "mem")),
        P(("ens", "mem")),
        P("ens", None, None, "lon", None),
        P(None, "lon", None),
        P("lon", None),
    )
    out_specs = (P(("ens", "mem"), None, None, "lon", None), P(("ens", "mem"), None))
    return jax.shard_map(body, mesh=mesh, in_specs=in_specs, out_specs=out_specs, check_vma=False)
```

```python
import functools
import jax
import jax.numpy as jnp
from jax import lax
from jax.experimental import pallas as pl
from jax.experimental.pallas import tpu as pltpu
from jax.sharding import PartitionSpec as P

STEPS = 3
TIME_STEP = 0.2
TILE = 8
TOP = 2 * TILE
CUTS = (0, 2, 4)
VMEM_LIMIT = 48 * 1024 * 1024

ANY = pl.BlockSpec(memory_space=pl.ANY)
HBM = pl.BlockSpec(memory_space=pltpu.HBM)
VMEM = pl.BlockSpec(memory_space=pltpu.VMEM)
SMEM = pl.BlockSpec(memory_space=pltpu.SMEM)


def call(kernel, out_shape, in_specs, out_specs, scratch_shapes, name, flops=0):
    return pl.pallas_call(
        kernel,
        out_shape=out_shape,
        in_specs=in_specs,
        out_specs=out_specs,
        scratch_shapes=scratch_shapes,
        name=name,
        compiler_params=pltpu.CompilerParams(vmem_limit_bytes=VMEM_LIMIT),
        cost_estimate=pl.CostEstimate(flops=flops, bytes_accessed=1 << 20, transcendentals=0),
    )


def f32(*shape):
    return jax.ShapeDtypeStruct(shape, jnp.float32)


def lane_steps(rows):
    lane = lax.broadcasted_iota(jnp.int32, (rows, 128), 1)
    north = jnp.where(lane == 127, 0.0, TIME_STEP).astype(jnp.float32)
    south = jnp.where(lane == 0, 0.0, TIME_STEP).astype(jnp.float32)
    return north, south


def advance(source, target, coef, fields, blocks):
    north_step, south_step = lane_steps(TILE)
    for level in range(source.shape[1]):
        for block in blocks:
            row = TILE + TILE * block
            here = pl.ds(row, TILE)
            zonal = source[0, level, here, :]
            merid = source[1, level, here, :]
            spot = pl.ds(TILE * block, TILE)
            east = coef[level, 0, spot, :] - TIME_STEP * jnp.minimum(zonal, 0.0)
            west = coef[level, 1, spot, :] + TIME_STEP * jnp.maximum(zonal, 0.0)
            north = coef[level, 2, spot, :] - north_step * jnp.minimum(merid, 0.0)
            south = coef[level, 3, spot, :] + south_step * jnp.maximum(merid, 0.0)
            keep = 1.0 - ((east + west) + (north + south))
            for field in fields:
                centre = source[field, level, here, :]
                target[field, level, here, :] = (
                    keep * centre
                    + east * source[field, level, pl.ds(row + 1, TILE), :]
                    + west * source[field, level, pl.ds(row - 1, TILE), :]
                    + north * pltpu.roll(centre, 127, 1)
                    + south * pltpu.roll(centre, 1, 1)
                )


def observe(values, weight):
    total = jnp.zeros((TILE, 128), jnp.float32)
    for block in range(weight.shape[0] // TILE):
        square = jnp.zeros((TILE, 128), jnp.float32)
        for level in range(values.shape[1]):
            spot = values[2, level, pl.ds(TOP + TILE * block, TILE), :]
            square = square + spot * spot
        total = total + weight[pl.ds(TILE * block, TILE), :] * square
    return total


def early_rows(planes, own_planes, levels):
    own = 0
    added = own + 3 * own_planes
    kappa = added + 3 * planes
    total = kappa + 6 * levels
    return own, added, kappa, -(-total // TILE) * TILE


def field_parts():
    return [pl.ds(start, stop - start) for start, stop in zip(CUTS, CUTS[1:])]


def start_all(copies):
    for copy in copies:
        copy.start()
    return copies


def wait_all(copies):
    for copy in copies:
        copy.wait()


def edge_copies(source, target, sems, first):
    rows = source.shape[-2]
    lead = (slice(None),) * (len(source.shape) - 2)
    return [
        pltpu.make_async_copy(
            source.at[(*lead, pl.ds(0, TILE))], target.at[(*lead, pl.ds(0, TILE))], sems.at[first]
        ),
        pltpu.make_async_copy(
            source.at[(*lead, pl.ds(rows - TILE, TILE))], target.at[(*lead, pl.ds(TILE, TILE))], sems.at[first + 1]
        ),
    ]


def pair_put(out_a, out_b, even, offset, low_rows, high_rows):
    spot = pl.ds(offset, low_rows.shape[0])
    out_a[spot, :] = jnp.where(even, high_rows, low_rows)
    out_b[spot, :] = jnp.where(even, low_rows, high_rows)


def pair_get(halo, got_a, got_b, even):
    a, b = got_a[...], got_b[...]
    halo[0] = jnp.where(even, b, a)
    halo[1] = jnp.where(even, a, b)


def even_strip():
    return lax.rem(lax.axis_index("lon"), 2) == 0


def edge_kernel(own, edges, *refs):
    *inner, sems = refs
    rows = own.shape[3]
    wait_all(start_all(edge_copies(own.at[0], edges, sems, 0) + [
        pltpu.make_async_copy(own.at[0, part, :, pl.ds(TILE, rows - 2 * TILE), :], target, sems.at[2 + i])
        for i, (part, target) in enumerate(zip(field_parts(), inner))
    ]))


def early_kernel(general, ancestor, selector, edges, perturbations, kappa, out_a, out_b, chosen, added, spread, sems):
    fields, levels = edges.shape[:2]
    rows = kappa.shape[1]
    which = jnp.clip(selector[0], 0, perturbations.shape[0] - 1)
    chosen[0] = 2 if general else lax.axis_index("mem") ^ ancestor[0]
    chosen[1] = which
    strip = pl.ds(TOP, rows)
    wait_all(start_all([
        pltpu.make_async_copy(perturbations.at[which], added.at[:, :, strip, :], sems.at[0]),
        pltpu.make_async_copy(kappa, spread.at[:, strip, :], sems.at[1]),
    ]))
    even = even_strip()
    put = functools.partial(pair_put, out_a, out_b, even)
    at_own, at_added, at_kappa, _ = early_rows(fields * levels, 3 * levels, levels)
    end = TOP + rows
    for field in range(fields):
        for level in range(levels):
            plane = field * levels + level
            if field < 3:
                put(at_own + 3 * plane, edges[field, level, 0:3, :], edges[field, level, 13:16, :])
            put(at_added + 3 * plane, added[field, level, TOP : TOP + 3, :], added[field, level, end - 3 : end, :])
    for level in range(levels):
        put(at_kappa + 6 * level, spread[level, TOP : TOP + 6, :], spread[level, end - 6 : end, :])


def pick(rel, choices):
    for number, choice in enumerate(choices):
        pl.when(rel == number if number < 3 else rel > 2)(choice)


def late_kernel(chosen, edges, sister, got_edges, got_odd, out_a, out_b):
    fields, levels = edges.shape[:2]
    even = even_strip()

    def packed(source):
        rows = source.shape[2]

        def put():
            for field in range(fields):
                for level in range(levels):
                    low, high = source[field, level, 0:6, :], source[field, level, rows - 6 : rows, :]
                    pair_put(out_a, out_b, even, 6 * (field * levels + level), low, high)

        return put

    pick(chosen[0], [packed(edges), packed(sister.at[0]), packed(got_edges), packed(got_odd)])


def lay(target, fields, edges, inner):
    rows = inner[0].shape[2] + 2 * TILE
    for field in range(fields):
        number = max(i for i, start in enumerate(CUTS[:-1]) if start <= field)
        for level in range(target.shape[1]):
            target[field, level, pl.ds(TOP, TILE), :] = edges[field, level, 0:TILE, :]
            target[field, level, pl.ds(TOP + TILE, rows - 2 * TILE), :] = inner[number][field - CUTS[number], level]
            target[field, level, pl.ds(TOP + rows - TILE, TILE), :] = edges[field, level, TILE : 2 * TILE, :]


def prepare_kernel(edges, weight, got_a, got_b, spread, added_in, *refs):
    parts = len(CUTS) - 1
    inner, (coef, action, added, halo, present, following, padded) = refs[:parts], refs[parts:]
    fields, levels = edges.shape[:2]
    rows = weight.shape[0]
    lay(present, 3, edges, inner)
    pair_get(halo, got_a, got_b, even_strip())
    at_own, at_added, at_kappa, _ = early_rows(fields * levels, 3 * levels, levels)
    end = TOP + rows
    strip = pl.ds(TOP, rows)
    for level in range(levels):
        padded[level, strip, :] = spread[level, strip, :]
        padded[level, pl.ds(TOP - 6, 6), :] = halo[0, pl.ds(at_kappa + 6 * level, 6), :]
        padded[level, pl.ds(end, 6), :] = halo[1, pl.ds(at_kappa + 6 * level, 6), :]
        for field in range(fields):
            plane = field * levels + level
            if field < 3:
                present[field, level, pl.ds(TOP - 3, 3), :] = halo[0, pl.ds(at_own + 3 * plane, 3), :]
                present[field, level, pl.ds(end, 3), :] = halo[1, pl.ds(at_own + 3 * plane, 3), :]
            added[field, level, strip, :] = added_in[field, level, strip, :]
            added[field, level, pl.ds(TOP - 3, 3), :] = halo[0, pl.ds(at_added + 3 * plane, 3), :]
            added[field, level, pl.ds(end, 3), :] = halo[1, pl.ds(at_added + 3 * plane, 3), :]
    blocks = range(rows // TILE + 2)
    north_step, south_step = lane_steps(TILE)
    for level in range(levels):
        for block in blocks:
            row = TILE + TILE * block
            spot = pl.ds(TILE * block, TILE)
            centre = padded[level, pl.ds(row, TILE), :]
            half = 0.5 * TIME_STEP
            coef[level, 0, spot, :] = half * (centre + padded[level, pl.ds(row + 1, TILE), :])
            coef[level, 1, spot, :] = half * (centre + padded[level, pl.ds(row - 1, TILE), :])
            coef[level, 2, spot, :] = (0.5 * north_step) * (centre + pltpu.roll(centre, 127, 1))
            coef[level, 3, spot, :] = (0.5 * south_step) * (centre + pltpu.roll(centre, 1, 1))
    advance(present, following, coef, (0, 1, 2), blocks)
    total = observe(following, weight)
    advance(following, present, coef, (0, 1, 2), blocks)
    total = total + observe(present, weight)
    advance(present, following, coef, (2,), blocks[1:-1])
    action[...] = total + observe(following, weight)


def clone_kernel(scale, chosen, edges, sister, got_edges, got_odd, got_a, got_b, coef, weight, action, added, *refs):
    parts = len(CUTS) - 1
    inner, got_inner, odd_inner = [refs[i * parts : (i + 1) * parts] for i in range(3)]
    final, sums, halo, present, following, out_sems = refs[3 * parts :]
    fields, levels = edges.shape[:2]
    rows = weight.shape[0]
    end = TOP + rows
    strip = pl.ds(TOP, rows)

    def whole():
        for field in range(fields):
            for level in range(levels):
                present[field, level, strip, :] = sister[0, field, level]

    def joined(edges, inner):
        return lambda: lay(present, fields, edges, inner)

    pick(chosen[0], [joined(edges, inner), whole, joined(got_edges, got_inner), joined(got_odd, odd_inner)])
    pair_get(halo, got_a, got_b, even_strip())
    for field in range(fields):
        for level in range(levels):
            plane = field * levels + level
            present[field, level, pl.ds(TOP - 6, 6), :] = halo[0, pl.ds(6 * plane, 6), :]
            present[field, level, pl.ds(end, 6), :] = halo[1, pl.ds(6 * plane, 6), :]
    blocks = range(rows // TILE + 2)
    every = range(fields)

    def two_steps(pair, total):
        advance(present, following, coef, every, blocks)

        @pl.when(pair == 1)
        def _():
            for field in every:
                for level in range(levels):
                    for block in blocks:
                        spot = pl.ds(TILE + TILE * block, TILE)
                        following[field, level, spot, :] += added[field, level, spot, :]

        advance(following, present, coef, every, blocks)
        return total + jnp.where(pair == 1, 1.0, 0.0) * observe(present, weight)

    total = lax.fori_loop(0, 2, two_steps, jnp.zeros((TILE, 128), jnp.float32))
    advance(present, following, coef, every, blocks)
    total = total + observe(following, weight)
    half = levels // 2
    outs = []
    for low, high in ((0, half), (half, levels)):
        part = pl.ds(low, high - low)
        advance(following.at[:, part], present.at[:, part], coef.at[part], every, blocks[1:-1])
        outs += start_all([
            pltpu.make_async_copy(present.at[:, part, strip, :], final.at[0, :, part], out_sems.at[len(outs)])
        ])
    total = total + observe(present, weight)
    first = jnp.sum(action[...]) * scale
    second = jnp.sum(total) * scale
    lane = lax.broadcasted_iota(jnp.int32, (1, 128), 1)
    sums[...] = jnp.where(lane == 0, first, jnp.where(lane == 1, second, 0.0))
    wait_all(outs)


def body(initial_state, ancestor, selector, perturbations, diffusivity, region_weight):
    _, fields, levels, rows, lat = initial_state.shape
    members, strips = lax.axis_size("mem"), lax.axis_size("lon")
    planes = fields * levels
    general = members != 4
    scale = 1.0 / (levels * lat * rows * strips)
    dma = pltpu.SemaphoreType.DMA

    def scratch(*shape):
        return pltpu.VMEM(shape, jnp.float32)

    def across(value, axis, bit):
        return lax.ppermute(value, axis, [(i, i ^ bit) for i in range(lax.axis_size(axis))])

    def after(values, others):
        return lax.optimization_barrier((values, others))[0]

    def round_strips(a, b):
        pairs_a = [(i, i ^ 1) for i in range(strips)]
        pairs_b = [(i, (i + 1 if i % 2 else i - 1) % strips) for i in range(strips)]
        return lax.ppermute(a, "lon", pairs_a), lax.ppermute(b, "lon", pairs_b)

    own = pltpu.with_memory_space_constraint(initial_state, pltpu.HBM)
    perturbations = pltpu.with_memory_space_constraint(perturbations, pltpu.HBM)
    kappa = pltpu.with_memory_space_constraint(diffusivity, pltpu.HBM)
    sister = initial_state if general else across(initial_state, "mem", 1)

    early_total = early_rows(planes, 3 * levels, levels)[-1]
    parts = [f32(part.size, levels, rows - 2 * TILE, lat) for part in field_parts()]
    edges, *inner = call(
        edge_kernel,
        (f32(fields, levels, 2 * TILE, lat), *parts),
        [HBM],
        [ANY] * (1 + len(parts)),
        [dma((2 + len(parts),))],
        "edges",
    )(own)
    padded = rows + 2 * TOP
    early_a, early_b, chosen, added, spread = call(
        functools.partial(early_kernel, general),
        (
            f32(early_total, lat),
            f32(early_total, lat),
            jax.ShapeDtypeStruct((2,), jnp.int32),
            f32(fields, levels, padded, lat),
            f32(levels, padded, lat),
        ),
        [SMEM, SMEM, VMEM, HBM, HBM],
        (VMEM, VMEM, SMEM, VMEM, VMEM),
        [dma((2,))],
        "early_halo",
    )(ancestor, selector, after(edges, sister), perturbations, kappa)
    if general:
        picked = jnp.take(lax.all_gather(initial_state, "mem", axis=0, tiled=True), ancestor, axis=0)[0]
        got_edges = got_odd = jnp.concatenate([picked[:, :, :TILE], picked[:, :, rows - TILE :]], axis=2)
        got_inner = odd_inner = [picked[low:high, :, TILE : rows - TILE] for low, high in zip(CUTS, CUTS[1:])]
    else:
        got_edges = across(edges, "mem", 2)
        got_odd = across(got_edges, "mem", 1)
        got_inner = [across(part, "mem", 2) for part in inner]

    early = round_strips(early_a, early_b)
    late = call(
        late_kernel,
        (f32(6 * planes, lat), f32(6 * planes, lat)),
        [SMEM] + [VMEM] * 4,
        (VMEM, VMEM),
        [],
        "late_halo",
    )(chosen, edges, sister, got_edges, got_odd)
    packed = late
    late = round_strips(*late)

    coef, action, added = call(
        prepare_kernel,
        (f32(levels, 4, rows + 2 * TILE, lat), f32(TILE, lat), f32(fields, levels, padded, lat)),
        [VMEM] * (6 + len(parts)),
        (VMEM, VMEM, VMEM),
        [
            scratch(2, early_total, lat),
            scratch(3, levels, padded, lat),
            scratch(3, levels, padded, lat),
            scratch(levels, padded, lat),
        ],
        "prepare",
    )(edges, region_weight, *early, spread, added, *inner)
    if not general:
        odd_inner = [across(part, "mem", 1) for part in after(got_inner, (late, action))]
    final_state, sums = call(
        functools.partial(clone_kernel, scale),
        (f32(1, fields, levels, rows, lat), f32(1, lat)),
        [SMEM] + [VMEM] * (10 + 3 * len(parts)),
        (HBM, VMEM),
        [
            scratch(2, 6 * planes, lat),
            scratch(fields, levels, padded, lat),
            scratch(fields, levels, padded, lat),
            dma((2,)),
        ],
        "clone_window",
    )(chosen, edges, sister, got_edges, got_odd, *late, coef, region_weight, action, added, *inner, *got_inner, *odd_inner)
    if strips == 4:
        one, two, three = [across(sums, "lon", bit) for bit in (1, 2, 3)]
        sums = (sums + one) + (two + three)
    else:
        bit = 1
        while bit < strips:
            sums = sums + across(sums, "lon", bit)
            bit *= 2
    return final_state, sums[:, :2]


def solution(mesh):
    in_specs = (
        P(("ens", "mem"), None, None, "lon", None),
        P(("ens", "mem")),
        P(("ens", "mem")),
        P("ens", None, None, "lon", None),
        P(None, "lon", None),
        P("lon", None),
    )
    out_specs = (P(("ens", "mem"), None, None, "lon", None), P(("ens", "mem"), None))
    return jax.shard_map(body, mesh=mesh, in_specs=in_specs, out_specs=out_specs, check_vma=False)
```

```python
import functools
import jax
import jax.numpy as jnp
from jax import lax
from jax.experimental import pallas as pl
from jax.experimental.pallas import tpu as pltpu
from jax.sharding import PartitionSpec as P

STEPS = 3
TIME_STEP = 0.2
TILE = 8
TOP = 2 * TILE
CUTS = (0, 4)
VMEM_LIMIT = 48 * 1024 * 1024

ANY = pl.BlockSpec(memory_space=pl.ANY)
HBM = pl.BlockSpec(memory_space=pltpu.HBM)
VMEM = pl.BlockSpec(memory_space=pltpu.VMEM)
SMEM = pl.BlockSpec(memory_space=pltpu.SMEM)


def call(kernel, out_shape, in_specs, out_specs, scratch_shapes, name, flops=0):
    return pl.pallas_call(
        kernel,
        out_shape=out_shape,
        in_specs=in_specs,
        out_specs=out_specs,
        scratch_shapes=scratch_shapes,
        name=name,
        compiler_params=pltpu.CompilerParams(vmem_limit_bytes=VMEM_LIMIT),
        cost_estimate=pl.CostEstimate(flops=flops, bytes_accessed=1 << 20, transcendentals=0),
    )


def f32(*shape):
    return jax.ShapeDtypeStruct(shape, jnp.float32)


def lane_steps(rows):
    lane = lax.broadcasted_iota(jnp.int32, (rows, 128), 1)
    north = jnp.where(lane == 127, 0.0, TIME_STEP).astype(jnp.float32)
    south = jnp.where(lane == 0, 0.0, TIME_STEP).astype(jnp.float32)
    return north, south


def advance(source, target, coef, fields, blocks):
    north_step, south_step = lane_steps(TILE)
    for level in range(source.shape[1]):
        for block in blocks:
            row = TILE + TILE * block
            here = pl.ds(row, TILE)
            zonal = source[0, level, here, :]
            merid = source[1, level, here, :]
            spot = pl.ds(TILE * block, TILE)
            east = coef[level, 0, spot, :] - TIME_STEP * jnp.minimum(zonal, 0.0)
            west = coef[level, 1, spot, :] + TIME_STEP * jnp.maximum(zonal, 0.0)
            north = coef[level, 2, spot, :] - north_step * jnp.minimum(merid, 0.0)
            south = coef[level, 3, spot, :] + south_step * jnp.maximum(merid, 0.0)
            keep = 1.0 - ((east + west) + (north + south))
            for field in fields:
                centre = source[field, level, here, :]
                target[field, level, here, :] = (
                    keep * centre
                    + east * source[field, level, pl.ds(row + 1, TILE), :]
                    + west * source[field, level, pl.ds(row - 1, TILE), :]
                    + north * pltpu.roll(centre, 127, 1)
                    + south * pltpu.roll(centre, 1, 1)
                )


def observe(values, weight):
    total = jnp.zeros((TILE, 128), jnp.float32)
    for block in range(weight.shape[0] // TILE):
        square = jnp.zeros((TILE, 128), jnp.float32)
        for level in range(values.shape[1]):
            spot = values[2, level, pl.ds(TOP + TILE * block, TILE), :]
            square = square + spot * spot
        total = total + weight[pl.ds(TILE * block, TILE), :] * square
    return total


def early_rows(planes, own_planes, levels):
    own = 0
    added = own + 3 * own_planes
    kappa = added + 3 * planes
    total = kappa + 6 * levels
    return own, added, kappa, -(-total // TILE) * TILE


def field_parts():
    return [pl.ds(start, stop - start) for start, stop in zip(CUTS, CUTS[1:])]


def start_all(copies):
    for copy in copies:
        copy.start()
    return copies


def wait_all(copies):
    for copy in copies:
        copy.wait()


def edge_copies(source, target, sems, first):
    rows = source.shape[-2]
    lead = (slice(None),) * (len(source.shape) - 2)
    return [
        pltpu.make_async_copy(
            source.at[(*lead, pl.ds(0, TILE))], target.at[(*lead, pl.ds(0, TILE))], sems.at[first]
        ),
        pltpu.make_async_copy(
            source.at[(*lead, pl.ds(rows - TILE, TILE))], target.at[(*lead, pl.ds(TILE, TILE))], sems.at[first + 1]
        ),
    ]


def pair_put(out_a, out_b, even, offset, low_rows, high_rows):
    spot = pl.ds(offset, low_rows.shape[0])
    out_a[spot, :] = jnp.where(even, high_rows, low_rows)
    out_b[spot, :] = jnp.where(even, low_rows, high_rows)


def pair_get(halo, got_a, got_b, even):
    a, b = got_a[...], got_b[...]
    halo[0] = jnp.where(even, b, a)
    halo[1] = jnp.where(even, a, b)


def even_strip():
    return lax.rem(lax.axis_index("lon"), 2) == 0


def edge_kernel(own, edges, *refs):
    *inner, sems = refs
    rows = own.shape[3]
    wait_all(start_all(edge_copies(own.at[0], edges, sems, 0) + [
        pltpu.make_async_copy(own.at[0, part, :, pl.ds(TILE, rows - 2 * TILE), :], target, sems.at[2 + i])
        for i, (part, target) in enumerate(zip(field_parts(), inner))
    ]))


def early_kernel(general, ancestor, selector, edges, perturbations, kappa, out_a, out_b, chosen, added, spread, sems):
    fields, levels = edges.shape[:2]
    rows = kappa.shape[1]
    which = jnp.clip(selector[0], 0, perturbations.shape[0] - 1)
    chosen[0] = 2 if general else lax.axis_index("mem") ^ ancestor[0]
    chosen[1] = which
    strip = pl.ds(TOP, rows)
    wait_all(start_all([
        pltpu.make_async_copy(perturbations.at[which], added.at[:, :, strip, :], sems.at[0]),
        pltpu.make_async_copy(kappa, spread.at[:, strip, :], sems.at[1]),
    ]))
    even = even_strip()
    put = functools.partial(pair_put, out_a, out_b, even)
    at_own, at_added, at_kappa, _ = early_rows(fields * levels, 3 * levels, levels)
    end = TOP + rows
    for field in range(fields):
        for level in range(levels):
            plane = field * levels + level
            if field < 3:
                put(at_own + 3 * plane, edges[field, level, 0:3, :], edges[field, level, 13:16, :])
            put(at_added + 3 * plane, added[field, level, TOP : TOP + 3, :], added[field, level, end - 3 : end, :])
    for level in range(levels):
        put(at_kappa + 6 * level, spread[level, TOP : TOP + 6, :], spread[level, end - 6 : end, :])


def pick(rel, choices):
    for number, choice in enumerate(choices):
        pl.when(rel == number if number < 3 else rel > 2)(choice)


def late_kernel(chosen, edges, sister, got_edges, got_odd, out_a, out_b):
    fields, levels = edges.shape[:2]
    even = even_strip()

    def packed(source):
        rows = source.shape[2]

        def put():
            for field in range(fields):
                for level in range(levels):
                    low, high = source[field, level, 0:6, :], source[field, level, rows - 6 : rows, :]
                    pair_put(out_a, out_b, even, 6 * (field * levels + level), low, high)

        return put

    pick(chosen[0], [packed(edges), packed(sister.at[0]), packed(got_edges), packed(got_odd)])


def lay(target, fields, edges, inner):
    rows = inner[0].shape[2] + 2 * TILE
    for field in range(fields):
        number = max(i for i, start in enumerate(CUTS[:-1]) if start <= field)
        for level in range(target.shape[1]):
            target[field, level, pl.ds(TOP, TILE), :] = edges[field, level, 0:TILE, :]
            target[field, level, pl.ds(TOP + TILE, rows - 2 * TILE), :] = inner[number][field - CUTS[number], level]
            target[field, level, pl.ds(TOP + rows - TILE, TILE), :] = edges[field, level, TILE : 2 * TILE, :]


def prepare_kernel(edges, weight, got_a, got_b, spread, added_in, *refs):
    parts = len(CUTS) - 1
    inner, (coef, action, added, halo, present, following, padded) = refs[:parts], refs[parts:]
    fields, levels = edges.shape[:2]
    rows = weight.shape[0]
    lay(present, 3, edges, inner)
    pair_get(halo, got_a, got_b, even_strip())
    at_own, at_added, at_kappa, _ = early_rows(fields * levels, 3 * levels, levels)
    end = TOP + rows
    strip = pl.ds(TOP, rows)
    for level in range(levels):
        padded[level, strip, :] = spread[level, strip, :]
        padded[level, pl.ds(TOP - 6, 6), :] = halo[0, pl.ds(at_kappa + 6 * level, 6), :]
        padded[level, pl.ds(end, 6), :] = halo[1, pl.ds(at_kappa + 6 * level, 6), :]
        for field in range(fields):
            plane = field * levels + level
            if field < 3:
                present[field, level, pl.ds(TOP - 3, 3), :] = halo[0, pl.ds(at_own + 3 * plane, 3), :]
                present[field, level, pl.ds(end, 3), :] = halo[1, pl.ds(at_own + 3 * plane, 3), :]
            added[field, level, strip, :] = added_in[field, level, strip, :]
            added[field, level, pl.ds(TOP - 3, 3), :] = halo[0, pl.ds(at_added + 3 * plane, 3), :]
            added[field, level, pl.ds(end, 3), :] = halo[1, pl.ds(at_added + 3 * plane, 3), :]
    blocks = range(rows // TILE + 2)
    north_step, south_step = lane_steps(TILE)
    for level in range(levels):
        for block in blocks:
            row = TILE + TILE * block
            spot = pl.ds(TILE * block, TILE)
            centre = padded[level, pl.ds(row, TILE), :]
            half = 0.5 * TIME_STEP
            coef[level, 0, spot, :] = half * (centre + padded[level, pl.ds(row + 1, TILE), :])
            coef[level, 1, spot, :] = half * (centre + padded[level, pl.ds(row - 1, TILE), :])
            coef[level, 2, spot, :] = (0.5 * north_step) * (centre + pltpu.roll(centre, 127, 1))
            coef[level, 3, spot, :] = (0.5 * south_step) * (centre + pltpu.roll(centre, 1, 1))
    advance(present, following, coef, (0, 1, 2), blocks)
    total = observe(following, weight)
    advance(following, present, coef, (0, 1, 2), blocks)
    total = total + observe(present, weight)
    advance(present, following, coef, (2,), blocks[1:-1])
    action[...] = total + observe(following, weight)


def clone_kernel(scale, chosen, edges, sister, got_edges, got_odd, got_a, got_b, coef, weight, action, added, *refs):
    parts = len(CUTS) - 1
    inner, got_inner, odd_inner = [refs[i * parts : (i + 1) * parts] for i in range(3)]
    final, far, middle, near, halo, present, following, out_sems = refs[3 * parts :]
    fields, levels = edges.shape[:2]
    rows = weight.shape[0]
    end = TOP + rows
    strip = pl.ds(TOP, rows)

    def whole():
        for field in range(fields):
            for level in range(levels):
                present[field, level, strip, :] = sister[0, field, level]

    def joined(edges, inner):
        return lambda: lay(present, fields, edges, inner)

    pick(chosen[0], [joined(edges, inner), whole, joined(got_edges, got_inner), joined(got_odd, odd_inner)])
    pair_get(halo, got_a, got_b, even_strip())
    for field in range(fields):
        for level in range(levels):
            plane = field * levels + level
            present[field, level, pl.ds(TOP - 6, 6), :] = halo[0, pl.ds(6 * plane, 6), :]
            present[field, level, pl.ds(end, 6), :] = halo[1, pl.ds(6 * plane, 6), :]
    blocks = range(rows // TILE + 2)
    every = range(fields)

    def two_steps(pair, total):
        advance(present, following, coef, every, blocks)

        @pl.when(pair == 1)
        def _():
            for field in every:
                for level in range(levels):
                    for block in blocks:
                        spot = pl.ds(TILE + TILE * block, TILE)
                        following[field, level, spot, :] += added[field, level, spot, :]

        advance(following, present, coef, every, blocks)
        return total + jnp.where(pair == 1, 1.0, 0.0) * observe(present, weight)

    total = lax.fori_loop(0, 2, two_steps, jnp.zeros((TILE, 128), jnp.float32))
    advance(present, following, coef, every, blocks)
    total = total + observe(following, weight)
    half = levels // 2
    outs = []
    for low, high in ((0, half), (half, levels)):
        part = pl.ds(low, high - low)
        advance(following.at[:, part], present.at[:, part], coef.at[part], every, blocks[1:-1])
        outs += start_all([
            pltpu.make_async_copy(present.at[:, part, strip, :], final.at[0, :, part], out_sems.at[len(outs)])
        ])
    total = total + observe(present, weight)
    first = jnp.sum(action[...]) * scale
    second = jnp.sum(total) * scale
    lane = lax.broadcasted_iota(jnp.int32, (1, 128), 1)
    sums = jnp.where(lane == 0, first, jnp.where(lane == 1, second, 0.0))
    for ref in (far, middle, near):
        ref[...] = jnp.broadcast_to(sums, ref.shape)
    wait_all(outs)


def body(initial_state, ancestor, selector, perturbations, diffusivity, region_weight):
    _, fields, levels, rows, lat = initial_state.shape
    members, strips = lax.axis_size("mem"), lax.axis_size("lon")
    planes = fields * levels
    general = members != 4
    scale = 1.0 / (levels * lat * rows * strips)
    dma = pltpu.SemaphoreType.DMA

    def scratch(*shape):
        return pltpu.VMEM(shape, jnp.float32)

    def across(value, axis, bit):
        return lax.ppermute(value, axis, [(i, i ^ bit) for i in range(lax.axis_size(axis))])

    def after(values, others):
        return lax.optimization_barrier((values, others))[0]

    def round_strips(a, b):
        pairs_a = [(i, i ^ 1) for i in range(strips)]
        pairs_b = [(i, (i + 1 if i % 2 else i - 1) % strips) for i in range(strips)]
        return lax.ppermute(a, "lon", pairs_a), lax.ppermute(b, "lon", pairs_b)

    own = pltpu.with_memory_space_constraint(initial_state, pltpu.HBM)
    perturbations = pltpu.with_memory_space_constraint(perturbations, pltpu.HBM)
    kappa = pltpu.with_memory_space_constraint(diffusivity, pltpu.HBM)
    sister = initial_state if general else across(initial_state, "mem", 1)

    early_total = early_rows(planes, 3 * levels, levels)[-1]
    parts = [f32(part.size, levels, rows - 2 * TILE, lat) for part in field_parts()]
    edges, *inner = call(
        edge_kernel,
        (f32(fields, levels, 2 * TILE, lat), *parts),
        [HBM],
        [ANY] * (1 + len(parts)),
        [dma((2 + len(parts),))],
        "edges",
    )(own)
    padded = rows + 2 * TOP
    early_a, early_b, chosen, added, spread = call(
        functools.partial(early_kernel, general),
        (
            f32(early_total, lat),
            f32(early_total, lat),
            jax.ShapeDtypeStruct((2,), jnp.int32),
            f32(fields, levels, padded, lat),
            f32(levels, padded, lat),
        ),
        [SMEM, SMEM, VMEM, HBM, HBM],
        (VMEM, VMEM, SMEM, VMEM, VMEM),
        [dma((2,))],
        "early_halo",
    )(ancestor, selector, after(edges, sister), perturbations, kappa)
    if general:
        picked = jnp.take(lax.all_gather(initial_state, "mem", axis=0, tiled=True), ancestor, axis=0)[0]
        got_edges = got_odd = jnp.concatenate([picked[:, :, :TILE], picked[:, :, rows - TILE :]], axis=2)
        got_inner = odd_inner = [picked[low:high, :, TILE : rows - TILE] for low, high in zip(CUTS, CUTS[1:])]
    else:
        got_edges = across(edges, "mem", 2)
        got_odd = across(after(got_edges, early_a), "mem", 1)
        got_inner = [across(part, "mem", 2) for part in inner]

    early = round_strips(early_a, early_b)
    late = call(
        late_kernel,
        (f32(6 * planes, lat), f32(6 * planes, lat)),
        [SMEM] + [VMEM] * 4,
        (VMEM, VMEM),
        [],
        "late_halo",
        flops=1 << 30,
    )(chosen, edges, sister, got_edges, got_odd)
    packed = late
    late = round_strips(*late)

    coef, action, added = call(
        prepare_kernel,
        (f32(levels, 4, rows + 2 * TILE, lat), f32(TILE, lat), f32(fields, levels, padded, lat)),
        [VMEM] * (6 + len(parts)),
        (VMEM, VMEM, VMEM),
        [
            scratch(2, early_total, lat),
            scratch(3, levels, padded, lat),
            scratch(3, levels, padded, lat),
            scratch(levels, padded, lat),
        ],
        "prepare",
        flops=1 << 30,
    )(edges, region_weight, *early, spread, added, *inner)
    if not general:
        odd_inner = [across(part, "mem", 1) for part in after(got_inner, (late, action))]
    final_state, far, middle, near = call(
        functools.partial(clone_kernel, scale),
        (f32(1, fields, levels, rows, lat), f32(16, lat), f32(8, lat), f32(1, lat)),
        [SMEM] + [VMEM] * (10 + 3 * len(parts)),
        (HBM, VMEM, VMEM, VMEM),
        [
            scratch(2, 6 * planes, lat),
            scratch(fields, levels, padded, lat),
            scratch(fields, levels, padded, lat),
            dma((2,)),
        ],
        "clone_window",
    )(chosen, edges, sister, got_edges, got_odd, *late, coef, region_weight, action, added, *inner, *got_inner, *odd_inner)
    if strips == 4:
        three, two, one = across(far, "lon", 3), across(middle, "lon", 2), across(near, "lon", 1)
        sums = (near + one) + (two[:1] + three[:1])
    else:
        sums, bit = near, 1
        while bit < strips:
            sums = sums + across(sums, "lon", bit)
            bit *= 2
    return final_state, sums[:, :2]


def solution(mesh):
    in_specs = (
        P(("ens", "mem"), None, None, "lon", None),
        P(("ens", "mem")),
        P(("ens", "mem")),
        P("ens", None, None, "lon", None),
        P(None, "lon", None),
        P("lon", None),
    )
    out_specs = (P(("ens", "mem"), None, None, "lon", None), P(("ens", "mem"), None))
    return jax.shard_map(body, mesh=mesh, in_specs=in_specs, out_specs=out_specs, check_vma=False)
```

```python
import functools
import jax
import jax.numpy as jnp
from jax import lax
from jax.experimental import pallas as pl
from jax.experimental.pallas import tpu as pltpu
from jax.sharding import PartitionSpec as P

STEPS = 3
TIME_STEP = 0.2
TILE = 8
TOP = 2 * TILE
VMEM_LIMIT = 48 * 1024 * 1024

ANY = pl.BlockSpec(memory_space=pl.ANY)
HBM = pl.BlockSpec(memory_space=pltpu.HBM)
VMEM = pl.BlockSpec(memory_space=pltpu.VMEM)
SMEM = pl.BlockSpec(memory_space=pltpu.SMEM)


def call(kernel, out_shape, in_specs, out_specs, scratch_shapes, name, flops=0):
    return pl.pallas_call(
        kernel,
        out_shape=out_shape,
        in_specs=in_specs,
        out_specs=out_specs,
        scratch_shapes=scratch_shapes,
        name=name,
        compiler_params=pltpu.CompilerParams(vmem_limit_bytes=VMEM_LIMIT),
        cost_estimate=pl.CostEstimate(flops=flops, bytes_accessed=1 << 20, transcendentals=0),
    )


def f32(*shape):
    return jax.ShapeDtypeStruct(shape, jnp.float32)


def lane_steps(rows):
    lane = lax.broadcasted_iota(jnp.int32, (rows, 128), 1)
    north = jnp.where(lane == 127, 0.0, TIME_STEP).astype(jnp.float32)
    south = jnp.where(lane == 0, 0.0, TIME_STEP).astype(jnp.float32)
    return north, south


def face_factors(level, zonal, merid, coef, block):
    north_step, south_step = lane_steps(TILE)
    spot = pl.ds(TILE * block, TILE)
    east = coef[level, 0, spot, :] - TIME_STEP * jnp.minimum(zonal, 0.0)
    west = coef[level, 1, spot, :] + TIME_STEP * jnp.maximum(zonal, 0.0)
    north = coef[level, 2, spot, :] - north_step * jnp.minimum(merid, 0.0)
    south = coef[level, 3, spot, :] + south_step * jnp.maximum(merid, 0.0)
    return 1.0 - ((east + west) + (north + south)), east, west, north, south


def stepped(source, row, factors):
    keep, east, west, north, south = factors
    centre = source[pl.ds(row, TILE), :]
    return (
        keep * centre
        + east * source[pl.ds(row + 1, TILE), :]
        + west * source[pl.ds(row - 1, TILE), :]
        + north * pltpu.roll(centre, 127, 1)
        + south * pltpu.roll(centre, 1, 1)
    )


def advance(source, target, coef, fields, blocks):
    for level in range(source.shape[1]):
        for block in blocks:
            row = TILE + TILE * block
            here = pl.ds(row, TILE)
            factors = face_factors(level, source[0, level, here, :], source[1, level, here, :], coef, block)
            for field in fields:
                target[field, level, here, :] = stepped(source.at[field, level], row, factors)


def observe(values, weight):
    total = jnp.zeros((TILE, 128), jnp.float32)
    for block in range(weight.shape[0] // TILE):
        square = jnp.zeros((TILE, 128), jnp.float32)
        for level in range(values.shape[1]):
            spot = values[2, level, pl.ds(TOP + TILE * block, TILE), :]
            square = square + spot * spot
        total = total + weight[pl.ds(TILE * block, TILE), :] * square
    return total


def early_rows(planes, own_planes, levels):
    own = 0
    added = own + 3 * own_planes
    kappa = added + 3 * planes
    total = kappa + 6 * levels
    return own, added, kappa, -(-total // TILE) * TILE


def start_all(copies):
    for copy in copies:
        copy.start()
    return copies


def wait_all(copies):
    for copy in copies:
        copy.wait()


def edge_copies(source, target, sems, first):
    rows = source.shape[-2]
    lead = (slice(None),) * (len(source.shape) - 2)
    return [
        pltpu.make_async_copy(
            source.at[(*lead, pl.ds(0, TILE))], target.at[(*lead, pl.ds(0, TILE))], sems.at[first]
        ),
        pltpu.make_async_copy(
            source.at[(*lead, pl.ds(rows - TILE, TILE))], target.at[(*lead, pl.ds(TILE, TILE))], sems.at[first + 1]
        ),
    ]


def pair_put(out_a, out_b, even, offset, low_rows, high_rows):
    spot = pl.ds(offset, low_rows.shape[0])
    out_a[spot, :] = jnp.where(even, high_rows, low_rows)
    out_b[spot, :] = jnp.where(even, low_rows, high_rows)


def pair_get(halo, got_a, got_b, even):
    a, b = got_a[...], got_b[...]
    halo[0] = jnp.where(even, b, a)
    halo[1] = jnp.where(even, a, b)


def even_strip():
    return lax.rem(lax.axis_index("lon"), 2) == 0


def edge_kernel(own, edges, sems):
    wait_all(start_all(edge_copies(own.at[0], edges, sems, 0)))


def inner_kernel(own, inner, sem):
    rows = own.shape[3]
    wait_all(start_all([pltpu.make_async_copy(own.at[0, :, :, pl.ds(TILE, rows - 2 * TILE), :], inner, sem)]))


def early_kernel(general, ancestor, selector, edges, perturbations, kappa, out_a, out_b, chosen, added, spread, sems):
    fields, levels = edges.shape[:2]
    rows = kappa.shape[1]
    which = jnp.clip(selector[0], 0, perturbations.shape[0] - 1)
    chosen[0] = 2 if general else lax.axis_index("mem") ^ ancestor[0]
    chosen[1] = which
    strip = pl.ds(TOP, rows)
    wait_all(start_all([
        pltpu.make_async_copy(perturbations.at[which], added.at[:, :, strip, :], sems.at[0]),
        pltpu.make_async_copy(kappa, spread.at[:, strip, :], sems.at[1]),
    ]))
    even = even_strip()
    put = functools.partial(pair_put, out_a, out_b, even)
    at_own, at_added, at_kappa, _ = early_rows(fields * levels, 3 * levels, levels)
    end = TOP + rows
    for field in range(fields):
        for level in range(levels):
            plane = field * levels + level
            if field < 3:
                put(at_own + 3 * plane, edges[field, level, 0:3, :], edges[field, level, 13:16, :])
            put(at_added + 3 * plane, added[field, level, TOP : TOP + 3, :], added[field, level, end - 3 : end, :])
    for level in range(levels):
        put(at_kappa + 6 * level, spread[level, TOP : TOP + 6, :], spread[level, end - 6 : end, :])


def pick(rel, choices):
    for number, choice in enumerate(choices):
        pl.when(rel == number if number < 3 else rel > 2)(choice)


def late_kernel(chosen, edges, sister, got_edges, got_odd, out_a, out_b):
    fields, levels = edges.shape[:2]
    even = even_strip()

    def packed(source):
        rows = source.shape[2]

        def put():
            for field in range(fields):
                for level in range(levels):
                    low, high = source[field, level, 0:6, :], source[field, level, rows - 6 : rows, :]
                    pair_put(out_a, out_b, even, 6 * (field * levels + level), low, high)

        return put

    pick(chosen[0], [packed(edges), packed(sister.at[0]), packed(got_edges), packed(got_odd)])


def lay(target, field, edges, inner):
    rows = inner.shape[2] + 2 * TILE
    for level in range(inner.shape[1]):
        target[level, pl.ds(TOP, TILE), :] = edges[field, level, 0:TILE, :]
        target[level, pl.ds(TOP + TILE, rows - 2 * TILE), :] = inner[field, level]
        target[level, pl.ds(TOP + rows - TILE, TILE), :] = edges[field, level, TILE : 2 * TILE, :]


def prepare_kernel(edges, inner, weight, got_a, got_b, spread, added_in, coef, action, added,
                   halo, present, following, padded):
    fields, levels = edges.shape[:2]
    rows = weight.shape[0]
    for field in range(3):
        lay(present.at[field], field, edges, inner)
    pair_get(halo, got_a, got_b, even_strip())
    at_own, at_added, at_kappa, _ = early_rows(fields * levels, 3 * levels, levels)
    end = TOP + rows
    strip = pl.ds(TOP, rows)
    for level in range(levels):
        padded[level, strip, :] = spread[level, strip, :]
        padded[level, pl.ds(TOP - 6, 6), :] = halo[0, pl.ds(at_kappa + 6 * level, 6), :]
        padded[level, pl.ds(end, 6), :] = halo[1, pl.ds(at_kappa + 6 * level, 6), :]
        for field in range(fields):
            plane = field * levels + level
            if field < 3:
                present[field, level, pl.ds(TOP - 3, 3), :] = halo[0, pl.ds(at_own + 3 * plane, 3), :]
                present[field, level, pl.ds(end, 3), :] = halo[1, pl.ds(at_own + 3 * plane, 3), :]
            added[field, level, strip, :] = added_in[field, level, strip, :]
            added[field, level, pl.ds(TOP - 3, 3), :] = halo[0, pl.ds(at_added + 3 * plane, 3), :]
            added[field, level, pl.ds(end, 3), :] = halo[1, pl.ds(at_added + 3 * plane, 3), :]
    blocks = range(rows // TILE + 2)
    north_step, south_step = lane_steps(TILE)
    for level in range(levels):
        for block in blocks:
            row = TILE + TILE * block
            spot = pl.ds(TILE * block, TILE)
            centre = padded[level, pl.ds(row, TILE), :]
            half = 0.5 * TIME_STEP
            coef[level, 0, spot, :] = half * (centre + padded[level, pl.ds(row + 1, TILE), :])
            coef[level, 1, spot, :] = half * (centre + padded[level, pl.ds(row - 1, TILE), :])
            coef[level, 2, spot, :] = (0.5 * north_step) * (centre + pltpu.roll(centre, 127, 1))
            coef[level, 3, spot, :] = (0.5 * south_step) * (centre + pltpu.roll(centre, 1, 1))
    advance(present, following, coef, (0, 1, 2), blocks)
    total = observe(following, weight)
    advance(following, present, coef, (0, 1, 2), blocks)
    total = total + observe(present, weight)
    advance(present, following, coef, (2,), blocks[1:-1])
    action[...] = total + observe(following, weight)


def wind_kernel(scale, chosen, edges, inner, sister, got_edges, got_odd, got_inner, odd_inner, got_a, got_b,
                coef, weight, action, added, winds, humid, warm, far, middle, near, halo, present, following):
    levels, rows = edges.shape[1], weight.shape[0]
    end = TOP + rows
    strip = pl.ds(TOP, rows)
    targets = [winds.at[0, 0], winds.at[0, 1], present, humid]

    def whole():
        for field, target in enumerate(targets):
            for level in range(levels):
                target[level, strip, :] = sister[0, field, level]

    def joined(edges, inner):
        def put():
            for field, target in enumerate(targets):
                lay(target, field, edges, inner)

        return put

    pick(chosen[0], [joined(edges, inner), whole, joined(got_edges, got_inner), joined(got_odd, odd_inner)])
    pair_get(halo, got_a, got_b, even_strip())
    for field, target in enumerate(targets):
        for level in range(levels):
            at = 6 * (field * levels + level)
            target[level, pl.ds(TOP - 6, 6), :] = halo[0, pl.ds(at, 6), :]
            target[level, pl.ds(end, 6), :] = halo[1, pl.ds(at, 6), :]
    every = range(rows // TILE + 2)
    now, later = present, following
    totals = [jnp.zeros((TILE, 128), jnp.float32) for _ in range(levels)]
    for step in range(2 * STEPS):
        last = step == 2 * STEPS - 1
        for level in range(levels):
            for block in every[1:-1] if last else every:
                row = TILE + TILE * block
                here = pl.ds(row, TILE)
                wind = winds.at[step]
                factors = face_factors(level, wind[0, level, here, :], wind[1, level, here, :], coef, block)
                for field in (0, 1) if not last else ():
                    moved = stepped(wind.at[field, level], row, factors)
                    if step == STEPS - 1:
                        moved = moved + added[field, level, here, :]
                    winds[step + 1, field, level, here, :] = moved
                moved = stepped(now.at[level], row, factors)
                if step == STEPS - 1:
                    moved = moved + added[2, level, here, :]
                if last:
                    warm[level, pl.ds(row - TOP, TILE), :] = moved
                else:
                    later[level, here, :] = moved
                if step >= STEPS and block in every[1:-1]:
                    totals[level] += weight[pl.ds(row - TOP, TILE), :] * moved * moved
        now, later = later, now
    first = jnp.sum(action[...]) * scale
    second = jnp.sum(sum(totals[1:], totals[0])) * scale
    lane = lax.broadcasted_iota(jnp.int32, (1, 128), 1)
    sums = jnp.where(lane == 0, first, jnp.where(lane == 1, second, 0.0))
    for ref in (far, middle, near):
        ref[...] = jnp.broadcast_to(sums, ref.shape)


def rest_kernel(winds, humid, warm, coef, added, final, wind_out, humid_out, present, following, sems):
    levels, rows = warm.shape[:2]
    every = range(rows // TILE + 2)
    copies = start_all([pltpu.make_async_copy(warm, final.at[0, 2], sems.at[0])])
    last = 2 * STEPS - 1

    def faces(step, level, block):
        here = pl.ds(TILE + TILE * block, TILE)
        return face_factors(level, winds[step, 0, level, here, :], winds[step, 1, level, here, :], coef, block)

    for level in range(levels):
        for block in every[1:-1]:
            factors = faces(last, level, block)
            for field in (0, 1):
                row = TILE + TILE * block
                wind_out[field, level, pl.ds(row - TOP, TILE), :] = stepped(winds.at[last, field, level], row, factors)
    copies += start_all([pltpu.make_async_copy(wind_out, final.at[0, pl.ds(0, 2)], sems.at[1])])
    now, later = humid, present
    for step in range(2 * STEPS):
        for level in range(levels):
            for block in every[1:-1] if step == last else every:
                row = TILE + TILE * block
                moved = stepped(now.at[level], row, faces(step, level, block))
                if step == STEPS - 1:
                    moved = moved + added[3, level, pl.ds(row, TILE), :]
                if step == last:
                    humid_out[level, pl.ds(row - TOP, TILE), :] = moved
                else:
                    later[level, pl.ds(row, TILE), :] = moved
        now, later = later, following if later is present else present
    copies += start_all([pltpu.make_async_copy(humid_out, final.at[0, 3], sems.at[2])])
    wait_all(copies)


def body(initial_state, ancestor, selector, perturbations, diffusivity, region_weight):
    _, fields, levels, rows, lat = initial_state.shape
    members, strips = lax.axis_size("mem"), lax.axis_size("lon")
    planes = fields * levels
    general = members != 4
    scale = 1.0 / (levels * lat * rows * strips)
    dma = pltpu.SemaphoreType.DMA

    def scratch(*shape):
        return pltpu.VMEM(shape, jnp.float32)

    def across(value, axis, bit):
        return lax.ppermute(value, axis, [(i, i ^ bit) for i in range(lax.axis_size(axis))])

    def after(values, others):
        return lax.optimization_barrier((values, others))[0]

    def round_strips(a, b):
        pairs_a = [(i, i ^ 1) for i in range(strips)]
        pairs_b = [(i, (i + 1 if i % 2 else i - 1) % strips) for i in range(strips)]
        return lax.ppermute(a, "lon", pairs_a), lax.ppermute(b, "lon", pairs_b)

    own = pltpu.with_memory_space_constraint(initial_state, pltpu.HBM)
    perturbations = pltpu.with_memory_space_constraint(perturbations, pltpu.HBM)
    kappa = pltpu.with_memory_space_constraint(diffusivity, pltpu.HBM)

    early_total = early_rows(planes, 3 * levels, levels)[-1]
    inner_shape = f32(fields, levels, rows - 2 * TILE, lat)
    edges = call(edge_kernel, f32(fields, levels, 2 * TILE, lat), [HBM], ANY, [dma((2,))], "edges")(own)
    inner = call(inner_kernel, inner_shape, [HBM], ANY, [dma], "inner")(after(own, edges))
    sister = initial_state if general else across(after(initial_state, inner), "mem", 1)
    padded = rows + 2 * TOP
    early_a, early_b, chosen, added, spread = call(
        functools.partial(early_kernel, general),
        (
            f32(early_total, lat),
            f32(early_total, lat),
            jax.ShapeDtypeStruct((2,), jnp.int32),
            f32(fields, levels, padded, lat),
            f32(levels, padded, lat),
        ),
        [SMEM, SMEM, VMEM, HBM, HBM],
        (VMEM, VMEM, SMEM, VMEM, VMEM),
        [dma((2,))],
        "early_halo",
    )(ancestor, selector, after(edges, inner), perturbations, kappa)
    if general:
        picked = jnp.take(lax.all_gather(initial_state, "mem", axis=0, tiled=True), ancestor, axis=0)[0]
        got_edges = got_odd = jnp.concatenate([picked[:, :, :TILE], picked[:, :, rows - TILE :]], axis=2)
        got_inner = odd_inner = picked[:, :, TILE : rows - TILE]
    else:
        got_edges = across(edges, "mem", 2)
        got_odd = across(after(got_edges, early_a), "mem", 1)
        got_inner = across(inner, "mem", 2)

    early = round_strips(early_a, early_b)
    late = call(
        late_kernel,
        (f32(6 * planes, lat), f32(6 * planes, lat)),
        [SMEM] + [VMEM] * 4,
        (VMEM, VMEM),
        [],
        "late_halo",
        1 << 30,
    )(chosen, edges, sister, got_edges, got_odd)
    packed = late
    late = round_strips(*late)

    coef, action, added = call(
        prepare_kernel,
        (f32(levels, 4, rows + 2 * TILE, lat), f32(TILE, lat), f32(fields, levels, padded, lat)),
        [VMEM] * 7,
        (VMEM, VMEM, VMEM),
        [
            scratch(2, early_total, lat),
            scratch(3, levels, padded, lat),
            scratch(3, levels, padded, lat),
            scratch(levels, padded, lat),
        ],
        "prepare",
        1 << 30,
    )(edges, inner, region_weight, *early, spread, added)
    if not general:
        odd_inner = across(after(got_inner, (late, action)), "mem", 1)
    winds, humid, warm, far, middle, near = call(
        functools.partial(wind_kernel, scale),
        (
            f32(2 * STEPS, 2, levels, padded, lat),
            f32(levels, padded, lat),
            f32(levels, rows, lat),
            f32(16, lat),
            f32(8, lat),
            f32(1, lat),
        ),
        [SMEM] + [VMEM] * 13,
        (VMEM,) * 6,
        [scratch(2, 6 * planes, lat), scratch(levels, padded, lat), scratch(levels, padded, lat)],
        "clone_winds",
    )(chosen, edges, inner, sister, got_edges, got_odd, got_inner, odd_inner, *late, coef, region_weight, action, added)
    final_state = call(
        rest_kernel,
        f32(1, fields, levels, rows, lat),
        [VMEM] * 5,
        HBM,
        [
            scratch(2, levels, rows, lat),
            scratch(levels, rows, lat),
            scratch(levels, padded, lat),
            scratch(levels, padded, lat),
            dma((3,)),
        ],
        "clone_rest",
    )(winds, humid, warm, coef, added)
    if strips == 4:
        three, two, one = across(far, "lon", 3), across(middle, "lon", 2), across(near, "lon", 1)
        sums = (near + one) + (two[:1] + three[:1])
    else:
        sums, bit = near, 1
        while bit < strips:
            sums = sums + across(sums, "lon", bit)
            bit *= 2
    return final_state, sums[:, :2]


def solution(mesh):
    in_specs = (
        P(("ens", "mem"), None, None, "lon", None),
        P(("ens", "mem")),
        P(("ens", "mem")),
        P("ens", None, None, "lon", None),
        P(None, "lon", None),
        P("lon", None),
    )
    out_specs = (P(("ens", "mem"), None, None, "lon", None), P(("ens", "mem"), None))
    return jax.shard_map(body, mesh=mesh, in_specs=in_specs, out_specs=out_specs, check_vma=False)
```

```python
import functools
import jax
import jax.numpy as jnp
from jax import lax
from jax.experimental import pallas as pl
from jax.experimental.pallas import tpu as pltpu
from jax.sharding import PartitionSpec as P

STEPS = 3
TIME_STEP = 0.2
TILE = 8
TOP = 2 * TILE
VMEM_LIMIT = 12 * 1024 * 1024

ANY = pl.BlockSpec(memory_space=pl.ANY)
HBM = pl.BlockSpec(memory_space=pltpu.HBM)
VMEM = pl.BlockSpec(memory_space=pltpu.VMEM)
SMEM = pl.BlockSpec(memory_space=pltpu.SMEM)


def call(kernel, out_shape, in_specs, out_specs, scratch_shapes, name, flops=0):
    return pl.pallas_call(
        kernel,
        out_shape=out_shape,
        in_specs=in_specs,
        out_specs=out_specs,
        scratch_shapes=scratch_shapes,
        name=name,
        compiler_params=pltpu.CompilerParams(vmem_limit_bytes=VMEM_LIMIT),
        cost_estimate=pl.CostEstimate(flops=flops, bytes_accessed=1 << 20, transcendentals=0),
    )


def f32(*shape):
    return jax.ShapeDtypeStruct(shape, jnp.float32)


def lane_steps(rows):
    lane = lax.broadcasted_iota(jnp.int32, (rows, 128), 1)
    north = jnp.where(lane == 127, 0.0, TIME_STEP).astype(jnp.float32)
    south = jnp.where(lane == 0, 0.0, TIME_STEP).astype(jnp.float32)
    return north, south


def face_factors(level, zonal, merid, coef, block):
    north_step, south_step = lane_steps(TILE)
    spot = pl.ds(TILE * block, TILE)
    east = coef[level, 0, spot, :] - TIME_STEP * jnp.minimum(zonal, 0.0)
    west = coef[level, 1, spot, :] + TIME_STEP * jnp.maximum(zonal, 0.0)
    north = coef[level, 2, spot, :] - north_step * jnp.minimum(merid, 0.0)
    south = coef[level, 3, spot, :] + south_step * jnp.maximum(merid, 0.0)
    return 1.0 - ((east + west) + (north + south)), east, west, north, south


def stepped(source, row, factors):
    keep, east, west, north, south = factors
    centre = source[pl.ds(row, TILE), :]
    return (
        keep * centre
        + east * source[pl.ds(row + 1, TILE), :]
        + west * source[pl.ds(row - 1, TILE), :]
        + north * pltpu.roll(centre, 127, 1)
        + south * pltpu.roll(centre, 1, 1)
    )


def advance(source, target, coef, fields, blocks):
    for level in range(source.shape[1]):
        for block in blocks:
            row = TILE + TILE * block
            here = pl.ds(row, TILE)
            factors = face_factors(level, source[0, level, here, :], source[1, level, here, :], coef, block)
            for field in fields:
                target[field, level, here, :] = stepped(source.at[field, level], row, factors)


def observe(values, weight):
    total = jnp.zeros((TILE, 128), jnp.float32)
    for block in range(weight.shape[0] // TILE):
        square = jnp.zeros((TILE, 128), jnp.float32)
        for level in range(values.shape[1]):
            spot = values[2, level, pl.ds(TOP + TILE * block, TILE), :]
            square = square + spot * spot
        total = total + weight[pl.ds(TILE * block, TILE), :] * square
    return total


def early_rows(planes, own_planes, levels):
    own = 0
    added = own + 3 * own_planes
    kappa = added + 3 * planes
    total = kappa + 6 * levels
    return own, added, kappa, -(-total // TILE) * TILE


def start_all(copies):
    for copy in copies:
        copy.start()
    return copies


def wait_all(copies):
    for copy in copies:
        copy.wait()


def edge_copies(source, target, sems, first):
    rows = source.shape[-2]
    lead = (slice(None),) * (len(source.shape) - 2)
    return [
        pltpu.make_async_copy(
            source.at[(*lead, pl.ds(0, TILE))], target.at[(*lead, pl.ds(0, TILE))], sems.at[first]
        ),
        pltpu.make_async_copy(
            source.at[(*lead, pl.ds(rows - TILE, TILE))], target.at[(*lead, pl.ds(TILE, TILE))], sems.at[first + 1]
        ),
    ]


def pair_put(out_a, out_b, even, offset, low_rows, high_rows):
    spot = pl.ds(offset, low_rows.shape[0])
    out_a[spot, :] = jnp.where(even, high_rows, low_rows)
    out_b[spot, :] = jnp.where(even, low_rows, high_rows)


def pair_get(halo, got_a, got_b, even):
    a, b = got_a[0 : halo.shape[1], :], got_b[0 : halo.shape[1], :]
    halo[0] = jnp.where(even, b, a)
    halo[1] = jnp.where(even, a, b)


def even_strip():
    return lax.rem(lax.axis_index("lon"), 2) == 0


def edge_kernel(own, edges, sems):
    wait_all(start_all(edge_copies(own.at[0], edges, sems, 0)))


def inner_kernel(own, inner, sem):
    rows = own.shape[3]
    wait_all(start_all([pltpu.make_async_copy(own.at[0, :, :, pl.ds(TILE, rows - 2 * TILE), :], inner, sem)]))


def early_kernel(general, ancestor, selector, edges, perturbations, kappa, out_a, out_b, chosen, added, spread, sems):
    fields, levels = edges.shape[:2]
    rows = kappa.shape[1]
    which = jnp.clip(selector[0], 0, perturbations.shape[0] - 1)
    chosen[0] = 2 if general else lax.axis_index("mem") ^ ancestor[0]
    chosen[1] = which
    strip = pl.ds(TOP, rows)
    wait_all(start_all([
        pltpu.make_async_copy(perturbations.at[which], added.at[:, :, strip, :], sems.at[0]),
        pltpu.make_async_copy(kappa, spread.at[:, strip, :], sems.at[1]),
    ]))
    even = even_strip()
    put = functools.partial(pair_put, out_a, out_b, even)
    at_own, at_added, at_kappa, _ = early_rows(fields * levels, 3 * levels, levels)
    end = TOP + rows
    for field in range(fields):
        for level in range(levels):
            plane = field * levels + level
            if field < 3:
                put(at_own + 3 * plane, edges[field, level, 0:3, :], edges[field, level, 13:16, :])
            put(at_added + 3 * plane, added[field, level, TOP : TOP + 3, :], added[field, level, end - 3 : end, :])
    for level in range(levels):
        put(at_kappa + 6 * level, spread[level, TOP : TOP + 6, :], spread[level, end - 6 : end, :])


def pick(rel, choices):
    for number, choice in enumerate(choices):
        pl.when(rel == number if number < 3 else rel > 2)(choice)


def late_kernel(chosen, edges, sister, got_edges, got_odd, out_a, out_b):
    fields, levels = edges.shape[:2]
    even = even_strip()

    def packed(source):
        rows = source.shape[2]

        def put():
            for field in range(fields):
                for level in range(levels):
                    low, high = source[field, level, 0:6, :], source[field, level, rows - 6 : rows, :]
                    pair_put(out_a, out_b, even, 6 * (field * levels + level), low, high)

        return put

    pick(chosen[0], [packed(edges), packed(sister.at[0]), packed(got_edges), packed(got_odd)])


def lay(target, field, edges, inner):
    rows = inner.shape[2] + 2 * TILE
    for level in range(inner.shape[1]):
        target[level, pl.ds(TOP, TILE), :] = edges[field, level, 0:TILE, :]
        target[level, pl.ds(TOP + TILE, rows - 2 * TILE), :] = inner[field, level]
        target[level, pl.ds(TOP + rows - TILE, TILE), :] = edges[field, level, TILE : 2 * TILE, :]


def prepare_kernel(edges, inner, weight, got_a, got_b, spread, added_in, coef, action, added,
                   halo, present, following, padded):
    fields, levels = edges.shape[:2]
    rows = weight.shape[0]
    for field in range(3):
        lay(present.at[field], field, edges, inner)
    pair_get(halo, got_a, got_b, even_strip())
    at_own, at_added, at_kappa, _ = early_rows(fields * levels, 3 * levels, levels)
    end = TOP + rows
    strip = pl.ds(TOP, rows)
    for level in range(levels):
        padded[level, strip, :] = spread[level, strip, :]
        padded[level, pl.ds(TOP - 6, 6), :] = halo[0, pl.ds(at_kappa + 6 * level, 6), :]
        padded[level, pl.ds(end, 6), :] = halo[1, pl.ds(at_kappa + 6 * level, 6), :]
        for field in range(fields):
            plane = field * levels + level
            if field < 3:
                present[field, level, pl.ds(TOP - 3, 3), :] = halo[0, pl.ds(at_own + 3 * plane, 3), :]
                present[field, level, pl.ds(end, 3), :] = halo[1, pl.ds(at_own + 3 * plane, 3), :]
            added[field, level, strip, :] = added_in[field, level, strip, :]
            added[field, level, pl.ds(TOP - 3, 3), :] = halo[0, pl.ds(at_added + 3 * plane, 3), :]
            added[field, level, pl.ds(end, 3), :] = halo[1, pl.ds(at_added + 3 * plane, 3), :]
    blocks = range(rows // TILE + 2)
    north_step, south_step = lane_steps(TILE)
    for level in range(levels):
        for block in blocks:
            row = TILE + TILE * block
            spot = pl.ds(TILE * block, TILE)
            centre = padded[level, pl.ds(row, TILE), :]
            half = 0.5 * TIME_STEP
            coef[level, 0, spot, :] = half * (centre + padded[level, pl.ds(row + 1, TILE), :])
            coef[level, 1, spot, :] = half * (centre + padded[level, pl.ds(row - 1, TILE), :])
            coef[level, 2, spot, :] = (0.5 * north_step) * (centre + pltpu.roll(centre, 127, 1))
            coef[level, 3, spot, :] = (0.5 * south_step) * (centre + pltpu.roll(centre, 1, 1))
    advance(present, following, coef, (0, 1, 2), blocks)
    total = observe(following, weight)
    advance(following, present, coef, (0, 1, 2), blocks)
    total = total + observe(present, weight)
    advance(present, following, coef, (2,), blocks[1:-1])
    action[...] = total + observe(following, weight)


def wind_kernel(scale, chosen, edges, inner, sister, got_edges, got_odd, got_inner, odd_inner, got_a, got_b,
                coef, weight, action, added, winds, humid, warm, far, middle, near, halo, present, following):
    levels, rows = edges.shape[1], weight.shape[0]
    end = TOP + rows
    strip = pl.ds(TOP, rows)
    targets = [winds.at[0, 0], winds.at[0, 1], present, humid]

    def whole():
        for field, target in enumerate(targets):
            for level in range(levels):
                target[level, strip, :] = sister[0, field, level]

    def joined(edges, inner):
        def put():
            for field, target in enumerate(targets):
                lay(target, field, edges, inner)

        return put

    pick(chosen[0], [joined(edges, inner), whole, joined(got_edges, got_inner), joined(got_odd, odd_inner)])
    pair_get(halo, got_a, got_b, even_strip())
    for field, target in enumerate(targets):
        for level in range(levels):
            at = 6 * (field * levels + level)
            target[level, pl.ds(TOP - 6, 6), :] = halo[0, pl.ds(at, 6), :]
            target[level, pl.ds(end, 6), :] = halo[1, pl.ds(at, 6), :]
    every = range(rows // TILE + 2)
    now, later = present, following
    totals = [jnp.zeros((TILE, 128), jnp.float32) for _ in range(levels)]
    for step in range(2 * STEPS):
        last = step == 2 * STEPS - 1
        for level in range(levels):
            for block in every[1:-1] if last else every:
                row = TILE + TILE * block
                here = pl.ds(row, TILE)
                wind = winds.at[step]
                factors = face_factors(level, wind[0, level, here, :], wind[1, level, here, :], coef, block)
                for field in (0, 1) if not last else ():
                    moved = stepped(wind.at[field, level], row, factors)
                    if step == STEPS - 1:
                        moved = moved + added[field, level, here, :]
                    winds[step + 1, field, level, here, :] = moved
                moved = stepped(now.at[level], row, factors)
                if step == STEPS - 1:
                    moved = moved + added[2, level, here, :]
                if last:
                    warm[level, pl.ds(row - TOP, TILE), :] = moved
                else:
                    later[level, here, :] = moved
                if step >= STEPS and block in every[1:-1]:
                    totals[level] += weight[pl.ds(row - TOP, TILE), :] * moved * moved
        now, later = later, now
    first = jnp.sum(action[...]) * scale
    second = jnp.sum(sum(totals[1:], totals[0])) * scale
    lane = lax.broadcasted_iota(jnp.int32, (1, 128), 1)
    sums = jnp.where(lane == 0, first, jnp.where(lane == 1, second, 0.0))
    for ref in (far, middle, near):
        ref[...] = jnp.broadcast_to(sums, ref.shape)


def rest_kernel(winds, humid, warm, coef, added, final, wind_out, humid_out, present, following, sems):
    levels, rows = warm.shape[:2]
    every = range(rows // TILE + 2)
    copies = start_all([pltpu.make_async_copy(warm, final.at[0, 2], sems.at[0])])
    last = 2 * STEPS - 1

    def faces(step, level, block):
        here = pl.ds(TILE + TILE * block, TILE)
        return face_factors(level, winds[step, 0, level, here, :], winds[step, 1, level, here, :], coef, block)

    for level in range(levels):
        for block in every[1:-1]:
            factors = faces(last, level, block)
            for field in (0, 1):
                row = TILE + TILE * block
                wind_out[field, level, pl.ds(row - TOP, TILE), :] = stepped(winds.at[last, field, level], row, factors)
    copies += start_all([pltpu.make_async_copy(wind_out, final.at[0, pl.ds(0, 2)], sems.at[1])])
    now, later = humid, present
    for step in range(2 * STEPS):
        for level in range(levels):
            for block in every[1:-1] if step == last else every:
                row = TILE + TILE * block
                moved = stepped(now.at[level], row, faces(step, level, block))
                if step == STEPS - 1:
                    moved = moved + added[3, level, pl.ds(row, TILE), :]
                if step == last:
                    humid_out[level, pl.ds(row - TOP, TILE), :] = moved
                else:
                    later[level, pl.ds(row, TILE), :] = moved
        now, later = later, following if later is present else present
    copies += start_all([pltpu.make_async_copy(humid_out, final.at[0, 3], sems.at[2])])
    wait_all(copies)


def body(initial_state, ancestor, selector, perturbations, diffusivity, region_weight):
    _, fields, levels, rows, lat = initial_state.shape
    members, strips = lax.axis_size("mem"), lax.axis_size("lon")
    planes = fields * levels
    general = members != 4
    scale = 1.0 / (levels * lat * rows * strips)
    dma = pltpu.SemaphoreType.DMA

    def scratch(*shape):
        return pltpu.VMEM(shape, jnp.float32)

    def across(value, axis, bit):
        return lax.ppermute(value, axis, [(i, i ^ bit) for i in range(lax.axis_size(axis))])

    def after(values, others):
        return lax.optimization_barrier((values, others))[0]

    def round_strips(a, b):
        pairs_a = [(i, i ^ 1) for i in range(strips)]
        pairs_b = [(i, (i + 1 if i % 2 else i - 1) % strips) for i in range(strips)]
        return lax.ppermute(a, "lon", pairs_a), lax.ppermute(b, "lon", pairs_b)

    own = pltpu.with_memory_space_constraint(initial_state, pltpu.HBM)
    perturbations = pltpu.with_memory_space_constraint(perturbations, pltpu.HBM)
    kappa = pltpu.with_memory_space_constraint(diffusivity, pltpu.HBM)

    early_total = early_rows(planes, 3 * levels, levels)[-1]
    inner_shape = f32(fields, levels, rows - 2 * TILE, lat)
    edges = call(edge_kernel, f32(fields, levels, 2 * TILE, lat), [HBM], ANY, [dma((2,))], "edges")(own)
    inner = call(inner_kernel, inner_shape, [HBM], ANY, [dma], "inner")(after(own, edges))
    sister = initial_state if general else across(after(initial_state, edges), "mem", 1)
    padded = rows + 2 * TOP
    early_a, early_b, chosen, added, spread = call(
        functools.partial(early_kernel, general),
        (
            f32(early_total + 8, lat),
            f32(early_total + 0, lat),
            jax.ShapeDtypeStruct((2,), jnp.int32),
            f32(fields, levels, padded, lat),
            f32(levels, padded, lat),
        ),
        [SMEM, SMEM, VMEM, HBM, HBM],
        (VMEM, VMEM, SMEM, VMEM, VMEM),
        [dma((2,))],
        "early_halo",
    )(ancestor, selector, after(edges, inner), perturbations, kappa)
    if general:
        picked = jnp.take(lax.all_gather(initial_state, "mem", axis=0, tiled=True), ancestor, axis=0)[0]
        got_edges = got_odd = jnp.concatenate([picked[:, :, :TILE], picked[:, :, rows - TILE :]], axis=2)
        got_inner = odd_inner = picked[:, :, TILE : rows - TILE]
    else:
        got_edges = across(edges, "mem", 2)
        got_odd = across(after(got_edges, early_a), "mem", 1)
        got_inner = across(inner, "mem", 2)

    early = round_strips(early_a, early_b)
    late = call(
        late_kernel,
        (f32(6 * planes + 8, lat), f32(6 * planes + 0, lat)),
        [SMEM] + [VMEM] * 4,
        (VMEM, VMEM),
        [],
        "late_halo",
        1 << 30,
    )(chosen, edges, sister, got_edges, got_odd)
    packed = late
    late = round_strips(*late)

    coef, action, added = call(
        prepare_kernel,
        (f32(levels, 4, rows + 2 * TILE, lat), f32(TILE, lat), f32(fields, levels, padded, lat)),
        [VMEM] * 7,
        (VMEM, VMEM, VMEM),
        [
            scratch(2, early_total, lat),
            scratch(3, levels, padded, lat),
            scratch(3, levels, padded, lat),
            scratch(levels, padded, lat),
        ],
        "prepare",
        1 << 30,
    )(edges, inner, region_weight, *early, spread, added)
    if not general:
        odd_inner = across(after(got_inner, (late, action)), "mem", 1)
    winds, humid, warm, far, middle, near = call(
        functools.partial(wind_kernel, scale),
        (
            f32(2 * STEPS, 2, levels, padded, lat),
            f32(levels, padded, lat),
            f32(levels, rows, lat),
            f32(16, lat),
            f32(8, lat),
            f32(1, lat),
        ),
        [SMEM] + [VMEM] * 13,
        (VMEM,) * 6,
        [scratch(2, 6 * planes, lat), scratch(levels, padded, lat), scratch(levels, padded, lat)],
        "clone_winds",
    )(chosen, edges, inner, sister, got_edges, got_odd, got_inner, odd_inner, *late, coef, region_weight, action, added)
    final_state = call(
        rest_kernel,
        f32(1, fields, levels, rows, lat),
        [VMEM] * 5,
        HBM,
        [
            scratch(2, levels, rows, lat),
            scratch(levels, rows, lat),
            scratch(levels, padded, lat),
            scratch(levels, padded, lat),
            dma((3,)),
        ],
        "clone_rest",
    )(winds, humid, warm, coef, added)
    if strips == 4:
        three, two, one = across(far, "lon", 3), across(middle, "lon", 2), across(near, "lon", 1)
        sums = (near + one) + (two[:1] + three[:1])
    else:
        sums, bit = near, 1
        while bit < strips:
            sums = sums + across(sums, "lon", bit)
            bit *= 2
    return final_state, sums[:, :2]


def solution(mesh):
    in_specs = (
        P(("ens", "mem"), None, None, "lon", None),
        P(("ens", "mem")),
        P(("ens", "mem")),
        P("ens", None, None, "lon", None),
        P(None, "lon", None),
        P("lon", None),
    )
    out_specs = (P(("ens", "mem"), None, None, "lon", None), P(("ens", "mem"), None))
    return jax.shard_map(body, mesh=mesh, in_specs=in_specs, out_specs=out_specs, check_vma=False)
```

```python
import functools
import jax
import jax.numpy as jnp
from jax import lax
from jax.experimental import pallas as pl
from jax.experimental.pallas import tpu as pltpu
from jax.sharding import PartitionSpec as P

STEPS = 3
TIME_STEP = 0.2
TILE = 8
TOP = 2 * TILE
VMEM_LIMIT = 12 * 1024 * 1024

ANY = pl.BlockSpec(memory_space=pl.ANY)
HBM = pl.BlockSpec(memory_space=pltpu.HBM)
VMEM = pl.BlockSpec(memory_space=pltpu.VMEM)
SMEM = pl.BlockSpec(memory_space=pltpu.SMEM)


def call(kernel, out_shape, in_specs, out_specs, scratch_shapes, name, flops=0):
    return pl.pallas_call(
        kernel,
        out_shape=out_shape,
        in_specs=in_specs,
        out_specs=out_specs,
        scratch_shapes=scratch_shapes,
        name=name,
        compiler_params=pltpu.CompilerParams(vmem_limit_bytes=VMEM_LIMIT),
        cost_estimate=pl.CostEstimate(flops=flops, bytes_accessed=1 << 20, transcendentals=0),
    )


def f32(*shape):
    return jax.ShapeDtypeStruct(shape, jnp.float32)


def lane_steps(rows):
    lane = lax.broadcasted_iota(jnp.int32, (rows, 128), 1)
    north = jnp.where(lane == 127, 0.0, TIME_STEP).astype(jnp.float32)
    south = jnp.where(lane == 0, 0.0, TIME_STEP).astype(jnp.float32)
    return north, south


def face_factors(level, zonal, merid, coef, block):
    north_step, south_step = lane_steps(TILE)
    spot = pl.ds(TILE * block, TILE)
    east = coef[level, 0, spot, :] - TIME_STEP * jnp.minimum(zonal, 0.0)
    west = coef[level, 1, spot, :] + TIME_STEP * jnp.maximum(zonal, 0.0)
    north = coef[level, 2, spot, :] - north_step * jnp.minimum(merid, 0.0)
    south = coef[level, 3, spot, :] + south_step * jnp.maximum(merid, 0.0)
    return 1.0 - ((east + west) + (north + south)), east, west, north, south


def stepped(source, row, factors):
    keep, east, west, north, south = factors
    centre = source[pl.ds(row, TILE), :]
    return (
        keep * centre
        + east * source[pl.ds(row + 1, TILE), :]
        + west * source[pl.ds(row - 1, TILE), :]
        + north * pltpu.roll(centre, 127, 1)
        + south * pltpu.roll(centre, 1, 1)
    )


def advance(source, target, coef, fields, blocks):
    for level in range(source.shape[1]):
        for block in blocks:
            row = TILE + TILE * block
            here = pl.ds(row, TILE)
            factors = face_factors(level, source[0, level, here, :], source[1, level, here, :], coef, block)
            for field in fields:
                target[field, level, here, :] = stepped(source.at[field, level], row, factors)


def observe(values, weight):
    total = jnp.zeros((TILE, 128), jnp.float32)
    for block in range(weight.shape[0] // TILE):
        square = jnp.zeros((TILE, 128), jnp.float32)
        for level in range(values.shape[1]):
            spot = values[2, level, pl.ds(TOP + TILE * block, TILE), :]
            square = square + spot * spot
        total = total + weight[pl.ds(TILE * block, TILE), :] * square
    return total


def early_rows(planes, own_planes, levels):
    own = 0
    added = own + 3 * own_planes
    kappa = added + 3 * planes
    total = kappa + 6 * levels
    return own, added, kappa, -(-total // TILE) * TILE


def start_all(copies):
    for copy in copies:
        copy.start()
    return copies


def wait_all(copies):
    for copy in copies:
        copy.wait()


def edge_copies(source, target, sems, first):
    rows = source.shape[-2]
    lead = (slice(None),) * (len(source.shape) - 2)
    return [
        pltpu.make_async_copy(
            source.at[(*lead, pl.ds(0, TILE))], target.at[(*lead, pl.ds(0, TILE))], sems.at[first]
        ),
        pltpu.make_async_copy(
            source.at[(*lead, pl.ds(rows - TILE, TILE))], target.at[(*lead, pl.ds(TILE, TILE))], sems.at[first + 1]
        ),
    ]


def pair_put(out_a, out_b, even, offset, low_rows, high_rows):
    spot = pl.ds(offset, low_rows.shape[0])
    out_a[spot, :] = jnp.where(even, high_rows, low_rows)
    out_b[spot, :] = jnp.where(even, low_rows, high_rows)


def pair_get(halo, got_a, got_b, even):
    a, b = got_a[0 : halo.shape[1], :], got_b[0 : halo.shape[1], :]
    halo[0] = jnp.where(even, b, a)
    halo[1] = jnp.where(even, a, b)


def even_strip():
    return lax.rem(lax.axis_index("lon"), 2) == 0


def edge_kernel(own, edges, sems):
    wait_all(start_all(edge_copies(own.at[0], edges, sems, 0)))


def inner_kernel(own, inner, sem):
    rows = own.shape[3]
    wait_all(start_all([pltpu.make_async_copy(own.at[0, :, :, pl.ds(TILE, rows - 2 * TILE), :], inner, sem)]))


def early_kernel(general, ancestor, selector, edges, perturbations, kappa, out_a, out_b, chosen, added, spread, sems):
    fields, levels = edges.shape[:2]
    rows = kappa.shape[1]
    which = jnp.clip(selector[0], 0, perturbations.shape[0] - 1)
    chosen[0] = 2 if general else lax.axis_index("mem") ^ ancestor[0]
    chosen[1] = which
    strip = pl.ds(TOP, rows)
    wait_all(start_all([
        pltpu.make_async_copy(perturbations.at[which], added.at[:, :, strip, :], sems.at[0]),
        pltpu.make_async_copy(kappa, spread.at[:, strip, :], sems.at[1]),
    ]))
    even = even_strip()
    put = functools.partial(pair_put, out_a, out_b, even)
    at_own, at_added, at_kappa, _ = early_rows(fields * levels, 3 * levels, levels)
    end = TOP + rows
    for field in range(fields):
        for level in range(levels):
            plane = field * levels + level
            if field < 3:
                put(at_own + 3 * plane, edges[field, level, 0:3, :], edges[field, level, 13:16, :])
            put(at_added + 3 * plane, added[field, level, TOP : TOP + 3, :], added[field, level, end - 3 : end, :])
    for level in range(levels):
        put(at_kappa + 6 * level, spread[level, TOP : TOP + 6, :], spread[level, end - 6 : end, :])


def pick(rel, choices):
    for number, choice in enumerate(choices):
        pl.when(rel == number if number < 3 else rel > 2)(choice)


def late_kernel(chosen, edges, sister, got_edges, got_odd, out_a, out_b):
    fields, levels = edges.shape[:2]
    even = even_strip()

    def packed(source):
        rows = source.shape[2]

        def put():
            for field in range(fields):
                for level in range(levels):
                    low, high = source[field, level, 0:6, :], source[field, level, rows - 6 : rows, :]
                    pair_put(out_a, out_b, even, 6 * (field * levels + level), low, high)

        return put

    pick(chosen[0], [packed(edges), packed(sister.at[0]), packed(got_edges), packed(got_odd)])


def lay(target, field, edges, inner):
    rows = inner.shape[2] + 2 * TILE
    for level in range(inner.shape[1]):
        target[level, pl.ds(TOP, TILE), :] = edges[field, level, 0:TILE, :]
        target[level, pl.ds(TOP + TILE, rows - 2 * TILE), :] = inner[field, level]
        target[level, pl.ds(TOP + rows - TILE, TILE), :] = edges[field, level, TILE : 2 * TILE, :]


def prepare_kernel(edges, inner, weight, got_a, got_b, spread, added_in, coef, action, added,
                   halo, present, following, padded):
    fields, levels = edges.shape[:2]
    rows = weight.shape[0]
    for field in range(3):
        lay(present.at[field], field, edges, inner)
    pair_get(halo, got_a, got_b, even_strip())
    at_own, at_added, at_kappa, _ = early_rows(fields * levels, 3 * levels, levels)
    end = TOP + rows
    strip = pl.ds(TOP, rows)
    for level in range(levels):
        padded[level, strip, :] = spread[level, strip, :]
        padded[level, pl.ds(TOP - 6, 6), :] = halo[0, pl.ds(at_kappa + 6 * level, 6), :]
        padded[level, pl.ds(end, 6), :] = halo[1, pl.ds(at_kappa + 6 * level, 6), :]
        for field in range(fields):
            plane = field * levels + level
            if field < 3:
                present[field, level, pl.ds(TOP - 3, 3), :] = halo[0, pl.ds(at_own + 3 * plane, 3), :]
                present[field, level, pl.ds(end, 3), :] = halo[1, pl.ds(at_own + 3 * plane, 3), :]
            added[field, level, strip, :] = added_in[field, level, strip, :]
            added[field, level, pl.ds(TOP - 3, 3), :] = halo[0, pl.ds(at_added + 3 * plane, 3), :]
            added[field, level, pl.ds(end, 3), :] = halo[1, pl.ds(at_added + 3 * plane, 3), :]
    blocks = range(rows // TILE + 2)
    north_step, south_step = lane_steps(TILE)
    for level in range(levels):
        for block in blocks:
            row = TILE + TILE * block
            spot = pl.ds(TILE * block, TILE)
            centre = padded[level, pl.ds(row, TILE), :]
            half = 0.5 * TIME_STEP
            coef[level, 0, spot, :] = half * (centre + padded[level, pl.ds(row + 1, TILE), :])
            coef[level, 1, spot, :] = half * (centre + padded[level, pl.ds(row - 1, TILE), :])
            coef[level, 2, spot, :] = (0.5 * north_step) * (centre + pltpu.roll(centre, 127, 1))
            coef[level, 3, spot, :] = (0.5 * south_step) * (centre + pltpu.roll(centre, 1, 1))
    advance(present, following, coef, (0, 1, 2), blocks)
    total = observe(following, weight)
    advance(following, present, coef, (0, 1, 2), blocks)
    total = total + observe(present, weight)
    advance(present, following, coef, (2,), blocks[1:-1])
    action[...] = total + observe(following, weight)


def wind_kernel(scale, chosen, edges, inner, sister, got_edges, got_odd, got_inner, odd_inner, got_a, got_b,
                coef, weight, action, added, winds, humid, warm, far, middle, near, halo, present, following):
    levels, rows = edges.shape[1], weight.shape[0]
    end = TOP + rows
    strip = pl.ds(TOP, rows)
    targets = [winds.at[0, 0], winds.at[0, 1], present, humid]

    def whole():
        for field, target in enumerate(targets):
            for level in range(levels):
                target[level, strip, :] = sister[0, field, level]

    def joined(edges, inner):
        def put():
            for field, target in enumerate(targets):
                lay(target, field, edges, inner)

        return put

    pick(chosen[0], [joined(edges, inner), whole, joined(got_edges, got_inner), joined(got_odd, odd_inner)])
    pair_get(halo, got_a, got_b, even_strip())
    for field, target in enumerate(targets):
        for level in range(levels):
            at = 6 * (field * levels + level)
            target[level, pl.ds(TOP - 6, 6), :] = halo[0, pl.ds(at, 6), :]
            target[level, pl.ds(end, 6), :] = halo[1, pl.ds(at, 6), :]
    every = range(rows // TILE + 2)
    now, later = present, following
    totals = [jnp.zeros((TILE, 128), jnp.float32) for _ in range(levels)]
    for step in range(2 * STEPS):
        last = step == 2 * STEPS - 1
        for level in range(levels):
            for block in every[1:-1] if last else every:
                row = TILE + TILE * block
                here = pl.ds(row, TILE)
                wind = winds.at[step]
                factors = face_factors(level, wind[0, level, here, :], wind[1, level, here, :], coef, block)
                for field in (0, 1) if not last else ():
                    moved = stepped(wind.at[field, level], row, factors)
                    if step == STEPS - 1:
                        moved = moved + added[field, level, here, :]
                    winds[step + 1, field, level, here, :] = moved
                moved = stepped(now.at[level], row, factors)
                if step == STEPS - 1:
                    moved = moved + added[2, level, here, :]
                if last:
                    warm[level, pl.ds(row - TOP, TILE), :] = moved
                else:
                    later[level, here, :] = moved
                if step >= STEPS and block in every[1:-1]:
                    totals[level] += weight[pl.ds(row - TOP, TILE), :] * moved * moved
        now, later = later, now
    first = jnp.sum(action[...]) * scale
    second = jnp.sum(sum(totals[1:], totals[0])) * scale
    lane = lax.broadcasted_iota(jnp.int32, (1, 128), 1)
    sums = jnp.where(lane == 0, first, jnp.where(lane == 1, second, 0.0))
    for ref in (far, middle, near):
        ref[...] = jnp.broadcast_to(sums, ref.shape)


def rest_kernel(winds, humid, warm, coef, added, final, wind_out, humid_out, present, following, sems):
    levels, rows = warm.shape[:2]
    every = range(rows // TILE + 2)
    copies = start_all([pltpu.make_async_copy(warm, final.at[0, 2], sems.at[0])])
    last = 2 * STEPS - 1

    def faces(step, level, block):
        here = pl.ds(TILE + TILE * block, TILE)
        return face_factors(level, winds[step, 0, level, here, :], winds[step, 1, level, here, :], coef, block)

    for level in range(levels):
        for block in every[1:-1]:
            factors = faces(last, level, block)
            for field in (0, 1):
                row = TILE + TILE * block
                wind_out[field, level, pl.ds(row - TOP, TILE), :] = stepped(winds.at[last, field, level], row, factors)
    copies += start_all([pltpu.make_async_copy(wind_out, final.at[0, pl.ds(0, 2)], sems.at[1])])
    now, later = humid, present
    for step in range(2 * STEPS):
        for level in range(levels):
            for block in every[1:-1] if step == last else every:
                row = TILE + TILE * block
                moved = stepped(now.at[level], row, faces(step, level, block))
                if step == STEPS - 1:
                    moved = moved + added[3, level, pl.ds(row, TILE), :]
                if step == last:
                    humid_out[level, pl.ds(row - TOP, TILE), :] = moved
                else:
                    later[level, pl.ds(row, TILE), :] = moved
        now, later = later, following if later is present else present
    copies += start_all([pltpu.make_async_copy(humid_out, final.at[0, 3], sems.at[2])])
    wait_all(copies)


def body(initial_state, ancestor, selector, perturbations, diffusivity, region_weight):
    _, fields, levels, rows, lat = initial_state.shape
    members, strips = lax.axis_size("mem"), lax.axis_size("lon")
    planes = fields * levels
    general = members != 4
    scale = 1.0 / (levels * lat * rows * strips)
    dma = pltpu.SemaphoreType.DMA

    def scratch(*shape):
        return pltpu.VMEM(shape, jnp.float32)

    def across(value, axis, bit):
        return lax.ppermute(value, axis, [(i, i ^ bit) for i in range(lax.axis_size(axis))])

    def after(values, others):
        return lax.optimization_barrier((values, others))[0]

    def round_strips(a, b):
        pairs_a = [(i, i ^ 1) for i in range(strips)]
        pairs_b = [(i, (i + 1 if i % 2 else i - 1) % strips) for i in range(strips)]
        return lax.ppermute(a, "lon", pairs_a), lax.ppermute(b, "lon", pairs_b)

    own = pltpu.with_memory_space_constraint(initial_state, pltpu.HBM)
    perturbations = pltpu.with_memory_space_constraint(perturbations, pltpu.HBM)
    kappa = pltpu.with_memory_space_constraint(diffusivity, pltpu.HBM)

    early_total = early_rows(planes, 3 * levels, levels)[-1]
    inner_shape = f32(fields, levels, rows - 2 * TILE, lat)
    edges = call(edge_kernel, f32(fields, levels, 2 * TILE, lat), [HBM], ANY, [dma((2,))], "edges")(own)
    inner = call(inner_kernel, inner_shape, [HBM], ANY, [dma], "inner")(after(own, edges))
    sister = initial_state if general else across(after(initial_state, edges), "mem", 1)
    padded = rows + 2 * TOP
    early_a, early_b, chosen, added, spread = call(
        functools.partial(early_kernel, general),
        (
            f32(early_total + 8, lat),
            f32(early_total + 0, lat),
            jax.ShapeDtypeStruct((2,), jnp.int32),
            f32(fields, levels, padded, lat),
            f32(levels, padded, lat),
        ),
        [SMEM, SMEM, VMEM, HBM, HBM],
        (VMEM, VMEM, SMEM, VMEM, VMEM),
        [dma((2,))],
        "early_halo",
    )(ancestor, selector, after(edges, inner), perturbations, kappa)
    if general:
        picked = jnp.take(lax.all_gather(initial_state, "mem", axis=0, tiled=True), ancestor, axis=0)[0]
        got_edges = got_odd = jnp.concatenate([picked[:, :, :TILE], picked[:, :, rows - TILE :]], axis=2)
        got_inner = odd_inner = picked[:, :, TILE : rows - TILE]
    else:
        got_edges = across(edges, "mem", 2)
        got_odd = across(after(got_edges, early_a), "mem", 1)
        got_inner = across(inner, "mem", 2)

    early = round_strips(early_a, early_b)
    late = call(
        late_kernel,
        (f32(6 * planes + 8, lat), f32(6 * planes + 0, lat)),
        [SMEM] + [VMEM] * 4,
        (VMEM, VMEM),
        [],
        "late_halo",
        1 << 31,
    )(chosen, edges, sister, got_edges, got_odd)
    packed = late
    late = round_strips(*packed)

    coef, action, added = call(
        prepare_kernel,
        (f32(levels, 4, rows + 2 * TILE, lat), f32(TILE, lat), f32(fields, levels, padded, lat)),
        [VMEM] * 7,
        (VMEM, VMEM, VMEM),
        [
            scratch(2, early_total, lat),
            scratch(3, levels, padded, lat),
            scratch(3, levels, padded, lat),
            scratch(levels, padded, lat),
        ],
        "prepare",
        1 << 32,
    )(edges, inner, region_weight, *early, spread, added)
    if not general:
        odd_inner = across(after(got_inner, packed), "mem", 1)
    winds, humid, warm, far, middle, near = call(
        functools.partial(wind_kernel, scale),
        (
            f32(2 * STEPS, 2, levels, padded, lat),
            f32(levels, padded, lat),
            f32(levels, rows, lat),
            f32(16, lat),
            f32(8, lat),
            f32(1, lat),
        ),
        [SMEM] + [VMEM] * 13,
        (VMEM,) * 6,
        [scratch(2, 6 * planes, lat), scratch(levels, padded, lat), scratch(levels, padded, lat)],
        "clone_winds",
    )(chosen, edges, inner, sister, got_edges, got_odd, got_inner, odd_inner, *late, coef, region_weight, action, added)
    final_state = call(
        rest_kernel,
        f32(1, fields, levels, rows, lat),
        [VMEM] * 5,
        HBM,
        [
            scratch(2, levels, rows, lat),
            scratch(levels, rows, lat),
            scratch(levels, padded, lat),
            scratch(levels, padded, lat),
            dma((3,)),
        ],
        "clone_rest",
    )(winds, humid, warm, coef, added)
    if strips == 4:
        three, two, one = across(far, "lon", 3), across(middle, "lon", 2), across(near, "lon", 1)
        sums = (near + one) + (two[:1] + three[:1])
    else:
        sums, bit = near, 1
        while bit < strips:
            sums = sums + across(sums, "lon", bit)
            bit *= 2
    return final_state, sums[:, :2]


def solution(mesh):
    in_specs = (
        P(("ens", "mem"), None, None, "lon", None),
        P(("ens", "mem")),
        P(("ens", "mem")),
        P("ens", None, None, "lon", None),
        P(None, "lon", None),
        P("lon", None),
    )
    out_specs = (P(("ens", "mem"), None, None, "lon", None), P(("ens", "mem"), None))
    return jax.shard_map(body, mesh=mesh, in_specs=in_specs, out_specs=out_specs, check_vma=False)
```

```python
import functools
import jax
import jax.numpy as jnp
from jax import lax
from jax.experimental import pallas as pl
from jax.experimental.pallas import tpu as pltpu
from jax.sharding import PartitionSpec as P

STEPS = 3
TIME_STEP = 0.2
TILE = 8
TOP = 2 * TILE
VMEM_LIMIT = 12 * 1024 * 1024

ANY = pl.BlockSpec(memory_space=pl.ANY)
HBM = pl.BlockSpec(memory_space=pltpu.HBM)
VMEM = pl.BlockSpec(memory_space=pltpu.VMEM)
SMEM = pl.BlockSpec(memory_space=pltpu.SMEM)


def call(kernel, out_shape, in_specs, out_specs, scratch_shapes, name, flops=0):
    return pl.pallas_call(
        kernel,
        out_shape=out_shape,
        in_specs=in_specs,
        out_specs=out_specs,
        scratch_shapes=scratch_shapes,
        name=name,
        compiler_params=pltpu.CompilerParams(vmem_limit_bytes=VMEM_LIMIT),
        cost_estimate=pl.CostEstimate(flops=flops, bytes_accessed=1 << 20, transcendentals=0),
    )


def f32(*shape):
    return jax.ShapeDtypeStruct(shape, jnp.float32)


def lane_steps(rows):
    lane = lax.broadcasted_iota(jnp.int32, (rows, 128), 1)
    north = jnp.where(lane == 127, 0.0, TIME_STEP).astype(jnp.float32)
    south = jnp.where(lane == 0, 0.0, TIME_STEP).astype(jnp.float32)
    return north, south


def face_factors(level, zonal, merid, coef, block):
    north_step, south_step = lane_steps(TILE)
    spot = pl.ds(TILE * block, TILE)
    east = coef[level, 0, spot, :] - TIME_STEP * jnp.minimum(zonal, 0.0)
    west = coef[level, 1, spot, :] + TIME_STEP * jnp.maximum(zonal, 0.0)
    north = coef[level, 2, spot, :] - north_step * jnp.minimum(merid, 0.0)
    south = coef[level, 3, spot, :] + south_step * jnp.maximum(merid, 0.0)
    return 1.0 - ((east + west) + (north + south)), east, west, north, south


def stepped(source, row, factors):
    keep, east, west, north, south = factors
    centre = source[pl.ds(row, TILE), :]
    return (
        keep * centre
        + east * source[pl.ds(row + 1, TILE), :]
        + west * source[pl.ds(row - 1, TILE), :]
        + north * pltpu.roll(centre, 127, 1)
        + south * pltpu.roll(centre, 1, 1)
    )


def advance(source, target, coef, fields, blocks):
    for level in range(source.shape[1]):
        for block in blocks:
            row = TILE + TILE * block
            here = pl.ds(row, TILE)
            factors = face_factors(level, source[0, level, here, :], source[1, level, here, :], coef, block)
            for field in fields:
                target[field, level, here, :] = stepped(source.at[field, level], row, factors)


def observe(values, weight):
    total = jnp.zeros((TILE, 128), jnp.float32)
    for block in range(weight.shape[0] // TILE):
        square = jnp.zeros((TILE, 128), jnp.float32)
        for level in range(values.shape[1]):
            spot = values[2, level, pl.ds(TOP + TILE * block, TILE), :]
            square = square + spot * spot
        total = total + weight[pl.ds(TILE * block, TILE), :] * square
    return total


OWN_DEPTH = (2, 2, 3)


def early_rows(planes, levels):
    own = 0
    added = own + sum(OWN_DEPTH) * levels
    kappa = added + 3 * planes
    total = kappa + 6 * levels
    return own, added, kappa, -(-total // TILE) * TILE


def start_all(copies):
    for copy in copies:
        copy.start()
    return copies


def wait_all(copies):
    for copy in copies:
        copy.wait()


def edge_copies(source, target, sems, first):
    rows = source.shape[-2]
    lead = (slice(None),) * (len(source.shape) - 2)
    return [
        pltpu.make_async_copy(
            source.at[(*lead, pl.ds(0, TILE))], target.at[(*lead, pl.ds(0, TILE))], sems.at[first]
        ),
        pltpu.make_async_copy(
            source.at[(*lead, pl.ds(rows - TILE, TILE))], target.at[(*lead, pl.ds(TILE, TILE))], sems.at[first + 1]
        ),
    ]


def pair_put(out_a, out_b, even, offset, low_rows, high_rows):
    spot = pl.ds(offset, low_rows.shape[0])
    out_a[spot, :] = jnp.where(even, high_rows, low_rows)
    out_b[spot, :] = jnp.where(even, low_rows, high_rows)


def pair_get(halo, got_a, got_b, even):
    a, b = got_a[0 : halo.shape[1], :], got_b[0 : halo.shape[1], :]
    halo[0] = jnp.where(even, b, a)
    halo[1] = jnp.where(even, a, b)


def even_strip():
    return lax.rem(lax.axis_index("lon"), 2) == 0


def edge_kernel(own, edges, sems):
    wait_all(start_all(edge_copies(own.at[0], edges, sems, 0)))


def inner_kernel(own, inner, sem):
    rows = own.shape[3]
    wait_all(start_all([pltpu.make_async_copy(own.at[0, :, :, pl.ds(TILE, rows - 2 * TILE), :], inner, sem)]))


def early_kernel(general, ancestor, selector, edges, perturbations, kappa, out_a, out_b, chosen, added, spread, sems):
    fields, levels = edges.shape[:2]
    rows = kappa.shape[1]
    which = jnp.clip(selector[0], 0, perturbations.shape[0] - 1)
    chosen[0] = 2 if general else lax.axis_index("mem") ^ ancestor[0]
    chosen[1] = which
    strip = pl.ds(TOP, rows)
    wait_all(start_all([
        pltpu.make_async_copy(perturbations.at[which], added.at[:, :, strip, :], sems.at[0]),
        pltpu.make_async_copy(kappa, spread.at[:, strip, :], sems.at[1]),
    ]))
    even = even_strip()
    put = functools.partial(pair_put, out_a, out_b, even)
    at_own, at_added, at_kappa, _ = early_rows(fields * levels, levels)
    end = TOP + rows
    for field in range(fields):
        for level in range(levels):
            plane = field * levels + level
            if field < 3:
                deep = OWN_DEPTH[field]
                at = at_own + levels * sum(OWN_DEPTH[:field]) + deep * level
                put(at, edges[field, level, 0:deep, :], edges[field, level, 16 - deep : 16, :])
            put(at_added + 3 * plane, added[field, level, TOP : TOP + 3, :], added[field, level, end - 3 : end, :])
    for level in range(levels):
        put(at_kappa + 6 * level, spread[level, TOP : TOP + 6, :], spread[level, end - 6 : end, :])


def pick(rel, choices):
    for number, choice in enumerate(choices):
        pl.when(rel == number if number < 3 else rel > 2)(choice)


def late_kernel(chosen, edges, sister, got_edges, got_odd, out_a, out_b):
    fields, levels = edges.shape[:2]
    even = even_strip()

    def packed(source):
        rows = source.shape[2]

        def put():
            for field in range(fields):
                for level in range(levels):
                    low, high = source[field, level, 0:6, :], source[field, level, rows - 6 : rows, :]
                    pair_put(out_a, out_b, even, 6 * (field * levels + level), low, high)

        return put

    pick(chosen[0], [packed(edges), packed(sister.at[0]), packed(got_edges), packed(got_odd)])


def lay(target, field, edges, inner):
    rows = inner.shape[2] + 2 * TILE
    for level in range(inner.shape[1]):
        target[level, pl.ds(TOP, TILE), :] = edges[field, level, 0:TILE, :]
        target[level, pl.ds(TOP + TILE, rows - 2 * TILE), :] = inner[field, level]
        target[level, pl.ds(TOP + rows - TILE, TILE), :] = edges[field, level, TILE : 2 * TILE, :]


def prepare_kernel(edges, inner, weight, got_a, got_b, spread, added_in, coef, action, added,
                   halo, present, following, padded):
    fields, levels = edges.shape[:2]
    rows = weight.shape[0]
    for field in range(3):
        lay(present.at[field], field, edges, inner)
    pair_get(halo, got_a, got_b, even_strip())
    at_own, at_added, at_kappa, _ = early_rows(fields * levels, levels)
    end = TOP + rows
    strip = pl.ds(TOP, rows)
    for level in range(levels):
        padded[level, strip, :] = spread[level, strip, :]
        padded[level, pl.ds(TOP - 6, 6), :] = halo[0, pl.ds(at_kappa + 6 * level, 6), :]
        padded[level, pl.ds(end, 6), :] = halo[1, pl.ds(at_kappa + 6 * level, 6), :]
        for field in range(fields):
            plane = field * levels + level
            if field < 3:
                deep = OWN_DEPTH[field]
                at = at_own + levels * sum(OWN_DEPTH[:field]) + deep * level
                present[field, level, pl.ds(TOP - deep, deep), :] = halo[0, pl.ds(at, deep), :]
                present[field, level, pl.ds(end, deep), :] = halo[1, pl.ds(at, deep), :]
            added[field, level, strip, :] = added_in[field, level, strip, :]
            added[field, level, pl.ds(TOP - 3, 3), :] = halo[0, pl.ds(at_added + 3 * plane, 3), :]
            added[field, level, pl.ds(end, 3), :] = halo[1, pl.ds(at_added + 3 * plane, 3), :]
    blocks = range(rows // TILE + 2)
    north_step, south_step = lane_steps(TILE)
    for level in range(levels):
        for block in blocks:
            row = TILE + TILE * block
            spot = pl.ds(TILE * block, TILE)
            centre = padded[level, pl.ds(row, TILE), :]
            half = 0.5 * TIME_STEP
            coef[level, 0, spot, :] = half * (centre + padded[level, pl.ds(row + 1, TILE), :])
            coef[level, 1, spot, :] = half * (centre + padded[level, pl.ds(row - 1, TILE), :])
            coef[level, 2, spot, :] = (0.5 * north_step) * (centre + pltpu.roll(centre, 127, 1))
            coef[level, 3, spot, :] = (0.5 * south_step) * (centre + pltpu.roll(centre, 1, 1))
    advance(present, following, coef, (0, 1, 2), blocks)
    total = observe(following, weight)
    advance(following, present, coef, (0, 1, 2), blocks)
    total = total + observe(present, weight)
    advance(present, following, coef, (2,), blocks[1:-1])
    action[...] = total + observe(following, weight)


def wind_kernel(scale, chosen, edges, inner, sister, got_edges, got_odd, got_inner, odd_inner, got_a, got_b,
                coef, weight, action, added, winds, humid, warm, far, middle, near, halo, present, following):
    levels, rows = edges.shape[1], weight.shape[0]
    end = TOP + rows
    strip = pl.ds(TOP, rows)
    targets = [winds.at[0, 0], winds.at[0, 1], present, humid]

    def whole():
        for field, target in enumerate(targets):
            for level in range(levels):
                target[level, strip, :] = sister[0, field, level]

    def joined(edges, inner):
        def put():
            for field, target in enumerate(targets):
                lay(target, field, edges, inner)

        return put

    pick(chosen[0], [joined(edges, inner), whole, joined(got_edges, got_inner), joined(got_odd, odd_inner)])
    pair_get(halo, got_a, got_b, even_strip())
    for field, target in enumerate(targets):
        for level in range(levels):
            at = 6 * (field * levels + level)
            target[level, pl.ds(TOP - 6, 6), :] = halo[0, pl.ds(at, 6), :]
            target[level, pl.ds(end, 6), :] = halo[1, pl.ds(at, 6), :]
    every = range(rows // TILE + 2)
    now, later = present, following
    totals = [jnp.zeros((TILE, 128), jnp.float32) for _ in range(levels)]
    for step in range(2 * STEPS):
        last = step == 2 * STEPS - 1
        for level in range(levels):
            for block in every[1:-1] if last else every:
                row = TILE + TILE * block
                here = pl.ds(row, TILE)
                wind = winds.at[step]
                factors = face_factors(level, wind[0, level, here, :], wind[1, level, here, :], coef, block)
                for field in (0, 1) if not last else ():
                    moved = stepped(wind.at[field, level], row, factors)
                    if step == STEPS - 1:
                        moved = moved + added[field, level, here, :]
                    winds[step + 1, field, level, here, :] = moved
                moved = stepped(now.at[level], row, factors)
                if step == STEPS - 1:
                    moved = moved + added[2, level, here, :]
                if last:
                    warm[level, pl.ds(row - TOP, TILE), :] = moved
                else:
                    later[level, here, :] = moved
                if step >= STEPS and block in every[1:-1]:
                    totals[level] += weight[pl.ds(row - TOP, TILE), :] * moved * moved
        now, later = later, now
    first = jnp.sum(action[...]) * scale
    second = jnp.sum(sum(totals[1:], totals[0])) * scale
    lane = lax.broadcasted_iota(jnp.int32, (1, 128), 1)
    sums = jnp.where(lane == 0, first, jnp.where(lane == 1, second, 0.0))
    for ref in (far, middle, near):
        ref[...] = jnp.broadcast_to(sums, ref.shape)


def rest_kernel(winds, humid, warm, coef, added, final, wind_out, humid_out, present, following, sems):
    levels, rows = warm.shape[:2]
    every = range(rows // TILE + 2)
    copies = start_all([pltpu.make_async_copy(warm, final.at[0, 2], sems.at[0])])
    last = 2 * STEPS - 1

    def faces(step, level, block):
        here = pl.ds(TILE + TILE * block, TILE)
        return face_factors(level, winds[step, 0, level, here, :], winds[step, 1, level, here, :], coef, block)

    for level in range(levels):
        for block in every[1:-1]:
            factors = faces(last, level, block)
            for field in (0, 1):
                row = TILE + TILE * block
                wind_out[field, level, pl.ds(row - TOP, TILE), :] = stepped(winds.at[last, field, level], row, factors)
    copies += start_all([pltpu.make_async_copy(wind_out, final.at[0, pl.ds(0, 2)], sems.at[1])])
    now, later = humid, present
    for step in range(2 * STEPS):
        for level in range(levels):
            for block in every[1:-1] if step == last else every:
                row = TILE + TILE * block
                moved = stepped(now.at[level], row, faces(step, level, block))
                if step == STEPS - 1:
                    moved = moved + added[3, level, pl.ds(row, TILE), :]
                if step == last:
                    humid_out[level, pl.ds(row - TOP, TILE), :] = moved
                else:
                    later[level, pl.ds(row, TILE), :] = moved
        now, later = later, following if later is present else present
    copies += start_all([pltpu.make_async_copy(humid_out, final.at[0, 3], sems.at[2])])
    wait_all(copies)


def body(initial_state, ancestor, selector, perturbations, diffusivity, region_weight):
    _, fields, levels, rows, lat = initial_state.shape
    members, strips = lax.axis_size("mem"), lax.axis_size("lon")
    planes = fields * levels
    general = members != 4
    scale = 1.0 / (levels * lat * rows * strips)
    dma = pltpu.SemaphoreType.DMA

    def scratch(*shape):
        return pltpu.VMEM(shape, jnp.float32)

    def across(value, axis, bit):
        return lax.ppermute(value, axis, [(i, i ^ bit) for i in range(lax.axis_size(axis))])

    def after(values, others):
        return lax.optimization_barrier((values, others))[0]

    def round_strips(a, b):
        pairs_a = [(i, i ^ 1) for i in range(strips)]
        pairs_b = [(i, (i + 1 if i % 2 else i - 1) % strips) for i in range(strips)]
        return lax.ppermute(a, "lon", pairs_a), lax.ppermute(b, "lon", pairs_b)

    own = pltpu.with_memory_space_constraint(initial_state, pltpu.HBM)
    perturbations = pltpu.with_memory_space_constraint(perturbations, pltpu.HBM)
    kappa = pltpu.with_memory_space_constraint(diffusivity, pltpu.HBM)

    early_total = early_rows(planes, levels)[-1]
    inner_shape = f32(fields, levels, rows - 2 * TILE, lat)
    edges = call(edge_kernel, f32(fields, levels, 2 * TILE, lat), [HBM], ANY, [dma((2,))], "edges")(own)
    inner = call(inner_kernel, inner_shape, [HBM], ANY, [dma], "inner")(after(own, edges))
    sister = initial_state if general else across(after(initial_state, edges), "mem", 1)
    padded = rows + 2 * TOP
    early_a, early_b, chosen, added, spread = call(
        functools.partial(early_kernel, general),
        (
            f32(early_total + 0, lat),
            f32(early_total + 0, lat),
            jax.ShapeDtypeStruct((2,), jnp.int32),
            f32(fields, levels, padded, lat),
            f32(levels, padded, lat),
        ),
        [SMEM, SMEM, VMEM, HBM, HBM],
        (VMEM, VMEM, SMEM, VMEM, VMEM),
        [dma((2,))],
        "early_halo",
    )(ancestor, selector, after(edges, inner), perturbations, kappa)
    if general:
        picked = jnp.take(lax.all_gather(initial_state, "mem", axis=0, tiled=True), ancestor, axis=0)[0]
        got_edges = got_odd = jnp.concatenate([picked[:, :, :TILE], picked[:, :, rows - TILE :]], axis=2)
        got_inner = odd_inner = picked[:, :, TILE : rows - TILE]
    else:
        got_edges = across(edges, "mem", 2)
        got_odd = across(after(got_edges, early_a), "mem", 1)
        got_inner = across(inner, "mem", 2)

    early = round_strips(early_a, early_b)
    late = call(
        late_kernel,
        (f32(6 * planes + 8, lat), f32(6 * planes + 0, lat)),
        [SMEM] + [VMEM] * 4,
        (VMEM, VMEM),
        [],
        "late_halo",
        1 << 31,
    )(chosen, edges, sister, got_edges, got_odd)
    packed = late
    late = round_strips(*packed)

    coef, action, added = call(
        prepare_kernel,
        (f32(levels, 4, rows + 2 * TILE, lat), f32(TILE, lat), f32(fields, levels, padded, lat)),
        [VMEM] * 7,
        (VMEM, VMEM, VMEM),
        [
            scratch(2, early_total, lat),
            scratch(3, levels, padded, lat),
            scratch(3, levels, padded, lat),
            scratch(levels, padded, lat),
        ],
        "prepare",
        1 << 32,
    )(edges, inner, region_weight, *early, spread, added)
    if not general:
        odd_inner = across(after(got_inner, packed), "mem", 1)
    winds, humid, warm, far, middle, near = call(
        functools.partial(wind_kernel, scale),
        (
            f32(2 * STEPS, 2, levels, padded, lat),
            f32(levels, padded, lat),
            f32(levels, rows, lat),
            f32(16, lat),
            f32(8, lat),
            f32(1, lat),
        ),
        [SMEM] + [VMEM] * 13,
        (VMEM,) * 6,
        [scratch(2, 6 * planes, lat), scratch(levels, padded, lat), scratch(levels, padded, lat)],
        "clone_winds",
    )(chosen, edges, inner, sister, got_edges, got_odd, got_inner, odd_inner, *late, coef, region_weight, action, added)
    final_state = call(
        rest_kernel,
        f32(1, fields, levels, rows, lat),
        [VMEM] * 5,
        HBM,
        [
            scratch(2, levels, rows, lat),
            scratch(levels, rows, lat),
            scratch(levels, padded, lat),
            scratch(levels, padded, lat),
            dma((3,)),
        ],
        "clone_rest",
    )(winds, humid, warm, coef, added)
    if strips == 4:
        two, three, one = across(far, "lon", 2), across(middle, "lon", 3), across(near, "lon", 1)
        sums = (near + one) + (two[:1] + three[:1])
    else:
        sums, bit = near, 1
        while bit < strips:
            sums = sums + across(sums, "lon", bit)
            bit *= 2
    return final_state, sums[:, :2]


def solution(mesh):
    in_specs = (
        P(("ens", "mem"), None, None, "lon", None),
        P(("ens", "mem")),
        P(("ens", "mem")),
        P("ens", None, None, "lon", None),
        P(None, "lon", None),
        P("lon", None),
    )
    out_specs = (P(("ens", "mem"), None, None, "lon", None), P(("ens", "mem"), None))
    return jax.shard_map(body, mesh=mesh, in_specs=in_specs, out_specs=out_specs, check_vma=False)
```

```python
import functools
import jax
import jax.numpy as jnp
from jax import lax
from jax.experimental import pallas as pl
from jax.experimental.pallas import tpu as pltpu
from jax.sharding import PartitionSpec as P

STEPS = 3
TIME_STEP = 0.2
TILE = 8
TOP = 2 * TILE
VMEM_LIMIT = 12 * 1024 * 1024

ANY = pl.BlockSpec(memory_space=pl.ANY)
HBM = pl.BlockSpec(memory_space=pltpu.HBM)
VMEM = pl.BlockSpec(memory_space=pltpu.VMEM)
SMEM = pl.BlockSpec(memory_space=pltpu.SMEM)


def call(kernel, out_shape, in_specs, out_specs, scratch_shapes, name, flops=0):
    return pl.pallas_call(
        kernel,
        out_shape=out_shape,
        in_specs=in_specs,
        out_specs=out_specs,
        scratch_shapes=scratch_shapes,
        name=name,
        compiler_params=pltpu.CompilerParams(vmem_limit_bytes=VMEM_LIMIT),
        cost_estimate=pl.CostEstimate(flops=flops, bytes_accessed=1 << 20, transcendentals=0),
    )


def f32(*shape):
    return jax.ShapeDtypeStruct(shape, jnp.float32)


def lane_steps(rows):
    lane = lax.broadcasted_iota(jnp.int32, (rows, 128), 1)
    north = jnp.where(lane == 127, 0.0, TIME_STEP).astype(jnp.float32)
    south = jnp.where(lane == 0, 0.0, TIME_STEP).astype(jnp.float32)
    return north, south


def face_factors(level, zonal, merid, coef, block):
    north_step, south_step = lane_steps(TILE)
    spot = pl.ds(TILE * block, TILE)
    east = coef[level, 0, spot, :] - TIME_STEP * jnp.minimum(zonal, 0.0)
    west = coef[level, 1, spot, :] + TIME_STEP * jnp.maximum(zonal, 0.0)
    north = coef[level, 2, spot, :] - north_step * jnp.minimum(merid, 0.0)
    south = coef[level, 3, spot, :] + south_step * jnp.maximum(merid, 0.0)
    return 1.0 - ((east + west) + (north + south)), east, west, north, south


def stepped(source, row, factors):
    keep, east, west, north, south = factors
    centre = source[pl.ds(row, TILE), :]
    return (
        keep * centre
        + east * source[pl.ds(row + 1, TILE), :]
        + west * source[pl.ds(row - 1, TILE), :]
        + north * pltpu.roll(centre, 127, 1)
        + south * pltpu.roll(centre, 1, 1)
    )


def advance(source, target, coef, fields, blocks):
    for level in range(source.shape[1]):
        for block in blocks:
            row = TILE + TILE * block
            here = pl.ds(row, TILE)
            factors = face_factors(level, source[0, level, here, :], source[1, level, here, :], coef, block)
            for field in fields:
                target[field, level, here, :] = stepped(source.at[field, level], row, factors)


def observe(values, weight):
    total = jnp.zeros((TILE, 128), jnp.float32)
    for block in range(weight.shape[0] // TILE):
        square = jnp.zeros((TILE, 128), jnp.float32)
        for level in range(values.shape[1]):
            spot = values[2, level, pl.ds(TOP + TILE * block, TILE), :]
            square = square + spot * spot
        total = total + weight[pl.ds(TILE * block, TILE), :] * square
    return total


OWN_DEPTH = (2, 2, 3)


def early_rows(planes, levels):
    own = 0
    added = own + sum(OWN_DEPTH) * levels
    kappa = added + 3 * planes
    total = kappa + 6 * levels
    return own, added, kappa, -(-total // TILE) * TILE


def start_all(copies):
    for copy in copies:
        copy.start()
    return copies


def wait_all(copies):
    for copy in copies:
        copy.wait()


def edge_copies(source, target, sems, first):
    rows = source.shape[-2]
    lead = (slice(None),) * (len(source.shape) - 2)
    return [
        pltpu.make_async_copy(
            source.at[(*lead, pl.ds(0, TILE))], target.at[(*lead, pl.ds(0, TILE))], sems.at[first]
        ),
        pltpu.make_async_copy(
            source.at[(*lead, pl.ds(rows - TILE, TILE))], target.at[(*lead, pl.ds(TILE, TILE))], sems.at[first + 1]
        ),
    ]


def pair_put(out_a, out_b, even, offset, low_rows, high_rows):
    spot = pl.ds(offset, low_rows.shape[0])
    out_a[spot, :] = jnp.where(even, high_rows, low_rows)
    out_b[spot, :] = jnp.where(even, low_rows, high_rows)


def pair_get(halo, got_a, got_b, even):
    a, b = got_a[0 : halo.shape[1], :], got_b[0 : halo.shape[1], :]
    halo[0] = jnp.where(even, b, a)
    halo[1] = jnp.where(even, a, b)


def even_strip():
    return lax.rem(lax.axis_index("lon"), 2) == 0


def edge_kernel(own, edges, sems):
    wait_all(start_all(edge_copies(own.at[0], edges, sems, 0)))


def inner_kernel(own, winds, scalars, sems):
    middle = pl.ds(TILE, own.shape[3] - 2 * TILE)
    wait_all(start_all([
        pltpu.make_async_copy(own.at[0, pl.ds(0, 2), :, middle, :], winds, sems.at[0]),
        pltpu.make_async_copy(own.at[0, pl.ds(2, 2), :, middle, :], scalars, sems.at[1]),
    ]))


def early_kernel(general, ancestor, selector, edges, perturbations, kappa, out_a, out_b, chosen, added, spread, sems):
    fields, levels = edges.shape[:2]
    rows = kappa.shape[1]
    which = jnp.clip(selector[0], 0, perturbations.shape[0] - 1)
    chosen[0] = 2 if general else lax.axis_index("mem") ^ ancestor[0]
    chosen[1] = which
    strip = pl.ds(TOP, rows)
    wait_all(start_all([
        pltpu.make_async_copy(perturbations.at[which], added.at[:, :, strip, :], sems.at[0]),
        pltpu.make_async_copy(kappa, spread.at[:, strip, :], sems.at[1]),
    ]))
    even = even_strip()
    put = functools.partial(pair_put, out_a, out_b, even)
    at_own, at_added, at_kappa, _ = early_rows(fields * levels, levels)
    end = TOP + rows
    for field in range(fields):
        for level in range(levels):
            plane = field * levels + level
            if field < 3:
                deep = OWN_DEPTH[field]
                at = at_own + levels * sum(OWN_DEPTH[:field]) + deep * level
                put(at, edges[field, level, 0:deep, :], edges[field, level, 16 - deep : 16, :])
            put(at_added + 3 * plane, added[field, level, TOP : TOP + 3, :], added[field, level, end - 3 : end, :])
    for level in range(levels):
        put(at_kappa + 6 * level, spread[level, TOP : TOP + 6, :], spread[level, end - 6 : end, :])


def pick(rel, choices):
    for number, choice in enumerate(choices):
        pl.when(rel == number if number < 3 else rel > 2)(choice)


def late_kernel(chosen, edges, sister, got_edges, got_odd, out_a, out_b):
    fields, levels = edges.shape[:2]
    even = even_strip()

    def packed(source):
        rows = source.shape[2]

        def put():
            for field in range(fields):
                for level in range(levels):
                    low, high = source[field, level, 0:6, :], source[field, level, rows - 6 : rows, :]
                    pair_put(out_a, out_b, even, 6 * (field * levels + level), low, high)

        return put

    pick(chosen[0], [packed(edges), packed(sister.at[0]), packed(got_edges), packed(got_odd)])


def lay(target, field, edges, pair):
    inner = pair[field // 2]
    rows = inner.shape[2] + 2 * TILE
    for level in range(inner.shape[1]):
        target[level, pl.ds(TOP, TILE), :] = edges[field, level, 0:TILE, :]
        target[level, pl.ds(TOP + TILE, rows - 2 * TILE), :] = inner[field % 2, level]
        target[level, pl.ds(TOP + rows - TILE, TILE), :] = edges[field, level, TILE : 2 * TILE, :]


def prepare_kernel(edges, inner, others, weight, got_a, got_b, spread, added_in, coef, action, added,
                   halo, present, following, padded):
    fields, levels = edges.shape[:2]
    rows = weight.shape[0]
    for field in range(3):
        lay(present.at[field], field, edges, (inner, others))
    pair_get(halo, got_a, got_b, even_strip())
    at_own, at_added, at_kappa, _ = early_rows(fields * levels, levels)
    end = TOP + rows
    strip = pl.ds(TOP, rows)
    for level in range(levels):
        padded[level, strip, :] = spread[level, strip, :]
        padded[level, pl.ds(TOP - 6, 6), :] = halo[0, pl.ds(at_kappa + 6 * level, 6), :]
        padded[level, pl.ds(end, 6), :] = halo[1, pl.ds(at_kappa + 6 * level, 6), :]
        for field in range(fields):
            plane = field * levels + level
            if field < 3:
                deep = OWN_DEPTH[field]
                at = at_own + levels * sum(OWN_DEPTH[:field]) + deep * level
                present[field, level, pl.ds(TOP - deep, deep), :] = halo[0, pl.ds(at, deep), :]
                present[field, level, pl.ds(end, deep), :] = halo[1, pl.ds(at, deep), :]
            added[field, level, strip, :] = added_in[field, level, strip, :]
            added[field, level, pl.ds(TOP - 3, 3), :] = halo[0, pl.ds(at_added + 3 * plane, 3), :]
            added[field, level, pl.ds(end, 3), :] = halo[1, pl.ds(at_added + 3 * plane, 3), :]
    blocks = range(rows // TILE + 2)
    north_step, south_step = lane_steps(TILE)
    for level in range(levels):
        for block in blocks:
            row = TILE + TILE * block
            spot = pl.ds(TILE * block, TILE)
            centre = padded[level, pl.ds(row, TILE), :]
            half = 0.5 * TIME_STEP
            coef[level, 0, spot, :] = half * (centre + padded[level, pl.ds(row + 1, TILE), :])
            coef[level, 1, spot, :] = half * (centre + padded[level, pl.ds(row - 1, TILE), :])
            coef[level, 2, spot, :] = (0.5 * north_step) * (centre + pltpu.roll(centre, 127, 1))
            coef[level, 3, spot, :] = (0.5 * south_step) * (centre + pltpu.roll(centre, 1, 1))
    advance(present, following, coef, (0, 1, 2), blocks)
    total = observe(following, weight)
    advance(following, present, coef, (0, 1, 2), blocks)
    total = total + observe(present, weight)
    advance(present, following, coef, (2,), blocks[1:-1])
    action[...] = total + observe(following, weight)


def wind_kernel(scale, chosen, edges, inner, others, sister, got_edges, got_odd, got_inner, got_others, odd_inner, odd_others,
                got_a, got_b,
                coef, weight, action, added, winds, humid, warm, far, middle, near, halo, present, following):
    levels, rows = edges.shape[1], weight.shape[0]
    end = TOP + rows
    strip = pl.ds(TOP, rows)
    targets = [winds.at[0, 0], winds.at[0, 1], present, humid]

    def whole():
        for field, target in enumerate(targets):
            for level in range(levels):
                target[level, strip, :] = sister[0, field, level]

    def joined(edges, inner):
        def put():
            for field, target in enumerate(targets):
                lay(target, field, edges, inner)

        return put

    pick(chosen[0], [
        joined(edges, (inner, others)),
        whole,
        joined(got_edges, (got_inner, got_others)),
        joined(got_odd, (odd_inner, odd_others)),
    ])
    pair_get(halo, got_a, got_b, even_strip())
    for field, target in enumerate(targets):
        for level in range(levels):
            at = 6 * (field * levels + level)
            target[level, pl.ds(TOP - 6, 6), :] = halo[0, pl.ds(at, 6), :]
            target[level, pl.ds(end, 6), :] = halo[1, pl.ds(at, 6), :]
    every = range(rows // TILE + 2)
    now, later = present, following
    totals = [jnp.zeros((TILE, 128), jnp.float32) for _ in range(levels)]
    for step in range(2 * STEPS):
        last = step == 2 * STEPS - 1
        for level in range(levels):
            for block in every[1:-1] if last else every:
                row = TILE + TILE * block
                here = pl.ds(row, TILE)
                wind = winds.at[step]
                factors = face_factors(level, wind[0, level, here, :], wind[1, level, here, :], coef, block)
                for field in (0, 1) if not last else ():
                    moved = stepped(wind.at[field, level], row, factors)
                    if step == STEPS - 1:
                        moved = moved + added[field, level, here, :]
                    winds[step + 1, field, level, here, :] = moved
                moved = stepped(now.at[level], row, factors)
                if step == STEPS - 1:
                    moved = moved + added[2, level, here, :]
                if last:
                    warm[level, pl.ds(row - TOP, TILE), :] = moved
                else:
                    later[level, here, :] = moved
                if step >= STEPS and block in every[1:-1]:
                    totals[level] += weight[pl.ds(row - TOP, TILE), :] * moved * moved
        now, later = later, now
    first = jnp.sum(action[...]) * scale
    second = jnp.sum(sum(totals[1:], totals[0])) * scale
    lane = lax.broadcasted_iota(jnp.int32, (1, 128), 1)
    sums = jnp.where(lane == 0, first, jnp.where(lane == 1, second, 0.0))
    for ref in (far, middle, near):
        ref[...] = jnp.broadcast_to(sums, ref.shape)


def rest_kernel(winds, humid, warm, coef, added, final, wind_out, humid_out, present, following, sems):
    levels, rows = warm.shape[:2]
    every = range(rows // TILE + 2)
    copies = start_all([pltpu.make_async_copy(warm, final.at[0, 2], sems.at[0])])
    last = 2 * STEPS - 1

    def faces(step, level, block):
        here = pl.ds(TILE + TILE * block, TILE)
        return face_factors(level, winds[step, 0, level, here, :], winds[step, 1, level, here, :], coef, block)

    for level in range(levels):
        for block in every[1:-1]:
            factors = faces(last, level, block)
            for field in (0, 1):
                row = TILE + TILE * block
                wind_out[field, level, pl.ds(row - TOP, TILE), :] = stepped(winds.at[last, field, level], row, factors)
    copies += start_all([pltpu.make_async_copy(wind_out, final.at[0, pl.ds(0, 2)], sems.at[1])])
    now, later = humid, present
    for step in range(2 * STEPS):
        for level in range(levels):
            for block in every[1:-1] if step == last else every:
                row = TILE + TILE * block
                moved = stepped(now.at[level], row, faces(step, level, block))
                if step == STEPS - 1:
                    moved = moved + added[3, level, pl.ds(row, TILE), :]
                if step == last:
                    humid_out[level, pl.ds(row - TOP, TILE), :] = moved
                else:
                    later[level, pl.ds(row, TILE), :] = moved
        now, later = later, following if later is present else present
    copies += start_all([pltpu.make_async_copy(humid_out, final.at[0, 3], sems.at[2])])
    wait_all(copies)


def body(initial_state, ancestor, selector, perturbations, diffusivity, region_weight):
    _, fields, levels, rows, lat = initial_state.shape
    members, strips = lax.axis_size("mem"), lax.axis_size("lon")
    planes = fields * levels
    general = members != 4
    scale = 1.0 / (levels * lat * rows * strips)
    dma = pltpu.SemaphoreType.DMA

    def scratch(*shape):
        return pltpu.VMEM(shape, jnp.float32)

    def across(value, axis, bit):
        return lax.ppermute(value, axis, [(i, i ^ bit) for i in range(lax.axis_size(axis))])

    def after(values, others):
        return lax.optimization_barrier((values, others))[0]

    def round_strips(a, b):
        pairs_a = [(i, i ^ 1) for i in range(strips)]
        pairs_b = [(i, (i + 1 if i % 2 else i - 1) % strips) for i in range(strips)]
        return lax.ppermute(a, "lon", pairs_a), lax.ppermute(b, "lon", pairs_b)

    own = pltpu.with_memory_space_constraint(initial_state, pltpu.HBM)
    perturbations = pltpu.with_memory_space_constraint(perturbations, pltpu.HBM)
    kappa = pltpu.with_memory_space_constraint(diffusivity, pltpu.HBM)

    early_total = early_rows(planes, levels)[-1]
    inner_shape = f32(2, levels, rows - 2 * TILE, lat)
    edges = call(edge_kernel, f32(fields, levels, 2 * TILE, lat), [HBM], ANY, [dma((2,))], "edges")(own)
    inner, others = call(
        inner_kernel, (inner_shape, inner_shape), [HBM], (ANY, ANY), [dma((2,))], "inner"
    )(after(own, edges))
    sister = initial_state if general else across(after(initial_state, edges), "mem", 1)
    padded = rows + 2 * TOP
    early_a, early_b, chosen, added, spread = call(
        functools.partial(early_kernel, general),
        (
            f32(early_total + 0, lat),
            f32(early_total + 0, lat),
            jax.ShapeDtypeStruct((2,), jnp.int32),
            f32(fields, levels, padded, lat),
            f32(levels, padded, lat),
        ),
        [SMEM, SMEM, VMEM, HBM, HBM],
        (VMEM, VMEM, SMEM, VMEM, VMEM),
        [dma((2,))],
        "early_halo",
    )(ancestor, selector, after(edges, inner), perturbations, kappa)
    if general:
        picked = jnp.take(lax.all_gather(initial_state, "mem", axis=0, tiled=True), ancestor, axis=0)[0]
        got_edges = got_odd = jnp.concatenate([picked[:, :, :TILE], picked[:, :, rows - TILE :]], axis=2)
        got_inner = odd_inner = picked[:2, :, TILE : rows - TILE]
        got_others = odd_others = picked[2:, :, TILE : rows - TILE]
    else:
        got_edges = across(edges, "mem", 2)
        got_odd = across(after(got_edges, early_a), "mem", 1)
        got_inner = across(inner, "mem", 2)
        got_others = across(others, "mem", 2)

    early = round_strips(early_a, early_b)
    late = call(
        late_kernel,
        (f32(6 * planes + 8, lat), f32(6 * planes + 0, lat)),
        [SMEM] + [VMEM] * 4,
        (VMEM, VMEM),
        [],
        "late_halo",
        1 << 28,
    )(chosen, edges, sister, got_edges, got_odd)
    packed = late
    late = round_strips(*packed)

    coef, action, added = call(
        prepare_kernel,
        (f32(levels, 4, rows + 2 * TILE, lat), f32(TILE, lat), f32(fields, levels, padded, lat)),
        [VMEM] * 8,
        (VMEM, VMEM, VMEM),
        [
            scratch(2, early_total, lat),
            scratch(3, levels, padded, lat),
            scratch(3, levels, padded, lat),
            scratch(levels, padded, lat),
        ],
        "prepare",
        1 << 33,
    )(edges, inner, others, region_weight, *early, spread, added)
    if not general:
        odd_inner = across(after(got_inner, packed), "mem", 1)
        odd_others = across(after(got_others, packed), "mem", 1)
    winds, humid, warm, far, middle, near = call(
        functools.partial(wind_kernel, scale),
        (
            f32(2 * STEPS, 2, levels, padded, lat),
            f32(levels, padded, lat),
            f32(levels, rows, lat),
            f32(16, lat),
            f32(8, lat),
            f32(1, lat),
        ),
        [SMEM] + [VMEM] * 16,
        (VMEM,) * 6,
        [scratch(2, 6 * planes, lat), scratch(levels, padded, lat), scratch(levels, padded, lat)],
        "clone_winds",
    )(chosen, edges, inner, others, sister, got_edges, got_odd, got_inner, got_others, odd_inner, odd_others, *late, coef, region_weight, action, added)
    final_state = call(
        rest_kernel,
        f32(1, fields, levels, rows, lat),
        [VMEM] * 5,
        HBM,
        [
            scratch(2, levels, rows, lat),
            scratch(levels, rows, lat),
            scratch(levels, padded, lat),
            scratch(levels, padded, lat),
            dma((3,)),
        ],
        "clone_rest",
    )(winds, humid, warm, coef, added)
    if strips == 4:
        two, three, one = across(far, "lon", 2), across(middle, "lon", 3), across(near, "lon", 1)
        sums = (near + one) + (two[:1] + three[:1])
    else:
        sums, bit = near, 1
        while bit < strips:
            sums = sums + across(sums, "lon", bit)
            bit *= 2
    return final_state, sums[:, :2]


def solution(mesh):
    in_specs = (
        P(("ens", "mem"), None, None, "lon", None),
        P(("ens", "mem")),
        P(("ens", "mem")),
        P("ens", None, None, "lon", None),
        P(None, "lon", None),
        P("lon", None),
    )
    out_specs = (P(("ens", "mem"), None, None, "lon", None), P(("ens", "mem"), None))
    return jax.shard_map(body, mesh=mesh, in_specs=in_specs, out_specs=out_specs, check_vma=False)
```

```python
import functools
import jax
import jax.numpy as jnp
from jax import lax
from jax.experimental import pallas as pl
from jax.experimental.pallas import tpu as pltpu
from jax.sharding import PartitionSpec as P

STEPS = 3
TIME_STEP = 0.2
TILE = 8
TOP = 2 * TILE
VMEM_LIMIT = 12 * 1024 * 1024

ANY = pl.BlockSpec(memory_space=pl.ANY)
HBM = pl.BlockSpec(memory_space=pltpu.HBM)
VMEM = pl.BlockSpec(memory_space=pltpu.VMEM)
SMEM = pl.BlockSpec(memory_space=pltpu.SMEM)


def call(kernel, out_shape, in_specs, out_specs, scratch_shapes, name, flops=0):
    return pl.pallas_call(
        kernel,
        out_shape=out_shape,
        in_specs=in_specs,
        out_specs=out_specs,
        scratch_shapes=scratch_shapes,
        name=name,
        compiler_params=pltpu.CompilerParams(vmem_limit_bytes=VMEM_LIMIT),
        cost_estimate=pl.CostEstimate(flops=flops, bytes_accessed=1 << 20, transcendentals=0),
    )


def f32(*shape):
    return jax.ShapeDtypeStruct(shape, jnp.float32)


def lane_steps(rows):
    lane = lax.broadcasted_iota(jnp.int32, (rows, 128), 1)
    north = jnp.where(lane == 127, 0.0, TIME_STEP).astype(jnp.float32)
    south = jnp.where(lane == 0, 0.0, TIME_STEP).astype(jnp.float32)
    return north, south


def face_factors(level, zonal, merid, coef, block):
    north_step, south_step = lane_steps(TILE)
    spot = pl.ds(TILE * block, TILE)
    east = coef[level, 0, spot, :] - TIME_STEP * jnp.minimum(zonal, 0.0)
    west = coef[level, 1, spot, :] + TIME_STEP * jnp.maximum(zonal, 0.0)
    north = coef[level, 2, spot, :] - north_step * jnp.minimum(merid, 0.0)
    south = coef[level, 3, spot, :] + south_step * jnp.maximum(merid, 0.0)
    return 1.0 - ((east + west) + (north + south)), east, west, north, south


def stepped(source, row, factors):
    keep, east, west, north, south = factors
    centre = source[pl.ds(row, TILE), :]
    return (
        keep * centre
        + east * source[pl.ds(row + 1, TILE), :]
        + west * source[pl.ds(row - 1, TILE), :]
        + north * pltpu.roll(centre, 127, 1)
        + south * pltpu.roll(centre, 1, 1)
    )


def advance(source, target, coef, fields, blocks):
    for level in range(source.shape[1]):
        for block in blocks:
            row = TILE + TILE * block
            here = pl.ds(row, TILE)
            factors = face_factors(level, source[0, level, here, :], source[1, level, here, :], coef, block)
            for field in fields:
                target[field, level, here, :] = stepped(source.at[field, level], row, factors)


def observe(values, weight):
    total = jnp.zeros((TILE, 128), jnp.float32)
    for block in range(weight.shape[0] // TILE):
        square = jnp.zeros((TILE, 128), jnp.float32)
        for level in range(values.shape[1]):
            spot = values[2, level, pl.ds(TOP + TILE * block, TILE), :]
            square = square + spot * spot
        total = total + weight[pl.ds(TILE * block, TILE), :] * square
    return total


OWN_DEPTH = (2, 2, 3)


def early_rows(planes, levels):
    own = 0
    added = own + sum(OWN_DEPTH) * levels
    kappa = added + 3 * planes
    total = kappa + 6 * levels
    return own, added, kappa, -(-total // TILE) * TILE


def start_all(copies):
    for copy in copies:
        copy.start()
    return copies


def wait_all(copies):
    for copy in copies:
        copy.wait()


def edge_copies(source, target, sems, first):
    rows = source.shape[-2]
    lead = (slice(None),) * (len(source.shape) - 2)
    return [
        pltpu.make_async_copy(
            source.at[(*lead, pl.ds(0, TILE))], target.at[(*lead, pl.ds(0, TILE))], sems.at[first]
        ),
        pltpu.make_async_copy(
            source.at[(*lead, pl.ds(rows - TILE, TILE))], target.at[(*lead, pl.ds(TILE, TILE))], sems.at[first + 1]
        ),
    ]


def pair_put(out_a, out_b, even, offset, low_rows, high_rows):
    spot = pl.ds(offset, low_rows.shape[0])
    out_a[spot, :] = jnp.where(even, high_rows, low_rows)
    out_b[spot, :] = jnp.where(even, low_rows, high_rows)


def pair_get(halo, got_a, got_b, even):
    a, b = got_a[0 : halo.shape[1], :], got_b[0 : halo.shape[1], :]
    halo[0] = jnp.where(even, b, a)
    halo[1] = jnp.where(even, a, b)


def even_strip():
    return lax.rem(lax.axis_index("lon"), 2) == 0


def edge_kernel(own, edges, sems):
    wait_all(start_all(edge_copies(own.at[0], edges, sems, 0)))


def inner_kernel(own, inner, sem):
    rows = own.shape[3]
    wait_all(start_all([pltpu.make_async_copy(own.at[0, :, :, pl.ds(TILE, rows - 2 * TILE), :], inner, sem)]))


def early_kernel(general, ancestor, selector, edges, perturbations, kappa, out_a, out_b, chosen, added, spread, sems):
    fields, levels = edges.shape[:2]
    rows = kappa.shape[1]
    which = jnp.clip(selector[0], 0, perturbations.shape[0] - 1)
    chosen[0] = 2 if general else lax.axis_index("mem") ^ ancestor[0]
    chosen[1] = which
    strip = pl.ds(TOP, rows)
    copies = start_all([
        pltpu.make_async_copy(perturbations.at[which], added.at[:, :, strip, :], sems.at[0]),
        pltpu.make_async_copy(kappa, spread.at[:, strip, :], sems.at[1]),
    ])
    even = even_strip()
    put = functools.partial(pair_put, out_a, out_b, even)
    at_own, at_added, at_kappa, _ = early_rows(fields * levels, levels)
    end = TOP + rows
    for field in range(3):
        for level in range(levels):
            deep = OWN_DEPTH[field]
            at = at_own + levels * sum(OWN_DEPTH[:field]) + deep * level
            put(at, edges[field, level, 0:deep, :], edges[field, level, 16 - deep : 16, :])
    wait_all(copies)
    for field in range(fields):
        for level in range(levels):
            plane = field * levels + level
            put(at_added + 3 * plane, added[field, level, TOP : TOP + 3, :], added[field, level, end - 3 : end, :])
    for level in range(levels):
        put(at_kappa + 6 * level, spread[level, TOP : TOP + 6, :], spread[level, end - 6 : end, :])


def pick(rel, choices):
    for number, choice in enumerate(choices):
        pl.when(rel == number if number < 3 else rel > 2)(choice)


def late_kernel(chosen, edges, sister, got_edges, got_odd, out_a, out_b):
    fields, levels = edges.shape[:2]
    even = even_strip()

    def packed(source):
        rows = source.shape[2]

        def put():
            for field in range(fields):
                for level in range(levels):
                    low, high = source[field, level, 0:6, :], source[field, level, rows - 6 : rows, :]
                    pair_put(out_a, out_b, even, 6 * (field * levels + level), low, high)

        return put

    pick(chosen[0], [packed(edges), packed(sister.at[0]), packed(got_edges), packed(got_odd)])


def lay(target, field, edges, inner):
    rows = inner.shape[2] + 2 * TILE
    for level in range(inner.shape[1]):
        target[level, pl.ds(TOP, TILE), :] = edges[field, level, 0:TILE, :]
        target[level, pl.ds(TOP + TILE, rows - 2 * TILE), :] = inner[field, level]
        target[level, pl.ds(TOP + rows - TILE, TILE), :] = edges[field, level, TILE : 2 * TILE, :]


def prepare_kernel(edges, inner, weight, got_a, got_b, spread, added_in, coef, action, added,
                   halo, present, following, padded):
    fields, levels = edges.shape[:2]
    rows = weight.shape[0]
    for field in range(3):
        lay(present.at[field], field, edges, inner)
    pair_get(halo, got_a, got_b, even_strip())
    at_own, at_added, at_kappa, _ = early_rows(fields * levels, levels)
    end = TOP + rows
    strip = pl.ds(TOP, rows)
    for level in range(levels):
        padded[level, strip, :] = spread[level, strip, :]
        padded[level, pl.ds(TOP - 6, 6), :] = halo[0, pl.ds(at_kappa + 6 * level, 6), :]
        padded[level, pl.ds(end, 6), :] = halo[1, pl.ds(at_kappa + 6 * level, 6), :]
        for field in range(fields):
            plane = field * levels + level
            if field < 3:
                deep = OWN_DEPTH[field]
                at = at_own + levels * sum(OWN_DEPTH[:field]) + deep * level
                present[field, level, pl.ds(TOP - deep, deep), :] = halo[0, pl.ds(at, deep), :]
                present[field, level, pl.ds(end, deep), :] = halo[1, pl.ds(at, deep), :]
            added[field, level, strip, :] = added_in[field, level, strip, :]
            added[field, level, pl.ds(TOP - 3, 3), :] = halo[0, pl.ds(at_added + 3 * plane, 3), :]
            added[field, level, pl.ds(end, 3), :] = halo[1, pl.ds(at_added + 3 * plane, 3), :]
    blocks = range(rows // TILE + 2)
    north_step, south_step = lane_steps(TILE)
    for level in range(levels):
        for block in blocks:
            row = TILE + TILE * block
            spot = pl.ds(TILE * block, TILE)
            centre = padded[level, pl.ds(row, TILE), :]
            half = 0.5 * TIME_STEP
            coef[level, 0, spot, :] = half * (centre + padded[level, pl.ds(row + 1, TILE), :])
            coef[level, 1, spot, :] = half * (centre + padded[level, pl.ds(row - 1, TILE), :])
            coef[level, 2, spot, :] = (0.5 * north_step) * (centre + pltpu.roll(centre, 127, 1))
            coef[level, 3, spot, :] = (0.5 * south_step) * (centre + pltpu.roll(centre, 1, 1))
    advance(present, following, coef, (0, 1, 2), blocks)
    total = observe(following, weight)
    advance(following, present, coef, (0, 1, 2), blocks)
    total = total + observe(present, weight)
    advance(present, following, coef, (2,), blocks[1:-1])
    action[...] = total + observe(following, weight)


def wind_kernel(scale, chosen, edges, inner, sister, got_edges, got_odd, got_inner, odd_inner, got_a, got_b,
                coef, weight, action, added, winds, warm, far, middle, near, halo, present, following):
    levels, rows = edges.shape[1], weight.shape[0]
    end = TOP + rows
    strip = pl.ds(TOP, rows)
    targets = [winds.at[0, 0], winds.at[0, 1], present]

    def whole():
        for field, target in enumerate(targets):
            for level in range(levels):
                target[level, strip, :] = sister[0, field, level]

    def joined(edges, inner):
        def put():
            for field, target in enumerate(targets):
                lay(target, field, edges, inner)

        return put

    pick(chosen[0], [joined(edges, inner), whole, joined(got_edges, got_inner), joined(got_odd, odd_inner)])
    pair_get(halo, got_a, got_b, even_strip())
    for field, target in enumerate(targets):
        for level in range(levels):
            at = 6 * (field * levels + level)
            target[level, pl.ds(TOP - 6, 6), :] = halo[0, pl.ds(at, 6), :]
            target[level, pl.ds(end, 6), :] = halo[1, pl.ds(at, 6), :]
    every = range(rows // TILE + 2)
    now, later = present, following
    totals = [jnp.zeros((TILE, 128), jnp.float32) for _ in range(levels)]
    for step in range(2 * STEPS):
        last = step == 2 * STEPS - 1
        for level in range(levels):
            for block in every[1:-1] if last else every:
                row = TILE + TILE * block
                here = pl.ds(row, TILE)
                wind = winds.at[step]
                factors = face_factors(level, wind[0, level, here, :], wind[1, level, here, :], coef, block)
                for field in (0, 1) if not last else ():
                    moved = stepped(wind.at[field, level], row, factors)
                    if step == STEPS - 1:
                        moved = moved + added[field, level, here, :]
                    winds[step + 1, field, level, here, :] = moved
                moved = stepped(now.at[level], row, factors)
                if step == STEPS - 1:
                    moved = moved + added[2, level, here, :]
                if last:
                    warm[level, pl.ds(row - TOP, TILE), :] = moved
                else:
                    later[level, here, :] = moved
                if step >= STEPS and block in every[1:-1]:
                    totals[level] += weight[pl.ds(row - TOP, TILE), :] * moved * moved
        now, later = later, now
    first = jnp.sum(action[...]) * scale
    second = jnp.sum(sum(totals[1:], totals[0])) * scale
    lane = lax.broadcasted_iota(jnp.int32, (1, 128), 1)
    sums = jnp.where(lane == 0, first, jnp.where(lane == 1, second, 0.0))
    for ref in (far, middle, near):
        ref[...] = jnp.broadcast_to(sums, ref.shape)


def rest_kernel(chosen, edges, inner, sister, got_edges, got_odd, got_inner, odd_inner, got_a, got_b, winds, warm, coef,
                added, final, wind_out, humid_out, halo, humid, present, following, sems):
    levels, rows = warm.shape[:2]
    every = range(rows // TILE + 2)
    copies = start_all([pltpu.make_async_copy(warm, final.at[0, 2], sems.at[0])])
    last = 2 * STEPS - 1

    def faces(step, level, block):
        here = pl.ds(TILE + TILE * block, TILE)
        return face_factors(level, winds[step, 0, level, here, :], winds[step, 1, level, here, :], coef, block)

    for level in range(levels):
        for block in every[1:-1]:
            factors = faces(last, level, block)
            for field in (0, 1):
                row = TILE + TILE * block
                wind_out[field, level, pl.ds(row - TOP, TILE), :] = stepped(winds.at[last, field, level], row, factors)
    copies += start_all([pltpu.make_async_copy(wind_out, final.at[0, pl.ds(0, 2)], sems.at[1])])
    end = TOP + rows

    def whole():
        for level in range(levels):
            humid[level, pl.ds(TOP, rows), :] = sister[0, 3, level]

    def joined(edges, inner):
        return lambda: lay(humid, 3, edges, inner)

    pick(chosen[0], [joined(edges, inner), whole, joined(got_edges, got_inner), joined(got_odd, odd_inner)])
    pair_get(halo, got_a, got_b, even_strip())
    for level in range(levels):
        at = 6 * (3 * levels + level)
        humid[level, pl.ds(TOP - 6, 6), :] = halo[0, pl.ds(at, 6), :]
        humid[level, pl.ds(end, 6), :] = halo[1, pl.ds(at, 6), :]
    now, later = humid, present
    for step in range(2 * STEPS):
        for level in range(levels):
            for block in every[1:-1] if step == last else every:
                row = TILE + TILE * block
                moved = stepped(now.at[level], row, faces(step, level, block))
                if step == STEPS - 1:
                    moved = moved + added[3, level, pl.ds(row, TILE), :]
                if step == last:
                    humid_out[level, pl.ds(row - TOP, TILE), :] = moved
                else:
                    later[level, pl.ds(row, TILE), :] = moved
        now, later = later, following if later is present else present
    copies += start_all([pltpu.make_async_copy(humid_out, final.at[0, 3], sems.at[2])])
    wait_all(copies)


def body(initial_state, ancestor, selector, perturbations, diffusivity, region_weight):
    _, fields, levels, rows, lat = initial_state.shape
    members, strips = lax.axis_size("mem"), lax.axis_size("lon")
    planes = fields * levels
    general = members != 4
    scale = 1.0 / (levels * lat * rows * strips)
    dma = pltpu.SemaphoreType.DMA

    def scratch(*shape):
        return pltpu.VMEM(shape, jnp.float32)

    def across(value, axis, bit):
        return lax.ppermute(value, axis, [(i, i ^ bit) for i in range(lax.axis_size(axis))])

    def after(values, others):
        return lax.optimization_barrier((values, others))[0]

    def round_strips(a, b):
        pairs_a = [(i, i ^ 1) for i in range(strips)]
        pairs_b = [(i, (i + 1 if i % 2 else i - 1) % strips) for i in range(strips)]
        return lax.ppermute(a, "lon", pairs_a), lax.ppermute(b, "lon", pairs_b)

    own = pltpu.with_memory_space_constraint(initial_state, pltpu.HBM)
    perturbations = pltpu.with_memory_space_constraint(perturbations, pltpu.HBM)
    kappa = pltpu.with_memory_space_constraint(diffusivity, pltpu.HBM)

    early_total = early_rows(planes, levels)[-1]
    inner_shape = f32(fields, levels, rows - 2 * TILE, lat)
    edges = call(edge_kernel, f32(fields, levels, 2 * TILE, lat), [HBM], ANY, [dma((2,))], "edges")(own)
    inner = call(inner_kernel, inner_shape, [HBM], ANY, [dma], "inner")(after(own, edges))
    sister = initial_state if general else across(after(initial_state, edges), "mem", 1)
    padded = rows + 2 * TOP
    early_a, early_b, chosen, added, spread = call(
        functools.partial(early_kernel, general),
        (
            f32(early_total + 0, lat),
            f32(early_total + 0, lat),
            jax.ShapeDtypeStruct((2,), jnp.int32),
            f32(fields, levels, padded, lat),
            f32(levels, padded, lat),
        ),
        [SMEM, SMEM, VMEM, HBM, HBM],
        (VMEM, VMEM, SMEM, VMEM, VMEM),
        [dma((2,))],
        "early_halo",
    )(ancestor, selector, after(edges, inner), perturbations, kappa)
    if general:
        picked = jnp.take(lax.all_gather(initial_state, "mem", axis=0, tiled=True), ancestor, axis=0)[0]
        got_edges = got_odd = jnp.concatenate([picked[:, :, :TILE], picked[:, :, rows - TILE :]], axis=2)
        got_inner = odd_inner = picked[:, :, TILE : rows - TILE]
    else:
        got_edges = across(edges, "mem", 2)
        got_odd = across(after(got_edges, early_a), "mem", 1)
        got_inner = across(inner, "mem", 2)

    early = round_strips(early_a, early_b)
    late = call(
        late_kernel,
        (f32(6 * planes, lat), f32(6 * planes + TILE, lat)),
        [SMEM] + [VMEM] * 4,
        (VMEM, VMEM),
        [],
        "late_halo",
        1 << 31,
    )(chosen, edges, sister, got_edges, got_odd)
    packed = late
    late = round_strips(*packed)

    coef, action, added = call(
        prepare_kernel,
        (f32(levels, 4, rows + 2 * TILE, lat), f32(TILE, lat), f32(fields, levels, padded, lat)),
        [VMEM] * 7,
        (VMEM, VMEM, VMEM),
        [
            scratch(2, early_total, lat),
            scratch(3, levels, padded, lat),
            scratch(3, levels, padded, lat),
            scratch(levels, padded, lat),
        ],
        "prepare",
        1 << 32,
    )(edges, inner, region_weight, *early, spread, added)
    if not general:
        odd_inner = across(after(got_inner, packed), "mem", 1)
    winds, warm, far, middle, near = call(
        functools.partial(wind_kernel, scale),
        (
            f32(2 * STEPS, 2, levels, padded, lat),
            f32(levels, rows, lat),
            f32(16, lat),
            f32(8, lat),
            f32(1, lat),
        ),
        [SMEM] + [VMEM] * 13,
        (VMEM,) * 5,
        [scratch(2, 6 * planes, lat), scratch(levels, padded, lat), scratch(levels, padded, lat)],
        "clone_winds",
    )(chosen, edges, inner, sister, got_edges, got_odd, got_inner, odd_inner, *late, coef, region_weight, action, added)
    final_state = call(
        rest_kernel,
        f32(1, fields, levels, rows, lat),
        [SMEM] + [VMEM] * 13,
        HBM,
        [
            scratch(2, levels, rows, lat),
            scratch(levels, rows, lat),
            scratch(2, 6 * planes, lat),
            scratch(levels, padded, lat),
            scratch(levels, padded, lat),
            scratch(levels, padded, lat),
            dma((3,)),
        ],
        "clone_rest",
    )(chosen, edges, inner, sister, got_edges, got_odd, got_inner, odd_inner, *late, winds, warm, coef, added)
    if strips == 4:
        two, three, one = across(far, "lon", 2), across(middle, "lon", 3), across(near, "lon", 1)
        sums = (near + one) + (two[:1] + three[:1])
    else:
        sums, bit = near, 1
        while bit < strips:
            sums = sums + across(sums, "lon", bit)
            bit *= 2
    return final_state, sums[:, :2]


def solution(mesh):
    in_specs = (
        P(("ens", "mem"), None, None, "lon", None),
        P(("ens", "mem")),
        P(("ens", "mem")),
        P("ens", None, None, "lon", None),
        P(None, "lon", None),
        P("lon", None),
    )
    out_specs = (P(("ens", "mem"), None, None, "lon", None), P(("ens", "mem"), None))
    return jax.shard_map(body, mesh=mesh, in_specs=in_specs, out_specs=out_specs, check_vma=False)
```

```python
import functools
import jax
import jax.numpy as jnp
from jax import lax
from jax.experimental import pallas as pl
from jax.experimental.pallas import tpu as pltpu
from jax.sharding import PartitionSpec as P

STEPS = 3
TIME_STEP = 0.2
TILE = 8
TOP = 2 * TILE
VMEM_LIMIT = 12 * 1024 * 1024

ANY = pl.BlockSpec(memory_space=pl.ANY)
HBM = pl.BlockSpec(memory_space=pltpu.HBM)
VMEM = pl.BlockSpec(memory_space=pltpu.VMEM)
SMEM = pl.BlockSpec(memory_space=pltpu.SMEM)


def call(kernel, out_shape, in_specs, out_specs, scratch_shapes, name, flops=0):
    return pl.pallas_call(
        kernel,
        out_shape=out_shape,
        in_specs=in_specs,
        out_specs=out_specs,
        scratch_shapes=scratch_shapes,
        name=name,
        compiler_params=pltpu.CompilerParams(vmem_limit_bytes=VMEM_LIMIT),
        cost_estimate=pl.CostEstimate(flops=flops, bytes_accessed=1 << 20, transcendentals=0),
    )


def f32(*shape):
    return jax.ShapeDtypeStruct(shape, jnp.float32)


def lane_steps(rows):
    lane = lax.broadcasted_iota(jnp.int32, (rows, 128), 1)
    north = jnp.where(lane == 127, 0.0, TIME_STEP).astype(jnp.float32)
    south = jnp.where(lane == 0, 0.0, TIME_STEP).astype(jnp.float32)
    return north, south


def face_factors(level, zonal, merid, coef, block):
    north_step, south_step = lane_steps(TILE)
    spot = pl.ds(TILE * block, TILE)
    east = coef[level, 0, spot, :] - TIME_STEP * jnp.minimum(zonal, 0.0)
    west = coef[level, 1, spot, :] + TIME_STEP * jnp.maximum(zonal, 0.0)
    north = coef[level, 2, spot, :] - north_step * jnp.minimum(merid, 0.0)
    south = coef[level, 3, spot, :] + south_step * jnp.maximum(merid, 0.0)
    return 1.0 - ((east + west) + (north + south)), east, west, north, south


def stepped(source, row, factors):
    keep, east, west, north, south = factors
    centre = source[pl.ds(row, TILE), :]
    return (
        keep * centre
        + east * source[pl.ds(row + 1, TILE), :]
        + west * source[pl.ds(row - 1, TILE), :]
        + north * pltpu.roll(centre, 127, 1)
        + south * pltpu.roll(centre, 1, 1)
    )


def advance(source, target, coef, fields, blocks):
    for level in range(source.shape[1]):
        for block in blocks:
            row = TILE + TILE * block
            here = pl.ds(row, TILE)
            factors = face_factors(level, source[0, level, here, :], source[1, level, here, :], coef, block)
            for field in fields:
                target[field, level, here, :] = stepped(source.at[field, level], row, factors)


def observe(values, weight):
    total = jnp.zeros((TILE, 128), jnp.float32)
    for block in range(weight.shape[0] // TILE):
        square = jnp.zeros((TILE, 128), jnp.float32)
        for level in range(values.shape[1]):
            spot = values[2, level, pl.ds(TOP + TILE * block, TILE), :]
            square = square + spot * spot
        total = total + weight[pl.ds(TILE * block, TILE), :] * square
    return total


OWN_DEPTH = (2, 2, 3)


def early_rows(planes, levels):
    own = 0
    added = own + sum(OWN_DEPTH) * levels
    kappa = added + 3 * planes
    total = kappa + 6 * levels
    return own, added, kappa, -(-total // TILE) * TILE


def start_all(copies):
    for copy in copies:
        copy.start()
    return copies


def wait_all(copies):
    for copy in copies:
        copy.wait()


def edge_copies(source, target, sems, first):
    rows = source.shape[-2]
    lead = (slice(None),) * (len(source.shape) - 2)
    return [
        pltpu.make_async_copy(
            source.at[(*lead, pl.ds(0, TILE))], target.at[(*lead, pl.ds(0, TILE))], sems.at[first]
        ),
        pltpu.make_async_copy(
            source.at[(*lead, pl.ds(rows - TILE, TILE))], target.at[(*lead, pl.ds(TILE, TILE))], sems.at[first + 1]
        ),
    ]


def pair_put(out_a, out_b, even, offset, low_rows, high_rows):
    spot = pl.ds(offset, low_rows.shape[0])
    out_a[spot, :] = jnp.where(even, high_rows, low_rows)
    out_b[spot, :] = jnp.where(even, low_rows, high_rows)


def pair_get(halo, got_a, got_b, even):
    a, b = got_a[0 : halo.shape[1], :], got_b[0 : halo.shape[1], :]
    halo[0] = jnp.where(even, b, a)
    halo[1] = jnp.where(even, a, b)


def even_strip():
    return lax.rem(lax.axis_index("lon"), 2) == 0


def edge_kernel(own, edges, sems):
    wait_all(start_all(edge_copies(own.at[0], edges, sems, 0)))


def inner_kernel(own, inner, sem):
    rows = own.shape[3]
    wait_all(start_all([pltpu.make_async_copy(own.at[0, :, :, pl.ds(TILE, rows - 2 * TILE), :], inner, sem)]))


def early_kernel(general, ancestor, selector, edges, perturbations, kappa, out_a, out_b, chosen, added, spread, sems):
    fields, levels = edges.shape[:2]
    rows = kappa.shape[1]
    which = jnp.clip(selector[0], 0, perturbations.shape[0] - 1)
    chosen[0] = 2 if general else lax.axis_index("mem") ^ ancestor[0]
    chosen[1] = which
    strip = pl.ds(TOP, rows)
    wait_all(start_all([
        pltpu.make_async_copy(perturbations.at[which], added.at[:, :, strip, :], sems.at[0]),
        pltpu.make_async_copy(kappa, spread.at[:, strip, :], sems.at[1]),
    ]))
    even = even_strip()
    put = functools.partial(pair_put, out_a, out_b, even)
    at_own, at_added, at_kappa, _ = early_rows(fields * levels, levels)
    end = TOP + rows
    for field in range(fields):
        for level in range(levels):
            plane = field * levels + level
            if field < 3:
                deep = OWN_DEPTH[field]
                at = at_own + levels * sum(OWN_DEPTH[:field]) + deep * level
                put(at, edges[field, level, 0:deep, :], edges[field, level, 16 - deep : 16, :])
            put(at_added + 3 * plane, added[field, level, TOP : TOP + 3, :], added[field, level, end - 3 : end, :])
    for level in range(levels):
        put(at_kappa + 6 * level, spread[level, TOP : TOP + 6, :], spread[level, end - 6 : end, :])


def pick(rel, choices):
    for number, choice in enumerate(choices):
        pl.when(rel == number if number < 3 else rel > 2)(choice)


def late_kernel(chosen, edges, sister, got_edges, got_odd, out_a, out_b):
    fields, levels = edges.shape[:2]
    even = even_strip()

    def packed(source):
        rows = source.shape[2]

        def put():
            for field in range(fields):
                for level in range(levels):
                    low, high = source[field, level, 0:6, :], source[field, level, rows - 6 : rows, :]
                    pair_put(out_a, out_b, even, 6 * (field * levels + level), low, high)

        return put

    pick(chosen[0], [packed(edges), packed(sister.at[0]), packed(got_edges), packed(got_odd)])


def lay(target, field, edges, inner):
    rows = inner.shape[2] + 2 * TILE
    for level in range(inner.shape[1]):
        target[level, pl.ds(TOP, TILE), :] = edges[field, level, 0:TILE, :]
        target[level, pl.ds(TOP + TILE, rows - 2 * TILE), :] = inner[field, level]
        target[level, pl.ds(TOP + rows - TILE, TILE), :] = edges[field, level, TILE : 2 * TILE, :]


def prepare_kernel(edges, inner, weight, got_a, got_b, spread, added_in, coef, action, added,
                   halo, present, following, padded):
    fields, levels = edges.shape[:2]
    rows = weight.shape[0]
    for field in range(3):
        lay(present.at[field], field, edges, inner)
    pair_get(halo, got_a, got_b, even_strip())
    at_own, at_added, at_kappa, _ = early_rows(fields * levels, levels)
    end = TOP + rows
    strip = pl.ds(TOP, rows)
    for level in range(levels):
        padded[level, strip, :] = spread[level, strip, :]
        padded[level, pl.ds(TOP - 6, 6), :] = halo[0, pl.ds(at_kappa + 6 * level, 6), :]
        padded[level, pl.ds(end, 6), :] = halo[1, pl.ds(at_kappa + 6 * level, 6), :]
        for field in range(fields):
            plane = field * levels + level
            if field < 3:
                deep = OWN_DEPTH[field]
                at = at_own + levels * sum(OWN_DEPTH[:field]) + deep * level
                present[field, level, pl.ds(TOP - deep, deep), :] = halo[0, pl.ds(at, deep), :]
                present[field, level, pl.ds(end, deep), :] = halo[1, pl.ds(at, deep), :]
            added[field, level, strip, :] = added_in[field, level, strip, :]
            added[field, level, pl.ds(TOP - 3, 3), :] = halo[0, pl.ds(at_added + 3 * plane, 3), :]
            added[field, level, pl.ds(end, 3), :] = halo[1, pl.ds(at_added + 3 * plane, 3), :]
    blocks = range(rows // TILE + 2)
    north_step, south_step = lane_steps(TILE)
    for level in range(levels):
        for block in blocks:
            row = TILE + TILE * block
            spot = pl.ds(TILE * block, TILE)
            centre = padded[level, pl.ds(row, TILE), :]
            half = 0.5 * TIME_STEP
            coef[level, 0, spot, :] = half * (centre + padded[level, pl.ds(row + 1, TILE), :])
            coef[level, 1, spot, :] = half * (centre + padded[level, pl.ds(row - 1, TILE), :])
            coef[level, 2, spot, :] = (0.5 * north_step) * (centre + pltpu.roll(centre, 127, 1))
            coef[level, 3, spot, :] = (0.5 * south_step) * (centre + pltpu.roll(centre, 1, 1))
    advance(present, following, coef, (0, 1, 2), blocks)
    total = observe(following, weight)
    advance(following, present, coef, (0, 1, 2), blocks)
    total = total + observe(present, weight)
    advance(present, following, coef, (2,), blocks[1:-1])
    action[...] = total + observe(following, weight)


def wind_kernel(scale, chosen, edges, inner, sister, got_edges, got_odd, got_inner, odd_inner, got_a, got_b,
                coef, weight, action, added, winds, humid, warm, far, middle, near, halo, present, following):
    levels, rows = edges.shape[1], weight.shape[0]
    end = TOP + rows
    strip = pl.ds(TOP, rows)
    targets = [winds.at[0, 0], winds.at[0, 1], present, humid]

    def whole():
        for field, target in enumerate(targets):
            for level in range(levels):
                target[level, strip, :] = sister[0, field, level]

    def joined(edges, inner):
        def put():
            for field, target in enumerate(targets):
                lay(target, field, edges, inner)

        return put

    pick(chosen[0], [joined(edges, inner), whole, joined(got_edges, got_inner), joined(got_odd, odd_inner)])
    pair_get(halo, got_a, got_b, even_strip())
    for field, target in enumerate(targets):
        for level in range(levels):
            at = 6 * (field * levels + level)
            target[level, pl.ds(TOP - 6, 6), :] = halo[0, pl.ds(at, 6), :]
            target[level, pl.ds(end, 6), :] = halo[1, pl.ds(at, 6), :]
    every = range(rows // TILE + 2)
    now, later = present, following
    totals = [jnp.zeros((TILE, 128), jnp.float32) for _ in range(levels)]
    for step in range(2 * STEPS):
        last = step == 2 * STEPS - 1
        for level in range(levels):
            for block in every[1:-1] if last else every:
                row = TILE + TILE * block
                here = pl.ds(row, TILE)
                wind = winds.at[step]
                factors = face_factors(level, wind[0, level, here, :], wind[1, level, here, :], coef, block)
                for field in (0, 1) if not last else ():
                    moved = stepped(wind.at[field, level], row, factors)
                    if step == STEPS - 1:
                        moved = moved + added[field, level, here, :]
                    winds[step + 1, field, level, here, :] = moved
                moved = stepped(now.at[level], row, factors)
                if step == STEPS - 1:
                    moved = moved + added[2, level, here, :]
                if last:
                    warm[level, pl.ds(row - TOP, TILE), :] = moved
                else:
                    later[level, here, :] = moved
                if step >= STEPS and block in every[1:-1]:
                    totals[level] += weight[pl.ds(row - TOP, TILE), :] * moved * moved
        now, later = later, now
    first = jnp.sum(action[...]) * scale
    second = jnp.sum(sum(totals[1:], totals[0])) * scale
    lane = lax.broadcasted_iota(jnp.int32, (1, 128), 1)
    sums = jnp.where(lane == 0, first, jnp.where(lane == 1, second, 0.0))
    for ref in (far, middle, near):
        ref[...] = jnp.broadcast_to(sums, ref.shape)


def rest_kernel(winds, humid, warm, coef, added, final, wind_out, humid_out, present, following, sems):
    levels, rows = warm.shape[:2]
    every = range(rows // TILE + 2)
    copies = start_all([pltpu.make_async_copy(warm, final.at[0, 2], sems.at[0])])
    last = 2 * STEPS - 1

    def faces(step, level, block):
        here = pl.ds(TILE + TILE * block, TILE)
        return face_factors(level, winds[step, 0, level, here, :], winds[step, 1, level, here, :], coef, block)

    for level in range(levels):
        for block in every[1:-1]:
            factors = faces(last, level, block)
            for field in (0, 1):
                row = TILE + TILE * block
                wind_out[field, level, pl.ds(row - TOP, TILE), :] = stepped(winds.at[last, field, level], row, factors)
    copies += start_all([pltpu.make_async_copy(wind_out, final.at[0, pl.ds(0, 2)], sems.at[1])])
    now, later = humid, present
    for step in range(2 * STEPS):
        for level in range(levels):
            for block in every[1:-1] if step == last else every:
                row = TILE + TILE * block
                moved = stepped(now.at[level], row, faces(step, level, block))
                if step == STEPS - 1:
                    moved = moved + added[3, level, pl.ds(row, TILE), :]
                if step == last:
                    humid_out[level, pl.ds(row - TOP, TILE), :] = moved
                else:
                    later[level, pl.ds(row, TILE), :] = moved
        now, later = later, following if later is present else present
    copies += start_all([pltpu.make_async_copy(humid_out, final.at[0, 3], sems.at[2])])
    wait_all(copies)


def body(initial_state, ancestor, selector, perturbations, diffusivity, region_weight):
    _, fields, levels, rows, lat = initial_state.shape
    members, strips = lax.axis_size("mem"), lax.axis_size("lon")
    planes = fields * levels
    general = members != 4
    scale = 1.0 / (levels * lat * rows * strips)
    dma = pltpu.SemaphoreType.DMA

    def scratch(*shape):
        return pltpu.VMEM(shape, jnp.float32)

    def across(value, axis, bit):
        return lax.ppermute(value, axis, [(i, i ^ bit) for i in range(lax.axis_size(axis))])

    def after(values, others):
        return lax.optimization_barrier((values, others))[0]

    def round_strips(a, b):
        pairs_a = [(i, i ^ 1) for i in range(strips)]
        pairs_b = [(i, (i + 1 if i % 2 else i - 1) % strips) for i in range(strips)]
        return lax.ppermute(a, "lon", pairs_a), lax.ppermute(b, "lon", pairs_b)

    own = pltpu.with_memory_space_constraint(initial_state, pltpu.HBM)
    perturbations = pltpu.with_memory_space_constraint(perturbations, pltpu.HBM)
    kappa = pltpu.with_memory_space_constraint(diffusivity, pltpu.HBM)

    early_total = early_rows(planes, levels)[-1]
    inner_shape = f32(fields, levels, rows - 2 * TILE, lat)
    edges = call(edge_kernel, f32(fields, levels, 2 * TILE, lat), [HBM], ANY, [dma((2,))], "edges")(own)
    inner = call(inner_kernel, inner_shape, [HBM], ANY, [dma], "inner")(after(own, edges))
    sister = initial_state if general else across(after(initial_state, edges), "mem", 1)
    padded = rows + 2 * TOP
    early_a, early_b, chosen, added, spread = call(
        functools.partial(early_kernel, general),
        (
            f32(early_total + 0, lat),
            f32(early_total + 0, lat),
            jax.ShapeDtypeStruct((2,), jnp.int32),
            f32(fields, levels, padded, lat),
            f32(levels, padded, lat),
        ),
        [SMEM, SMEM, VMEM, HBM, HBM],
        (VMEM, VMEM, SMEM, VMEM, VMEM),
        [dma((2,))],
        "early_halo",
    )(ancestor, selector, after(edges, inner), perturbations, kappa)
    if general:
        picked = jnp.take(lax.all_gather(initial_state, "mem", axis=0, tiled=True), ancestor, axis=0)[0]
        got_edges = got_odd = jnp.concatenate([picked[:, :, :TILE], picked[:, :, rows - TILE :]], axis=2)
        got_inner = odd_inner = picked[:, :, TILE : rows - TILE]
    else:
        got_edges = across(edges, "mem", 2)
        got_odd = across(after(got_edges, early_a), "mem", 1)
        got_inner = across(inner, "mem", 2)

    early = round_strips(after(early_a, got_odd), early_b)
    late = call(
        late_kernel,
        (f32(6 * planes + 8, lat), f32(6 * planes + 0, lat)),
        [SMEM] + [VMEM] * 4,
        (VMEM, VMEM),
        [],
        "late_halo",
        1 << 31,
    )(chosen, edges, sister, got_edges, got_odd)
    packed = late
    late = round_strips(*packed)

    coef, action, added = call(
        prepare_kernel,
        (f32(levels, 4, rows + 2 * TILE, lat), f32(TILE, lat), f32(fields, levels, padded, lat)),
        [VMEM] * 7,
        (VMEM, VMEM, VMEM),
        [
            scratch(2, early_total, lat),
            scratch(3, levels, padded, lat),
            scratch(3, levels, padded, lat),
            scratch(levels, padded, lat),
        ],
        "prepare",
        1 << 32,
    )(edges, inner, region_weight, *early, spread, added)
    if not general:
        odd_inner = across(after(got_inner, packed), "mem", 1)
    winds, humid, warm, far, middle, near = call(
        functools.partial(wind_kernel, scale),
        (
            f32(2 * STEPS, 2, levels, padded, lat),
            f32(levels, padded, lat),
            f32(levels, rows, lat),
            f32(16, lat),
            f32(8, lat),
            f32(1, lat),
        ),
        [SMEM] + [VMEM] * 13,
        (VMEM,) * 6,
        [scratch(2, 6 * planes, lat), scratch(levels, padded, lat), scratch(levels, padded, lat)],
        "clone_winds",
    )(chosen, edges, inner, sister, got_edges, got_odd, got_inner, odd_inner, *late, coef, region_weight, action, added)
    final_state = call(
        rest_kernel,
        f32(1, fields, levels, rows, lat),
        [VMEM] * 5,
        HBM,
        [
            scratch(2, levels, rows, lat),
            scratch(levels, rows, lat),
            scratch(levels, padded, lat),
            scratch(levels, padded, lat),
            dma((3,)),
        ],
        "clone_rest",
    )(winds, humid, warm, coef, added)
    if strips == 4:
        two, three, one = across(far, "lon", 2), across(middle, "lon", 3), across(near, "lon", 1)
        sums = (near + one) + (two[:1] + three[:1])
    else:
        sums, bit = near, 1
        while bit < strips:
            sums = sums + across(sums, "lon", bit)
            bit *= 2
    return final_state, sums[:, :2]


def solution(mesh):
    in_specs = (
        P(("ens", "mem"), None, None, "lon", None),
        P(("ens", "mem")),
        P(("ens", "mem")),
        P("ens", None, None, "lon", None),
        P(None, "lon", None),
        P("lon", None),
    )
    out_specs = (P(("ens", "mem"), None, None, "lon", None), P(("ens", "mem"), None))
    return jax.shard_map(body, mesh=mesh, in_specs=in_specs, out_specs=out_specs, check_vma=False)
```
